32 devices in a mesh: dp: 4 (over y, x), tok: 8 (over z, core).
Axes of the slice: x: 2, y: 2, z: 4, core: 2. Of those that a mesh axis runs over, the one named last changes fastest.
Arguments:
- encoder_input: bfloat16 [32, 512, 768], P(('dp', 'tok')), may hold values from -6 to 6
- decoder_input: bfloat16 [64, 768], P(('dp', 'tok')), may hold values from -6 to 6
- output_cotangent: bfloat16 [64, 768], P(('dp', 'tok')), may hold values from -6 to 6
- pair_lengths: int32 [32, 8], P(('dp', 'tok')), may hold values from 1 to 128, 512 in all within a row
- pair_offset: int32 [4, 8], P('dp'), may hold values from 0 to 7, as said below
- pair_query: int32 [4, 8], P('dp'), may hold values from 0 to 1, as said below
- attention_master: float32 [6, 768, 768], P(None, ('dp', 'tok')), may hold values from -0.21875 to 0.21875
- attention_moment: float32 [6, 768, 768], P(None, ('dp', 'tok')), may hold values from -24 to 24
- attention_average: float32 [6, 768, 768], P(None, ('dp', 'tok')), may hold values from -0.21875 to 0.21875
- feedforward_master: float32 [2, 768, 3072], P(None, ('dp', 'tok')), may hold values from -0.21875 to 0.21875
- feedforward_moment: float32 [2, 768, 3072], P(None, ('dp', 'tok')), may hold values from -24 to 24
- feedforward_average: float32 [2, 768, 3072], P(None, ('dp', 'tok')), may hold values from -0.21875 to 0.21875
- decoder_master: float32 [4, 768, 768], P(None, ('dp', 'tok')), may hold values from -0.21875 to 0.21875
- decoder_moment: float32 [4, 768, 768], P(None, ('dp', 'tok')), may hold values from -6 to 6
- decoder_average: float32 [4, 768, 768], P(None, ('dp', 'tok')), may hold values from -0.21875 to 0.21875
- expansion_master: float32 [2, 768, 3072], P(None, ('dp', 'tok')), may hold values from -0.21875 to 0.21875
- expansion_moment: float32 [2, 768, 3072], P(None, ('dp', 'tok')), may hold values from -6 to 6
- expansion_average: float32 [2, 768, 3072], P(None, ('dp', 'tok')), may hold values from -0.21875 to 0.21875
- gain_master: float32 [5, 768], replicated, may hold values from 0.5 to 1.5
- gain_moment: float32 [5, 768], replicated, may hold values from -40 to 40
- gain_average: float32 [5, 768], replicated, may hold values from 0.5 to 1.5
- bias_master: float32 [32, 12], replicated, may hold values from -4 to 4
- bias_moment: float32 [32, 12], replicated, may hold values from -16 to 16
- bias_average: float32 [32, 12], replicated, may hold values from -4 to 4
Outputs:
- decoder_output: float32 [64, 768], P(('dp', 'tok'))
- encoder_gradient: float32 [32, 512, 768], P(('dp', 'tok'))
- decoder_gradient: float32 [64, 768], P(('dp', 'tok'))
- attention_momentum: float32 [6, 768, 768], P(None, ('dp', 'tok'))
- attention_averaged: float32 [6, 768, 768], P(None, ('dp', 'tok'))
- attention_updated: float32 [6, 768, 768], P(None, ('dp', 'tok'))
- attention_copy: bfloat16 [6, 768, 768], P(None, ('dp', 'tok'))
- feedforward_momentum: float32 [2, 768, 3072], P(None, ('dp', 'tok'))
- feedforward_averaged: float32 [2, 768, 3072], P(None, ('dp', 'tok'))
- feedforward_updated: float32 [2, 768, 3072], P(None, ('dp', 'tok'))
- feedforward_copy: bfloat16 [2, 768, 3072], P(None, ('dp', 'tok'))
- decoder_momentum: float32 [4, 768, 768], P(None, ('dp', 'tok'))
- decoder_averaged: float32 [4, 768, 768], P(None, ('dp', 'tok'))
- decoder_updated: float32 [4, 768, 768], P(None, ('dp', 'tok'))
- decoder_copy: bfloat16 [4, 768, 768], P(None, ('dp', 'tok'))
- expansion_momentum: float32 [2, 768, 3072], P(None, ('dp', 'tok'))
- expansion_averaged: float32 [2, 768, 3072], P(None, ('dp', 'tok'))
- expansion_updated: float32 [2, 768, 3072], P(None, ('dp', 'tok'))
- expansion_copy: bfloat16 [2, 768, 3072], P(None, ('dp', 'tok'))
- gain_momentum: float32 [5, 768], replicated
- gain_averaged: float32 [5, 768], replicated
- gain_updated: float32 [5, 768], replicated
- gain_copy: bfloat16 [5, 768], replicated
- bias_momentum: float32 [32, 12], replicated
- bias_averaged: float32 [32, 12], replicated
- bias_updated: float32 [32, 12], replicated
- bias_copy: bfloat16 [32, 12], replicated
The draws below stay inside these ranges and needn't reach their ends.
Inputs may be any that keep to these rules, and one draw needn't show every extreme that they name: Each row is a permutation of the 8 values i and 4 + i for i below 4; pair k of the row on tok index t goes to tok index (t + pair_offset[n, k]) mod 8 of the same dp index n, so every device receives exactly 8 pairs, one from each of 8 devices. `pair_query`: each value appears exactly 4 times in a row. `pair_lengths`: each row's lengths sum to 512.
All inputs are finite; a program needn't handle non-finite values.
Results may differ from the reference program's by a relative error of at most 0.025.
The reference program's roundings to bfloat16 on the way count: a program that leaves them out, or rounds other values in their place, can miss the bound.
Values may be sent and summed in bfloat16 or wider, within the bound.
No kernel may reach another device: no remote copies, remote signals or barrier semaphores. Data moves between devices by JAX's collectives and lax.ppermute only.
A program may use at most 320 MiB of HBM per device.

```python
import math
import jax
import jax.numpy as jnp
import numpy as np
from jax import lax

D = 768
HEADS = 12
FF = 3072
BUCKETS = 32
ROW = 512
PAIRS = 8
QUERY_DEV = 2
SLOT = 128
PER_QUERY = 4
ROWS = 32
QUERIES = 64
N_DP = 4
N_TOK = 8


def offset_row(row_key):
    order = jax.random.permutation(row_key, PAIRS).astype(jnp.int32)
    half = PAIRS // 2
    return jnp.where(order < half, order, N_TOK // 2 + order - half).astype(jnp.int32)


def draw_pair_offset(key, part):
    row_keys = jax.random.split(jax.random.fold_in(key, 11), N_DP)
    return jax.vmap(offset_row)(row_keys)


def query_row(row_key):
    return (jax.random.permutation(row_key, PAIRS).astype(jnp.int32) // PER_QUERY).astype(jnp.int32)


def draw_pair_query(key, part):
    row_keys = jax.random.split(jax.random.fold_in(key, 23), N_DP)
    return jax.vmap(query_row)(row_keys)


def steps_of(rng, extent, cuts, low, largest):
    loudness, own = 1.0, jax.random.fold_in(rng, 6)
    for dim, blocks in cuts:
        draws = jnp.exp(jax.random.uniform(jax.random.fold_in(own, dim), (blocks,), jnp.float32, low / len(cuts), largest / len(cuts)))
        loudness = loudness * jnp.repeat(draws, extent[dim] // blocks).reshape([-1 if axis == dim else 1 for axis in range(len(extent))])
    return loudness


def length_profile(count, total, reach, skew):
    portions = [(1 << 20) // math.isqrt(standing ** skew) + 1 for standing in range(2, count + 1)]
    surplus, counts = total - reach - (count - 1), [1] * (count - 1)
    while surplus > 0:
        free = [i for i in range(count - 1) if counts[i] < reach]
        mass, budget = sum([portions[i] for i in free]), surplus
        for i in free:
            more = min(reach - counts[i], max(1, budget * portions[i] // mass), surplus)
            counts[i] = counts[i] + more
            surplus = surplus - more
    return np.array([reach] + counts)


def uneven_parts(rng, number_of, total, most, lean):
    if number_of == 2:
        one = jax.random.randint(rng, (), max(1, total - most), min(most, total - 1) + 1)
        return jnp.stack([one, total - one])
    tallies = jnp.asarray(length_profile(number_of, total, most, lean), jnp.int32)
    twos = (number_of - 1) // 2
    source_of, taker = tallies[1:1 + 2 * twos:2], tallies[2:2 + 2 * twos:2]
    slack = jnp.minimum(source_of - 1, most - taker)
    moved = jax.random.randint(jax.random.fold_in(rng, 1), (twos,), 0, 1 << 20) % (slack + 1)
    tallies = tallies.at[1:1 + 2 * twos:2].set(source_of - moved).at[2:2 + 2 * twos:2].set(taker + moved)
    return tallies[jax.random.permutation(jax.random.fold_in(rng, 2), number_of)]


def gaussian(own_key, dims, scale, bound, cuts=(), held_as=jnp.bfloat16):
    level = steps_of(own_key, dims, cuts, -0.22, 0.18) if cuts else 1.0
    entries = jax.random.normal(own_key, dims, jnp.float32) * scale * level
    return jnp.minimum(jnp.maximum(entries, -bound), bound).astype(held_as)


def setup_inputs(seed: int = 0) -> dict:
    key_of = jax.random.split(jax.random.key(seed), 25)
    encoder_input = gaussian(key_of[0], (ROWS, ROW, D), 1.0, 6.0, ((0, 32),))
    decoder_input = gaussian(key_of[1], (QUERIES, D), 1.0, 6.0, ((0, 32),))
    output_cotangent = gaussian(key_of[2], (QUERIES, D), 1.0, 6.0, ((0, 32),))
    pair_lengths = jax.vmap(lambda own: uneven_parts(own, PAIRS, ROW, SLOT, 2))(jax.random.split(key_of[3], ROWS)).reshape((ROWS, PAIRS)).astype(jnp.int32)
    pair_offset = draw_pair_offset(jax.random.fold_in(key_of[24], 71), 0)
    pair_query = draw_pair_query(jax.random.fold_in(key_of[24], 71), 0)
    attention_master = gaussian(key_of[6], (6, D, D), D ** -0.5, 0.21875, ((1, 32),), jnp.float32)
    attention_moment = gaussian(key_of[7], (6, D, D), (0.03 * (ROWS * ROW) ** 0.5), 24.0, ((1, 32),), jnp.float32)
    attention_average = gaussian(key_of[8], (6, D, D), D ** -0.5, 0.21875, ((1, 32),), jnp.float32)
    feedforward_master = gaussian(key_of[9], (2, D, FF), D ** -0.5, 0.21875, ((1, 32),), jnp.float32)
    feedforward_moment = gaussian(key_of[10], (2, D, FF), (0.03 * (ROWS * ROW) ** 0.5), 24.0, ((1, 32),), jnp.float32)
    feedforward_average = gaussian(key_of[11], (2, D, FF), D ** -0.5, 0.21875, ((1, 32),), jnp.float32)
    decoder_master = gaussian(key_of[12], (4, D, D), D ** -0.5, 0.21875, ((1, 32),), jnp.float32)
    decoder_moment = gaussian(key_of[13], (4, D, D), (0.3 * QUERIES ** 0.5), 6.0, ((1, 32),), jnp.float32)
    decoder_average = gaussian(key_of[14], (4, D, D), D ** -0.5, 0.21875, ((1, 32),), jnp.float32)
    expansion_master = gaussian(key_of[15], (2, D, FF), D ** -0.5, 0.21875, ((1, 32),), jnp.float32)
    expansion_moment = gaussian(key_of[16], (2, D, FF), (0.25 * QUERIES ** 0.5), 6.0, ((1, 32),), jnp.float32)
    expansion_average = gaussian(key_of[17], (2, D, FF), D ** -0.5, 0.21875, ((1, 32),), jnp.float32)
    gain_master = jnp.clip(1.0 + 0.1 * jax.random.normal(key_of[18], (5, D), jnp.float32), 0.5, 1.5)
    gain_moment = gaussian(key_of[19], (5, D), (0.05 * (ROWS * ROW) ** 0.5), 40.0, (), jnp.float32)
    gain_average = jnp.clip(1.0 + 0.1 * jax.random.normal(key_of[20], (5, D), jnp.float32), 0.5, 1.5)
    bias_master = gaussian(key_of[21], (BUCKETS, HEADS), 0.5, 4.0, (), jnp.float32)
    bias_moment = gaussian(key_of[22], (BUCKETS, HEADS), (0.02 * (ROWS * ROW) ** 0.5), 16.0, (), jnp.float32)
    bias_average = gaussian(key_of[23], (BUCKETS, HEADS), 0.5, 4.0, (), jnp.float32)
    return dict(encoder_input=encoder_input, decoder_input=decoder_input, output_cotangent=output_cotangent, pair_lengths=pair_lengths, pair_offset=pair_offset, pair_query=pair_query, attention_master=attention_master, attention_moment=attention_moment, attention_average=attention_average, feedforward_master=feedforward_master, feedforward_moment=feedforward_moment, feedforward_average=feedforward_average, decoder_master=decoder_master, decoder_moment=decoder_moment, decoder_average=decoder_average, expansion_master=expansion_master, expansion_moment=expansion_moment, expansion_average=expansion_average, gain_master=gain_master, gain_moment=gain_moment, gain_average=gain_average, bias_master=bias_master, bias_moment=bias_moment, bias_average=bias_average)


@jax.custom_vjp
def low(v):
    return lax.optimization_barrier(v.astype(jnp.bfloat16)).astype(jnp.float32)

@jax.custom_vjp
def low_back(v):
    return v

def low_keep(v):
    return (low(v), None)

def low_pass(kept, grad):
    return (grad,)

def back_keep(v):
    return (v, None)

def back_low(kept, grad):
    return (low(grad),)
low.defvjp(low_keep, low_pass)
low_back.defvjp(back_keep, back_low)
HIGHEST = lax.Precision.HIGHEST
EPSILON = 1e-06
SCALING = 0.125
NEGATIVE = -1e+30
MOMENTUM = 0.5
AVERAGING = 0.5
RATE = 0.02
THRESHOLDS = (12, 16, 23, 32, 46, 64, 91)

def bucket_ids(relative):
    magnitude = jnp.abs(relative)
    bucket = jnp.minimum(magnitude, 8)
    for limit in THRESHOLDS:
        bucket = bucket + (magnitude >= limit).astype(jnp.int32)
    return (bucket + 16 * (relative > 0).astype(jnp.int32)).astype(jnp.int32)

def rms_norm(values, gain):
    return values * lax.rsqrt(lax.optimization_barrier(jnp.mean(values * values, axis=-1, keepdims=True)) + EPSILON) * gain

def matmul(left, right):
    return jnp.dot(left, right, precision=HIGHEST, preferred_element_type=jnp.float32)

def softmax_rows(scores):
    peak = lax.optimization_barrier(jnp.max(scores, axis=-1, keepdims=True))
    expo = jnp.exp(scores - peak)
    return expo / lax.optimization_barrier(jnp.sum(expo, axis=-1, keepdims=True))

def encode_row(hidden, segment, attention, feedforward, gains, table):
    length, width = hidden.shape
    heads = table.shape[1]
    head_size = width // heads
    position = jnp.arange(length, dtype=jnp.int32)
    normed = low(rms_norm(hidden, gains[0]))
    queries = low(low_back(matmul(normed, attention[0]))).reshape(length, heads, head_size)
    keys = low(low_back(matmul(normed, attention[1]))).reshape(length, heads, head_size)
    values = low(low_back(matmul(normed, attention[2]))).reshape(length, heads, head_size)
    bias = jnp.transpose(table[bucket_ids(position[None, :] - position[:, None])], (2, 0, 1))
    raw = jnp.einsum('ihd,jhd->hij', queries, keys, precision=HIGHEST)
    scores = low_back(raw * SCALING + bias)
    same = segment[:, None] == segment[None, :]
    probs = low(softmax_rows(jnp.where(same[None], scores, NEGATIVE)))
    attended = low(low_back(jnp.einsum('hij,jhd->ihd', probs, values, precision=HIGHEST).reshape(length, width)))
    residual = hidden + low_back(matmul(attended, attention[3]))
    normed_two = low(rms_norm(residual, gains[1]))
    inner = low_back(matmul(normed_two, feedforward[0]))
    activated = low(jax.nn.gelu(inner))
    output = residual + low_back(jnp.einsum('if,df->id', activated, feedforward[1], precision=HIGHEST))
    return low(low_back(output))

def forward(encoder_x, decoder_x, attention_w, feedforward_w, decoder_w, expansion_w, gains, table, segment, token_query):
    attention = low(attention_w)
    feedforward = low(feedforward_w)
    decoder = low(decoder_w)
    expansion = low(expansion_w)
    width = encoder_x.shape[2]
    heads = table.shape[1]
    head_size = width // heads

    def row_step(pieces):
        return encode_row(pieces[0], pieces[1], attention, feedforward, gains, table)
    encoded = lax.map(jax.checkpoint(row_step), (encoder_x, segment))
    state = decoder_x
    self_in = low(rms_norm(state, gains[2]))
    self_values = low(low_back(matmul(self_in, decoder[0])))
    after_self = state + low_back(matmul(self_values, decoder[1]))
    cross_in = low(rms_norm(after_self, gains[3]))
    cross_query = low(low_back(matmul(cross_in, decoder[2]))).reshape(N_DP, N_TOK * QUERY_DEV, heads, head_size)
    grouped = encoded.reshape(N_DP, N_TOK * ROW, width)
    owners = token_query.reshape(N_DP, N_TOK * ROW)

    def group_step(pieces):
        context, owner, query_rows = pieces
        keys = low(low_back(matmul(context, attention[4]))).reshape(-1, heads, head_size)
        values = low(low_back(matmul(context, attention[5]))).reshape(-1, heads, head_size)

        def query_step(inputs):
            single, index = inputs
            raw = jnp.einsum('hd,jhd->hj', single, keys, precision=HIGHEST)
            scores = low_back(raw * SCALING)
            probs = low(softmax_rows(jnp.where((owner == index)[None, :], scores, NEGATIVE)))
            return jnp.einsum('hj,jhd->hd', probs, values, precision=HIGHEST).reshape(width)
        return lax.map(jax.checkpoint(query_step), (query_rows, jnp.arange(N_TOK * QUERY_DEV, dtype=jnp.int32)))
    cross_out = low(low_back(lax.map(group_step, (grouped, owners, cross_query)).reshape(-1, width)))
    after_cross = after_self + low_back(matmul(cross_out, decoder[3]))
    final_in = low(rms_norm(after_cross, gains[4]))
    final_inner = low_back(matmul(final_in, expansion[0]))
    final_act = low(jax.nn.gelu(final_inner))
    return after_cross + low_back(jnp.einsum('if,df->id', final_act, expansion[1], precision=HIGHEST))

def update(weight, moment, average, gradient):
    new_moment = MOMENTUM * moment + gradient
    new_weight = weight - RATE * (gradient + MOMENTUM * new_moment)
    new_average = AVERAGING * average + (1.0 - AVERAGING) * new_weight
    return (new_moment, new_average, new_weight, new_weight.astype(jnp.bfloat16))

def reference(encoder_input, decoder_input, output_cotangent, pair_lengths, pair_offset, pair_query, attention_master, attention_moment, attention_average, feedforward_master, feedforward_moment, feedforward_average, decoder_master, decoder_moment, decoder_average, expansion_master, expansion_moment, expansion_average, gain_master, gain_moment, gain_average, bias_master, bias_moment, bias_average):
    position = jnp.arange(ROW, dtype=jnp.int32)
    ends = jnp.cumsum(pair_lengths, axis=1).astype(jnp.int32)
    segment = lax.optimization_barrier(jnp.sum((position[None, :, None] >= ends[:, None, :]).astype(jnp.int32), axis=2)).astype(jnp.int32)
    row_ids = jnp.arange(ROWS, dtype=jnp.int32)
    group = (row_ids // N_TOK).astype(jnp.int32)
    target = ((row_ids[:, None] % N_TOK + pair_offset[group]) % N_TOK).astype(jnp.int32)
    pair_owner = (target * QUERY_DEV + pair_query[group]).astype(jnp.int32)
    token_query = jnp.take_along_axis(pair_owner, segment, axis=1).astype(jnp.int32)

    def wrapped(encoder_x, decoder_x, attention_w, feedforward_w, decoder_w, expansion_w, gains, table):
        return forward(encoder_x, decoder_x, attention_w, feedforward_w, decoder_w, expansion_w, gains, table, segment, token_query)
    output, pullback = jax.vjp(wrapped, encoder_input.astype(jnp.float32), decoder_input.astype(jnp.float32), attention_master, feedforward_master, decoder_master, expansion_master, gain_master, bias_master)
    grads = pullback(output_cotangent.astype(jnp.float32))
    att_m, att_a, att_w, att_c = update(attention_master, attention_moment, attention_average, grads[2])
    ffn_m, ffn_a, ffn_w, ffn_c = update(feedforward_master, feedforward_moment, feedforward_average, grads[3])
    dec_m, dec_a, dec_w, dec_c = update(decoder_master, decoder_moment, decoder_average, grads[4])
    exp_m, exp_a, exp_w, exp_c = update(expansion_master, expansion_moment, expansion_average, grads[5])
    gain_m, gain_a, gain_w, gain_c = update(gain_master, gain_moment, gain_average, grads[6])
    bias_m, bias_a, bias_w, bias_c = update(bias_master, bias_moment, bias_average, grads[7])
    return (output, grads[0], grads[1], att_m, att_a, att_w, att_c, ffn_m, ffn_a, ffn_w, ffn_c, dec_m, dec_a, dec_w, dec_c, exp_m, exp_a, exp_w, exp_c, gain_m, gain_a, gain_w, gain_c, bias_m, bias_a, bias_w, bias_c)
```

```python
import jax
import jax.numpy as jnp
from jax import lax
from jax.experimental import pallas as pl
from jax.experimental.pallas import tpu as pltpu
from jax.sharding import PartitionSpec as P

EPSILON = 1e-06
SCALING = 0.125
NEGATIVE = -1e30
MOMENTUM = 0.5
AVERAGING = 0.5
RATE = 0.02
THRESHOLDS = (12, 16, 23, 32, 46, 64, 91)
BF = jnp.bfloat16
F32 = jnp.float32
QB = 128
DIAG = 512
SPAN = 3 * QB
VMEM = 48 * 2**20


def bucket_ids(relative):
    magnitude = jnp.abs(relative)
    bucket = jnp.minimum(magnitude, 8)
    for limit in THRESHOLDS:
        bucket = bucket + (magnitude >= limit).astype(jnp.int32)
    return bucket + 16 * (relative > 0).astype(jnp.int32)


def rms_norm(values, gain):
    return values * lax.rsqrt(jnp.mean(values * values, axis=-1, keepdims=True) + EPSILON) * gain


def dot_nn(left, right):
    return lax.dot_general(left, right, (((1,), (0,)), ((), ())), preferred_element_type=F32)


def dot_nt(left, right):
    return lax.dot_general(left, right, (((1,), (1,)), ((), ())), preferred_element_type=F32)


def dot_tn(left, right):
    return lax.dot_general(left, right, (((0,), (0,)), ((), ())), preferred_element_type=F32)


def norm_back(values, gain, upstream):
    result, pullback = jax.vjp(rms_norm, values, gain)
    return pullback(upstream)


def gelu_back(values, upstream):
    result, pullback = jax.vjp(jax.nn.gelu, values)
    return pullback(upstream)[0]


def update(weight, moment, average, gradient):
    new_moment = MOMENTUM * moment + gradient
    new_weight = weight - RATE * (gradient + MOMENTUM * new_moment)
    new_average = AVERAGING * average + (1.0 - AVERAGING) * new_weight
    return (new_moment, new_average, new_weight, new_weight.astype(BF))


def window(block, blocks):
    return max(0, block - 1) * QB, min(blocks, block + 2) * QB


def diagonal_onehot(buckets):
    place = jnp.arange(DIAG, dtype=jnp.int32)
    relative = jnp.where(place < SPAN, place, place - DIAG) - QB
    return (bucket_ids(relative)[:, None] == jnp.arange(buckets, dtype=jnp.int32)[None, :]).astype(
        F32
    )


def bias_tile(rows_ref, head):
    row = jnp.broadcast_to(rows_ref[0, head : head + 1, :], (QB, DIAG))
    return pltpu.roll(row, 0, 1, stride=1, stride_axis=0)[:, :SPAN]


def attention_kernel(q_ref, k_ref, v_ref, rows_ref, column_ref, line_ref, out_ref):
    blocks = q_ref.shape[0] // QB
    half = lax.broadcasted_iota(jnp.int32, (QB, QB), 1) < 64
    bias = [bias_tile(rows_ref, head) for head in range(2)]
    for block in range(blocks):
        low, high = window(block, blocks)
        off = low - (block - 1) * QB
        mine = pl.ds(block * QB, QB)
        query = q_ref[mine, :]
        same = column_ref[mine, :] == line_ref[:, low:high]
        outs = []
        for head in range(2):
            part = jnp.where(half if head == 0 else ~half, query, jnp.zeros((), BF))
            scores = dot_nt(part, k_ref[low:high, :]) * SCALING
            scores = jnp.where(same, scores + bias[head][:, off : off + high - low], NEGATIVE)
            expo = jnp.exp(scores - jnp.max(scores, axis=1, keepdims=True))
            probs = (expo * (1.0 / jnp.sum(expo, axis=1, keepdims=True))).astype(BF)
            outs.append(dot_nn(probs, v_ref[low:high, :]))
        out_ref[mine, :] = jnp.where(half, outs[0], outs[1]).astype(BF)


def attention_back_kernel(
    q_ref,
    k_ref,
    v_ref,
    up_ref,
    rows_ref,
    column_ref,
    line_ref,
    gq_ref,
    gk_ref,
    gv_ref,
    diag_ref,
    gk_sum,
    gv_sum,
    grid_sum,
):
    blocks = q_ref.shape[0] // QB
    lanes = lax.broadcasted_iota(jnp.int32, (QB, QB), 1)
    half = lanes < 64
    flip = (lax.broadcasted_iota(jnp.int32, (QB, QB), 0) + lanes == QB - 1).astype(BF)
    bias = [bias_tile(rows_ref, head) for head in range(2)]
    gk_sum[...] = jnp.zeros_like(gk_sum)
    gv_sum[...] = jnp.zeros_like(gv_sum)
    grid_sum[...] = jnp.zeros_like(grid_sum)
    for block in range(blocks):
        low, high = window(block, blocks)
        off = low - (block - 1) * QB
        span = high - low
        mine = pl.ds(block * QB, QB)
        query = q_ref[mine, :]
        up = up_ref[mine, :]
        same = column_ref[mine, :] == line_ref[:, low:high]
        outs = []
        gks = 0.0
        gvs = 0.0
        for head in range(2):
            keep = half if head == 0 else ~half
            query_part = jnp.where(keep, query, jnp.zeros((), BF))
            up_part = jnp.where(keep, up, jnp.zeros((), BF))
            scores = dot_nt(query_part, k_ref[low:high, :]) * SCALING
            scores = jnp.where(same, scores + bias[head][:, off : off + span], NEGATIVE)
            expo = jnp.exp(scores - jnp.max(scores, axis=1, keepdims=True))
            probs = expo * (1.0 / jnp.sum(expo, axis=1, keepdims=True))
            grad = dot_nt(up_part, v_ref[low:high, :])
            inner = jnp.sum(probs * grad, axis=1, keepdims=True)
            grad = (probs * (grad - inner)).astype(BF)
            outs.append(dot_nn(grad, k_ref[low:high, :]))
            gvs = gvs + dot_tn(probs.astype(BF), up_part)
            gks = gks + dot_tn(grad, query_part)
            grid_sum[head, :, off : off + span] += dot_nn(flip, grad)
        gk_sum[low:high, :] += gks
        gv_sum[low:high, :] += gvs
        gq_ref[mine, :] = (jnp.where(half, outs[0], outs[1]) * SCALING).astype(BF)
    gk_ref[...] = (gk_sum[...] * SCALING).astype(BF)
    gv_ref[...] = gv_sum[...].astype(BF)
    for head in range(2):
        rolled = pltpu.roll(grid_sum[head], DIAG - QB + 1, 1, stride=1, stride_axis=0)
        diag_ref[0, head : head + 1, :] = jnp.sum(rolled, axis=0, keepdims=True)


def attention_specs(length, slabs):
    slab = pl.BlockSpec((length, 128), lambda h: (0, h))
    rows = pl.BlockSpec((1, 2, DIAG), lambda h: (h, 0, 0))
    column = pl.BlockSpec((length, 1), lambda h: (0, 0))
    line = pl.BlockSpec((1, length), lambda h: (0, 0))
    return [slab] * slabs + [rows, column, line], slab, rows


def attention_forward(q, k, v, rows, segment):
    length, width = q.shape
    pairs = width // 128
    specs, slab, _ = attention_specs(length, 3)
    area = 24 * 164000
    return pl.pallas_call(
        attention_kernel,
        grid=(pairs,),
        in_specs=specs,
        out_specs=slab,
        out_shape=jax.ShapeDtypeStruct((length, width), BF),
        compiler_params=pltpu.CompilerParams(vmem_limit_bytes=VMEM),
        cost_estimate=pl.CostEstimate(
            flops=4 * area * 128, bytes_accessed=8 * length * width, transcendentals=area
        ),
    )(q, k, v, rows.reshape(pairs, 2, DIAG), segment[:, None], segment[None, :])


def attention_backward(q, k, v, up, rows, segment):
    length, width = q.shape
    pairs = width // 128
    specs, slab, rows_spec = attention_specs(length, 4)
    shape = jax.ShapeDtypeStruct((length, width), BF)
    area = 24 * 164000
    gq, gk, gv, diag = pl.pallas_call(
        attention_back_kernel,
        grid=(pairs,),
        in_specs=specs,
        out_specs=[slab] * 3 + [rows_spec],
        out_shape=[shape] * 3 + [jax.ShapeDtypeStruct((pairs, 2, DIAG), F32)],
        scratch_shapes=[
            pltpu.VMEM((length, 128), F32),
            pltpu.VMEM((length, 128), F32),
            pltpu.VMEM((2, QB, DIAG), F32),
        ],
        compiler_params=pltpu.CompilerParams(vmem_limit_bytes=VMEM),
        cost_estimate=pl.CostEstimate(
            flops=10 * area * 128, bytes_accessed=14 * length * width, transcendentals=area
        ),
    )(q, k, v, up, rows.reshape(pairs, 2, DIAG), segment[:, None], segment[None, :])
    return gq, gk, gv, diag.reshape(width // 64, DIAG)


class Net:
    def __init__(self):
        self.n_dp = lax.axis_size("dp")
        self.n_tok = lax.axis_size("tok")
        self.n_z = self.n_tok // 2
        self.tree = self.n_dp == 4 and self.n_z == 4
        dp, tok = lax.axis_index("dp"), lax.axis_index("tok")
        self.core, self.z = tok % 2, tok // 2
        self.x, self.y = dp % 2, dp // 2

    def tok_to(self, array, where):
        return lax.ppermute(array, "tok", [(t, where(t)) for t in range(self.n_tok)])

    def swap_core(self, array):
        return self.tok_to(array, lambda t: t ^ 1)

    def shift_z(self, array, by):
        return self.tok_to(array, lambda t: (t + 2 * by) % self.n_tok)

    def shift_tok(self, array, by):
        return self.tok_to(array, lambda t: (t + by) % self.n_tok) if by % self.n_tok else array

    def flip_dp(self, array, bit):
        return lax.ppermute(array, "dp", [(d, d ^ bit) for d in range(self.n_dp)])

    def swap_x(self, array):
        return self.flip_dp(array, 1)

    def swap_y(self, array):
        return self.flip_dp(array, 2)

    def own_first(self, array, axis=-1):
        low, high = jnp.split(array, 2, axis=axis)
        flipped = jnp.concatenate([high, low], axis=axis)
        return jnp.where(self.core == 0, array, flipped)


def place_kernel(meta_ref, *refs):
    pieces, out_ref, sems = refs[:8], refs[8], refs[9]
    half = out_ref.shape[2] // 2
    copies = []
    for index, piece in enumerate(pieces):
        for block in range(4):
            row = pl.multiple_of(meta_ref[(index % 4) * 4 + block], 48)
            column = pl.multiple_of(meta_ref[16 + index // 4], 128)
            copies.append(
                pltpu.make_async_copy(
                    piece.at[:, pl.ds(block * 48, 48), :],
                    out_ref.at[:, pl.ds(row, 48), pl.ds(column, half)],
                    sems.at[index * 4 + block],
                )
            )
            copies[-1].start()
    for copy in copies:
        copy.wait()


def place(net, mine, theirs, own_columns, own_rows):
    count, rows, half = mine[0].shape
    spots = []
    for dy in range(2):
        for dx in range(2):
            top = net.y ^ dy ^ (net.core if own_rows else 0)
            for block in range(4):
                spots.append((top * 2 + (net.x ^ dx)) * rows + (net.z + 1 + block) % 4 * 48)
    first = 0 if own_columns else net.core
    spots += [first * half, (1 - first) * half]
    meta = jnp.stack([jnp.asarray(spot, jnp.int32) for spot in spots])
    return pl.pallas_call(
        place_kernel,
        in_specs=[pl.BlockSpec(memory_space=pltpu.SMEM)] + [pl.BlockSpec(memory_space=pl.ANY)] * 8,
        out_specs=pl.BlockSpec(memory_space=pltpu.VMEM),
        out_shape=jax.ShapeDtypeStruct((count, 4 * rows, 2 * half), BF),
        scratch_shapes=[pltpu.SemaphoreType.DMA((32,))],
        compiler_params=pltpu.CompilerParams(vmem_limit_bytes=VMEM),
        cost_estimate=pl.CostEstimate(
            flops=0, bytes_accessed=count * rows * half * 32, transcendentals=0
        ),
    )(meta, *mine, *theirs)


def gather(net, shard, route, own_columns=True, own_rows=False):
    if not net.tree:
        whole = lax.all_gather(shard, ("dp", "tok"), axis=1, tiled=True)
        whole = net.own_first(whole, 2) if own_columns else whole
        return net.own_first(whole, 1) if own_rows else whole
    low, high = jnp.split(shard, 2, axis=2)
    keep = jnp.where(net.core == 0, low, high)
    got = net.swap_core(jnp.where(net.core == 0, high, low))
    chip = jnp.concatenate(
        [jnp.where(net.core == 0, keep, got), jnp.where(net.core == 0, got, keep)], axis=1
    )
    line = jnp.concatenate([net.shift_z(chip, by) for by in (3, 2, 1)] + [chip], axis=1)
    if route == 0:
        over_x = net.swap_x(line)
        mine = [line, over_x, net.swap_y(line), net.swap_y(over_x)]
    else:
        over_y = net.swap_y(line)
        mine = [line, net.swap_x(line), over_y, net.swap_x(over_y)]
    theirs = [net.swap_core(piece) for piece in mine]
    return place(net, mine, theirs, own_columns, own_rows)


def pick(array, index, axis):
    return lax.dynamic_index_in_dim(array, index, axis, keepdims=False)


def add(*parts):
    total = parts[0].astype(F32)
    for part in parts[1:]:
        total = total + part.astype(F32)
    return total


def scatter(net, grad, route):
    count, rows, columns = grad.shape
    if not net.tree:
        whole = net.own_first(grad, 2)
        total = lax.psum_scatter(whole, ("dp", "tok"), scatter_dimension=1, tiled=True)
        return total.astype(F32)
    half = columns // 2
    mine = grad[:, :, :half].reshape(count, 2, 2, rows // 4, half)
    got = net.swap_core(grad[:, :, half:]).reshape(count, 2, 2, rows // 4, half)
    steps = [(1, net.y, net.swap_y), (1, net.x, net.swap_x)]
    if route == 0:
        steps = [(2, net.x, net.swap_x), (1, net.y, net.swap_y)]
    for axis, index, swap in steps:
        sent = add(pick(mine, 1 - index, axis), pick(got, 1 - index, axis)).astype(BF)
        mine = add(pick(mine, index, axis), pick(got, index, axis)).astype(BF)
        got = swap(sent)
    mine = mine.reshape(count, 4, rows // 16, half)
    got = got.reshape(count, 4, rows // 16, half)
    parts = [pick(mine, net.z, 1), pick(got, net.z, 1)]
    for by in (1, 2, 3):
        to = (net.z + by) % 4
        parts.append(net.shift_z(add(pick(mine, to, 1), pick(got, to, 1)).astype(BF), by))
    total = add(*parts).reshape(count, 2, rows // 32, half)
    keep = pick(total, net.core, 1)
    other = net.swap_core(pick(total, 1 - net.core, 1))
    low = jnp.where(net.core == 0, keep, other)
    high = jnp.where(net.core == 0, other, keep)
    return jnp.concatenate([low, high], axis=2)


def gather_small(net, array):
    if not net.tree:
        return lax.all_gather(array, ("dp", "tok"), axis=0, tiled=True)
    array = jnp.concatenate([array] + [net.shift_z(array, by) for by in (1, 2, 3)], axis=0)
    array = jnp.concatenate([array, net.swap_x(array)], axis=0)
    array = jnp.concatenate([array, net.swap_y(array)], axis=0)
    return jnp.concatenate([array, net.swap_core(array)], axis=0)


def sum_small(net, array):
    bit = 1
    while bit < net.n_tok:
        array = array + net.tok_to(array, lambda t, bit=bit: t ^ bit)
        bit *= 2
    bit = 1
    while bit < net.n_dp:
        array = array + net.flip_dp(array, bit)
        bit *= 2
    return array


def per_device(
    encoder_input,
    decoder_input,
    output_cotangent,
    pair_lengths,
    pair_offset,
    pair_query,
    attention_master,
    attention_moment,
    attention_average,
    feedforward_master,
    feedforward_moment,
    feedforward_average,
    decoder_master,
    decoder_moment,
    decoder_average,
    expansion_master,
    expansion_moment,
    expansion_average,
    gain_master,
    gain_moment,
    gain_average,
    bias_master,
    bias_moment,
    bias_average,
):
    net = Net()
    attention_low = attention_master.astype(BF)
    feedforward_low = feedforward_master.astype(BF)
    decoder_low = decoder_master.astype(BF)
    expansion_low = expansion_master.astype(BF)
    w_qkv = gather(net, attention_low[:3], 0)
    w_out = gather(net, attention_low[3:4], 1, own_columns=False, own_rows=True)[0]
    w_up = gather(net, feedforward_low[:1], 1)[0]
    w_down = gather(net, feedforward_low[1:], 0)[0]
    w_cross = gather(net, attention_low[4:], 1)
    w_dec = gather(net, decoder_low, 0, own_columns=False)
    x_up = gather(net, expansion_low[:1], 1, own_columns=False)[0]
    x_down = gather(net, expansion_low[1:], 0, own_columns=False)[0]

    length = encoder_input.shape[1]
    width = encoder_input.shape[2]
    buckets, heads = bias_master.shape
    head_size = width // heads
    pairs = pair_lengths.shape[1]
    counter = jnp.arange(pairs, dtype=jnp.int32)
    hidden = encoder_input[0].astype(F32)
    lengths = pair_lengths[0]
    ends = jnp.sum(
        jnp.where(counter[:, None] <= counter[None, :], lengths[:, None], 0), axis=0
    )
    position = jnp.arange(length, dtype=jnp.int32)
    segment = jnp.sum((position[:, None] >= ends[None, :]).astype(jnp.int32), axis=1)
    onehot = diagonal_onehot(buckets)
    bias_rows = jnp.sum(bias_master.T[:, None, :] * onehot[None], axis=2)
    bias_rows = net.own_first(bias_rows, 0)

    normed = rms_norm(hidden, gain_master[0]).astype(BF)
    queries, keys, values = (dot_nn(normed, w_qkv[i]).astype(BF) for i in range(3))
    attended = attention_forward(queries, keys, values, bias_rows, segment)
    residual = hidden + dot_nn(attended, w_out)
    normed_two = rms_norm(residual, gain_master[1]).astype(BF)
    inner = dot_nn(normed_two, w_up)
    activated = jax.nn.gelu(inner).astype(BF)
    encoded = (residual + dot_nt(activated, w_down)).astype(BF)
    cross_keys = dot_nn(encoded, w_cross[0]).astype(BF)
    cross_values = dot_nn(encoded, w_cross[1]).astype(BF)

    offsets = pair_offset[0]
    owners = pair_query[0]
    half = pairs // 2
    shifts = list(range(half)) + [net.n_tok // 2 + index for index in range(half)]
    match = offsets[None, :] == jnp.asarray(shifts, jnp.int32)[:, None]
    slot_query = jnp.sum(jnp.where(match, owners[None, :], 0), axis=1)

    def to_owner(rows):
        ordered = jnp.sum(jnp.where(match[:, :, None], rows[None], 0.0), axis=1)
        return jnp.concatenate(
            [net.shift_tok(ordered[i : i + 1], shift) for i, shift in enumerate(shifts)], axis=0
        )

    def to_tokens(rows):
        got = jnp.concatenate(
            [
                net.shift_tok(rows[i : i + 1], net.n_tok - shift)
                for i, shift in enumerate(shifts)
            ],
            axis=0,
        )
        return jnp.sum(jnp.where(match[:, :, None], got[:, None], 0.0), axis=0)

    state = decoder_input.astype(F32)
    nquery = state.shape[0]
    of_slot = slot_query[:, None] == jnp.arange(nquery, dtype=jnp.int32)[None, :]

    def per_slot(rows):
        return jnp.sum(jnp.where(of_slot[:, :, None], rows[None], 0.0), axis=1)

    self_in = rms_norm(state, gain_master[2]).astype(BF)
    self_values = dot_nn(self_in, w_dec[0]).astype(BF)
    after_self = state + dot_nn(self_values, w_dec[1])
    cross_in = rms_norm(after_self, gain_master[3]).astype(BF)
    cross_query = dot_nn(cross_in, w_dec[2]).astype(BF)
    upstream = output_cotangent.astype(F32)
    up_low = output_cotangent.astype(BF)
    grad_act = dot_nn(up_low, x_down)

    head_mask = (
        jnp.arange(width, dtype=jnp.int32)[None, :] // head_size
        == jnp.arange(heads, dtype=jnp.int32)[:, None]
    )

    def by_head(rows):
        spread = jnp.where(head_mask[None], rows[:, None, :], 0.0)
        return spread.reshape(pairs * heads, width).astype(BF)

    def from_heads(rows):
        rows = rows.reshape(pairs, heads, width)
        return jnp.sum(jnp.where(head_mask[None], rows, 0.0), axis=1)

    token_query = net.own_first(to_tokens(per_slot(cross_query.astype(F32))))
    query_heads = by_head(token_query)
    inside = (segment[None, :] == counter[:, None])[:, None, :]
    scores = dot_nt(query_heads, cross_keys).reshape(pairs, heads, length) * SCALING
    scores = jnp.where(inside, scores, NEGATIVE)
    peak = jnp.max(scores, axis=2)
    expo = jnp.exp(scores - peak[:, :, None])
    total = jnp.sum(expo, axis=2)
    weighted = from_heads(
        lax.dot_general(
            expo.reshape(pairs * heads, length),
            cross_values.astype(F32),
            (((1,), (0,)), ((), ())),
            precision=lax.Precision.HIGHEST,
            preferred_element_type=F32,
        )
    )
    sent = jnp.concatenate(
        [net.own_first(weighted), net.own_first(peak), net.own_first(total)], axis=1
    )
    got = to_owner(sent)
    slot_peak, slot_total = got[:, width : width + heads], got[:, width + heads :]
    chosen = of_slot.T[:, :, None]
    row_peak = jnp.max(jnp.where(chosen, slot_peak[None], NEGATIVE), axis=1)
    factor = jnp.where(chosen, jnp.exp(slot_peak[None] - row_peak[:, None]), 0.0)
    row_total = jnp.sum(factor * slot_total[None], axis=1)
    factor = factor / row_total[:, None]
    wide = jnp.repeat(factor, head_size, axis=2)
    cross_wide = jnp.sum(wide * got[None, :, :width], axis=1)
    cross_out = cross_wide.astype(BF)
    row_log = row_peak + jnp.log(row_total)

    after_cross = after_self + dot_nn(cross_out, w_dec[3])
    final_in = rms_norm(after_cross, gain_master[4]).astype(BF)
    final_inner = dot_nn(final_in, x_up)
    grad_inner = gelu_back(final_inner, grad_act).astype(BF)
    grad_final_in = dot_nt(grad_inner, x_up)
    grad_state_four, grad_gain_four = norm_back(after_cross, gain_master[4], grad_final_in)
    grad_cross_total = upstream + grad_state_four
    cross_grad_low = grad_cross_total.astype(BF)
    grad_cross_out = dot_nt(cross_grad_low, w_dec[3]).astype(BF).astype(F32)
    row_inner = jnp.sum((grad_cross_out * cross_wide).reshape(nquery, heads, head_size), axis=2)
    back = to_tokens(per_slot(jnp.concatenate([grad_cross_out, row_log, row_inner], axis=1)))
    final_act = jax.nn.gelu(final_inner).astype(BF)
    decoder_output = after_cross + dot_nt(final_act, x_down)

    grad_heads = by_head(net.own_first(back[:, :width]))
    token_log = net.own_first(back[:, width : width + heads])
    token_inner = net.own_first(back[:, width + heads :])
    probs = jnp.exp(scores - token_log[:, :, None])
    grad_probs = dot_nt(grad_heads, cross_values).reshape(pairs, heads, length)
    grad_scores = (probs * (grad_probs - token_inner[:, :, None])).astype(BF)
    grad_scores = grad_scores.reshape(pairs * heads, length)
    probs_low = probs.reshape(pairs * heads, length).astype(BF)
    grad_values_cross = dot_tn(probs_low, grad_heads).astype(BF)
    grad_keys_cross = (dot_tn(grad_scores, query_heads) * SCALING).astype(BF)
    grad_query_part = from_heads(dot_nn(grad_scores, cross_keys))
    got_query = to_owner(net.own_first(grad_query_part))
    grad_query_cross = (
        jnp.sum(jnp.where(chosen, got_query[None], 0.0), axis=1) * SCALING
    ).astype(BF)
    grad_encoded = (
        dot_nt(grad_keys_cross, w_cross[0]) + dot_nt(grad_values_cross, w_cross[1])
    ).astype(BF)
    grad_cross_proj = jnp.stack(
        [dot_tn(encoded, grad_keys_cross).astype(BF), dot_tn(encoded, grad_values_cross).astype(BF)]
    )
    sum_cross = scatter(net, grad_cross_proj, 1)

    grad_cross_in = dot_nt(grad_query_cross, w_dec[2])
    grad_state_three, grad_gain_three = norm_back(after_self, gain_master[3], grad_cross_in)
    grad_self_total = grad_cross_total + grad_state_three
    self_grad_low = grad_self_total.astype(BF)
    grad_self_values = dot_nt(self_grad_low, w_dec[1]).astype(BF)
    grad_self_in = dot_nt(grad_self_values, w_dec[0])
    grad_state_two, grad_gain_two = norm_back(state, gain_master[2], grad_self_in)
    decoder_gradient = grad_self_total + grad_state_two
    packed = [
        self_in,
        self_values,
        cross_in,
        cross_out,
        final_in,
        up_low,
        grad_self_values,
        self_grad_low,
        grad_query_cross,
        cross_grad_low,
        grad_inner,
        final_act,
    ]
    spread = gather_small(net, jnp.concatenate(packed, axis=1))
    rank = lax.axis_index("dp") * net.n_tok + lax.axis_index("tok")
    own = decoder_master.shape[1]
    lefts = [
        lax.dynamic_slice_in_dim(spread, i * width + rank * own, own, axis=1) for i in range(6)
    ]
    rights = [spread[:, (6 + i) * width : (7 + i) * width] for i in range(4)]
    wide_size = final_act.shape[1]
    grad_dec = jnp.stack([dot_tn(lefts[i], rights[i]) for i in range(4)])
    grad_exp = jnp.stack(
        [
            dot_tn(lefts[4], spread[:, 10 * width : 10 * width + wide_size]),
            dot_tn(lefts[5], spread[:, 10 * width + wide_size :]),
        ]
    )

    grad_down = dot_tn(grad_encoded, activated).astype(BF)
    sum_down = scatter(net, grad_down[None], 0)
    grad_activated = dot_nn(grad_encoded, w_down)
    grad_inner_enc = gelu_back(inner, grad_activated).astype(BF)
    grad_up = dot_tn(normed_two, grad_inner_enc).astype(BF)
    sum_up = scatter(net, grad_up[None], 1)
    grad_normed_two = dot_nt(grad_inner_enc, w_up)
    grad_resid, grad_gain_one = norm_back(residual, gain_master[1], grad_normed_two)
    grad_residual = grad_encoded.astype(F32) + grad_resid
    attn_low = grad_residual.astype(BF)
    grad_out = dot_tn(net.own_first(attended), net.own_first(attn_low)).astype(BF)
    sum_out = scatter(net, grad_out[None], 0)
    grad_attended = dot_nt(attn_low, w_out).astype(BF)
    grad_queries, grad_keys, grad_values, diagonals = attention_backward(
        queries, keys, values, grad_attended, bias_rows, segment
    )
    grad_normed = (
        dot_nt(grad_queries, w_qkv[0])
        + dot_nt(grad_keys, w_qkv[1])
        + dot_nt(grad_values, w_qkv[2])
    )
    grad_qkv = jnp.stack(
        [dot_tn(normed, grad).astype(BF) for grad in (grad_queries, grad_keys, grad_values)]
    )
    sum_qkv = scatter(net, grad_qkv, 1)
    grad_input_part, grad_gain_zero = norm_back(hidden, gain_master[0], grad_normed)
    encoder_gradient = (grad_residual + grad_input_part)[None]

    grad_table = jnp.dot(
        net.own_first(diagonals, 0),
        onehot,
        precision=lax.Precision.HIGHEST,
        preferred_element_type=F32,
    ).T
    gain_grad = jnp.concatenate(
        [grad_gain_zero, grad_gain_one, grad_gain_two, grad_gain_three, grad_gain_four]
    )
    small = sum_small(net, jnp.concatenate([gain_grad, grad_table.reshape(-1)]))
    gain_sum = small[: 5 * width].reshape(5, width)
    bias_sum = small[5 * width :].reshape(buckets, heads)

    results = [decoder_output, encoder_gradient, decoder_gradient]
    groups = (
        (
            attention_master,
            attention_moment,
            attention_average,
            jnp.concatenate([sum_qkv, sum_out, sum_cross], axis=0),
        ),
        (
            feedforward_master,
            feedforward_moment,
            feedforward_average,
            jnp.concatenate([sum_up, sum_down], axis=0),
        ),
        (decoder_master, decoder_moment, decoder_average, grad_dec),
        (expansion_master, expansion_moment, expansion_average, grad_exp),
        (gain_master, gain_moment, gain_average, gain_sum),
        (bias_master, bias_moment, bias_average, bias_sum),
    )
    for weight, moment, average, gradient in groups:
        results.extend(update(weight, moment, average, gradient))
    return tuple(results)


def solution(mesh):
    spread = P(("dp", "tok"), None)
    weights = P(None, ("dp", "tok"), None)
    in_specs = (
        P(("dp", "tok"), None, None),
        spread,
        spread,
        spread,
        P("dp", None),
        P("dp", None),
        *[weights] * 12,
        *[P()] * 6,
    )
    out_specs = (spread, P(("dp", "tok"), None, None), spread, *[weights] * 16, *[P()] * 8)
    return jax.shard_map(
        per_device, mesh=mesh, in_specs=in_specs, out_specs=out_specs, check_vma=False
    )
```

```python
import jax
import jax.numpy as jnp
from jax import lax
from jax.experimental import pallas as pl
from jax.experimental.pallas import tpu as pltpu
from jax.sharding import PartitionSpec as P

EPSILON = 1e-06
SCALING = 0.125
NEGATIVE = -1e30
MOMENTUM = 0.5
AVERAGING = 0.5
RATE = 0.02
THRESHOLDS = (12, 16, 23, 32, 46, 64, 91)
BF = jnp.bfloat16
F32 = jnp.float32
QB = 128
DIAG = 512
SPAN = 3 * QB
VMEM = 48 * 2**20


def bucket_ids(relative):
    magnitude = jnp.abs(relative)
    bucket = jnp.minimum(magnitude, 8)
    for limit in THRESHOLDS:
        bucket = bucket + (magnitude >= limit).astype(jnp.int32)
    return bucket + 16 * (relative > 0).astype(jnp.int32)


def rms_norm(values, gain):
    return values * lax.rsqrt(jnp.mean(values * values, axis=-1, keepdims=True) + EPSILON) * gain


def dot_nn(left, right):
    return lax.dot_general(left, right, (((1,), (0,)), ((), ())), preferred_element_type=F32)


def dot_nt(left, right):
    return lax.dot_general(left, right, (((1,), (1,)), ((), ())), preferred_element_type=F32)


def dot_tn(left, right):
    return lax.dot_general(left, right, (((0,), (0,)), ((), ())), preferred_element_type=F32)


def norm_back(values, gain, upstream):
    result, pullback = jax.vjp(rms_norm, values, gain)
    return pullback(upstream)


def gelu_back(values, upstream):
    result, pullback = jax.vjp(jax.nn.gelu, values)
    return pullback(upstream)[0]


def update(weight, moment, average, gradient):
    new_moment = MOMENTUM * moment + gradient
    new_weight = weight - RATE * (gradient + MOMENTUM * new_moment)
    new_average = AVERAGING * average + (1.0 - AVERAGING) * new_weight
    return (new_moment, new_average, new_weight, new_weight.astype(BF))


def window(block, blocks):
    return max(0, block - 1) * QB, min(blocks, block + 2) * QB


def diagonal_onehot(buckets):
    place = jnp.arange(DIAG, dtype=jnp.int32)
    relative = jnp.where(place < SPAN, place, place - DIAG) - QB
    return (bucket_ids(relative)[:, None] == jnp.arange(buckets, dtype=jnp.int32)[None, :]).astype(
        F32
    )


def bias_tile(rows_ref, head):
    row = jnp.broadcast_to(rows_ref[0, head : head + 1, :], (QB, DIAG))
    return pltpu.roll(row, 0, 1, stride=1, stride_axis=0)[:, :SPAN]


def attention_kernel(q_ref, k_ref, v_ref, rows_ref, column_ref, line_ref, out_ref):
    blocks = q_ref.shape[0] // QB
    half = lax.broadcasted_iota(jnp.int32, (QB, QB), 1) < 64
    bias = [bias_tile(rows_ref, head) for head in range(2)]
    for block in range(blocks):
        low, high = window(block, blocks)
        off = low - (block - 1) * QB
        mine = pl.ds(block * QB, QB)
        query = q_ref[mine, :]
        same = column_ref[mine, :] == line_ref[:, low:high]
        outs = []
        for head in range(2):
            part = jnp.where(half if head == 0 else ~half, query, jnp.zeros((), BF))
            scores = dot_nt(part, k_ref[low:high, :]) * SCALING
            scores = jnp.where(same, scores + bias[head][:, off : off + high - low], NEGATIVE)
            expo = jnp.exp(scores - jnp.max(scores, axis=1, keepdims=True))
            probs = (expo * (1.0 / jnp.sum(expo, axis=1, keepdims=True))).astype(BF)
            outs.append(dot_nn(probs, v_ref[low:high, :]))
        out_ref[mine, :] = jnp.where(half, outs[0], outs[1]).astype(BF)


def attention_back_kernel(
    q_ref,
    k_ref,
    v_ref,
    up_ref,
    rows_ref,
    column_ref,
    line_ref,
    gq_ref,
    gk_ref,
    gv_ref,
    diag_ref,
    gk_sum,
    gv_sum,
    grid_sum,
):
    blocks = q_ref.shape[0] // QB
    lanes = lax.broadcasted_iota(jnp.int32, (QB, QB), 1)
    half = lanes < 64
    flip = (lax.broadcasted_iota(jnp.int32, (QB, QB), 0) + lanes == QB - 1).astype(BF)
    bias = [bias_tile(rows_ref, head) for head in range(2)]
    gk_sum[...] = jnp.zeros_like(gk_sum)
    gv_sum[...] = jnp.zeros_like(gv_sum)
    grid_sum[...] = jnp.zeros_like(grid_sum)
    for block in range(blocks):
        low, high = window(block, blocks)
        off = low - (block - 1) * QB
        span = high - low
        mine = pl.ds(block * QB, QB)
        query = q_ref[mine, :]
        up = up_ref[mine, :]
        same = column_ref[mine, :] == line_ref[:, low:high]
        outs = []
        gks = 0.0
        gvs = 0.0
        for head in range(2):
            keep = half if head == 0 else ~half
            query_part = jnp.where(keep, query, jnp.zeros((), BF))
            up_part = jnp.where(keep, up, jnp.zeros((), BF))
            scores = dot_nt(query_part, k_ref[low:high, :]) * SCALING
            scores = jnp.where(same, scores + bias[head][:, off : off + span], NEGATIVE)
            expo = jnp.exp(scores - jnp.max(scores, axis=1, keepdims=True))
            probs = expo * (1.0 / jnp.sum(expo, axis=1, keepdims=True))
            grad = dot_nt(up_part, v_ref[low:high, :])
            inner = jnp.sum(probs * grad, axis=1, keepdims=True)
            grad = (probs * (grad - inner)).astype(BF)
            outs.append(dot_nn(grad, k_ref[low:high, :]))
            gvs = gvs + dot_tn(probs.astype(BF), up_part)
            gks = gks + dot_tn(grad, query_part)
            grid_sum[head, :, off : off + span] += dot_nn(flip, grad)
        gk_sum[low:high, :] += gks
        gv_sum[low:high, :] += gvs
        gq_ref[mine, :] = (jnp.where(half, outs[0], outs[1]) * SCALING).astype(BF)
    gk_ref[...] = (gk_sum[...] * SCALING).astype(BF)
    gv_ref[...] = gv_sum[...].astype(BF)
    for head in range(2):
        rolled = pltpu.roll(grid_sum[head], DIAG - QB + 1, 1, stride=1, stride_axis=0)
        diag_ref[0, head : head + 1, :] = jnp.sum(rolled, axis=0, keepdims=True)


def attention_specs(length, slabs, first=0):
    slab = pl.BlockSpec((length, 128), lambda h: (0, h + first))
    rows = pl.BlockSpec((1, 2, DIAG), lambda h: (h + first, 0, 0))
    column = pl.BlockSpec((length, 1), lambda h: (0, 0))
    line = pl.BlockSpec((1, length), lambda h: (0, 0))
    out = pl.BlockSpec((length, 128), lambda h: (0, h))
    out_rows = pl.BlockSpec((1, 2, DIAG), lambda h: (h, 0, 0))
    return [slab] * slabs + [rows, column, line], out, out_rows


def attention_forward(q, k, v, rows, segment):
    length, width = q.shape
    pairs = width // 128
    specs, slab, _ = attention_specs(length, 3)
    area = 24 * 164000
    return pl.pallas_call(
        attention_kernel,
        grid=(pairs,),
        in_specs=specs,
        out_specs=slab,
        out_shape=jax.ShapeDtypeStruct((length, width), BF),
        compiler_params=pltpu.CompilerParams(vmem_limit_bytes=VMEM),
        cost_estimate=pl.CostEstimate(
            flops=20 * area * 128, bytes_accessed=8 * length * width, transcendentals=area
        ),
    )(q, k, v, rows.reshape(pairs, 2, DIAG), segment[:, None], segment[None, :])


def attention_backward(q, k, v, up, rows, segment, first, count):
    length, width = q.shape
    pairs = width // 128
    specs, slab, rows_spec = attention_specs(length, 4, first)
    shape = jax.ShapeDtypeStruct((length, count * 128), BF)
    area = 4 * count * 164000
    gq, gk, gv, diag = pl.pallas_call(
        attention_back_kernel,
        grid=(count,),
        in_specs=specs,
        out_specs=[slab] * 3 + [rows_spec],
        out_shape=[shape] * 3 + [jax.ShapeDtypeStruct((count, 2, DIAG), F32)],
        scratch_shapes=[
            pltpu.VMEM((length, 128), F32),
            pltpu.VMEM((length, 128), F32),
            pltpu.VMEM((2, QB, DIAG), F32),
        ],
        compiler_params=pltpu.CompilerParams(vmem_limit_bytes=VMEM),
        cost_estimate=pl.CostEstimate(
            flops=40 * area * 128, bytes_accessed=14 * length * width, transcendentals=area
        ),
    )(q, k, v, up, rows.reshape(pairs, 2, DIAG), segment[:, None], segment[None, :])
    return gq, gk, gv, diag.reshape(2 * count, DIAG)


def spread_heads(rows, lane_head, heads):
    parts = [jnp.where(lane_head == head, rows, 0.0) for head in range(heads)]
    return jnp.concatenate(parts, axis=0).astype(BF)


def own_turn(rows, core):
    return jnp.where(core == 0, rows, pltpu.roll(rows, rows.shape[1] // 2, 1))


def cross_setup(core_ref, query_ref, key_ref, line_ref, heads):
    core = core_ref[0]
    pairs, width = query_ref.shape
    lane_head = lax.broadcasted_iota(jnp.int32, (pairs, width), 1) // (width // heads)
    query_heads = spread_heads(own_turn(query_ref[...], core), lane_head, heads)
    scores = dot_nt(query_heads, key_ref[...]) * SCALING
    row = lax.broadcasted_iota(jnp.int32, scores.shape, 0)
    inside = lax.rem(row, pairs) == line_ref[...]
    return core, lane_head, query_heads, scores, inside


def gather_heads(rows, lane_head, heads, core):
    pairs = lane_head.shape[0]
    total = jnp.zeros(lane_head.shape, F32)
    for head in range(heads):
        total = jnp.where(lane_head == head, rows[head * pairs : (head + 1) * pairs], total)
    return own_turn(total, core)


def cross_kernel(core_ref, query_ref, key_ref, value_ref, line_ref, out_ref, *, heads):
    pairs, width = query_ref.shape
    core, lane_head, _, scores, inside = cross_setup(core_ref, query_ref, key_ref, line_ref, heads)
    scores = jnp.where(inside, scores, NEGATIVE)
    peak = jnp.max(scores, axis=1, keepdims=True)
    expo = jnp.exp(scores - peak)
    total = jnp.sum(expo, axis=1, keepdims=True)
    high = expo.astype(BF)
    low = (expo - high.astype(F32)).astype(BF)
    weighted = dot_nn(high, value_ref[...]) + dot_nn(low, value_ref[...])
    out_ref[:, :width] = gather_heads(weighted, lane_head, heads, core)
    lane = lax.broadcasted_iota(jnp.int32, (pairs, 128), 1)
    peaks = jnp.zeros((pairs, 128), F32)
    totals = jnp.ones((pairs, 128), F32)
    for head in range(heads):
        there = lane == lax.rem(head + core * (heads // 2), heads)
        part = slice(head * pairs, (head + 1) * pairs)
        peaks = jnp.where(there, peak[part], peaks)
        totals = jnp.where(there, total[part], totals)
    out_ref[:, width : width + 128] = peaks
    out_ref[:, width + 128 :] = totals


def cross_back_kernel(
    core_ref, query_ref, up_ref, stat_ref, key_ref, value_ref, line_ref, gk_ref, gv_ref, gq_ref, *, heads
):
    pairs, width = query_ref.shape
    core, lane_head, query_heads, scores, inside = cross_setup(
        core_ref, query_ref, key_ref, line_ref, heads
    )
    up_heads = spread_heads(own_turn(up_ref[...], core), lane_head, heads)
    lane = lax.broadcasted_iota(jnp.int32, (pairs, 128), 1)
    logs = []
    inners = []
    for head in range(heads):
        there = lane == lax.rem(head + core * (heads // 2), heads)
        logs.append(jnp.sum(jnp.where(there, stat_ref[:, :128], 0.0), axis=1, keepdims=True))
        inners.append(jnp.sum(jnp.where(there, stat_ref[:, 128:], 0.0), axis=1, keepdims=True))
    log = jnp.concatenate(logs, axis=0)
    inner = jnp.concatenate(inners, axis=0)
    probs = jnp.exp(jnp.where(inside, scores - log, NEGATIVE))
    grad = dot_nt(up_heads, value_ref[...])
    grad = (probs * (grad - inner)).astype(BF)
    gv_ref[...] = dot_tn(probs.astype(BF), up_heads).astype(BF)
    gk_ref[...] = (dot_tn(grad, query_heads) * SCALING).astype(BF)
    gq_ref[...] = gather_heads(dot_nn(grad, key_ref[...]), lane_head, heads, core)


def cross_forward(core, query, keys, values, segment, heads):
    pairs, width = query.shape
    vmem = pl.BlockSpec(memory_space=pltpu.VMEM)
    return pl.pallas_call(
        lambda *refs: cross_kernel(*refs, heads=heads),
        in_specs=[pl.BlockSpec(memory_space=pltpu.SMEM)] + [vmem] * 4,
        out_specs=vmem,
        out_shape=jax.ShapeDtypeStruct((pairs, width + 256), F32),
        compiler_params=pltpu.CompilerParams(vmem_limit_bytes=VMEM),
        cost_estimate=pl.CostEstimate(
            flops=6 * 96 * keys.size, bytes_accessed=4 * keys.size, transcendentals=96 * 512
        ),
    )(core.reshape(1), query, keys, values, segment[None, :])


def cross_backward(core, query, up, stat, keys, values, segment, heads):
    pairs, width = query.shape
    vmem = pl.BlockSpec(memory_space=pltpu.VMEM)
    grad = jax.ShapeDtypeStruct(keys.shape, BF)
    return pl.pallas_call(
        lambda *refs: cross_back_kernel(*refs, heads=heads),
        in_specs=[pl.BlockSpec(memory_space=pltpu.SMEM)] + [vmem] * 6,
        out_specs=[vmem] * 3,
        out_shape=[grad, grad, jax.ShapeDtypeStruct((pairs, width), F32)],
        compiler_params=pltpu.CompilerParams(vmem_limit_bytes=VMEM),
        cost_estimate=pl.CostEstimate(
            flops=10 * 96 * keys.size, bytes_accessed=8 * keys.size, transcendentals=96 * 512
        ),
    )(core.reshape(1), query, up, stat, keys, values, segment[None, :])


class Net:
    def __init__(self):
        self.n_dp = lax.axis_size("dp")
        self.n_tok = lax.axis_size("tok")
        self.n_z = self.n_tok // 2
        self.tree = self.n_dp == 4 and self.n_z == 4
        self.dp, self.tok = lax.axis_index("dp"), lax.axis_index("tok")
        self.core, self.z = self.tok % 2, self.tok // 2
        self.x, self.y = self.dp % 2, self.dp // 2

    def tok_to(self, array, where):
        return lax.ppermute(array, "tok", [(t, where(t)) for t in range(self.n_tok)])

    def swap_core(self, array):
        return self.tok_to(array, lambda t: t ^ 1)

    def shift_z(self, array, by):
        return self.tok_to(array, lambda t: (t + 2 * by) % self.n_tok)

    def flip_dp(self, array, bit):
        return lax.ppermute(array, "dp", [(d, d ^ bit) for d in range(self.n_dp)])

    def swap_x(self, array):
        return self.flip_dp(array, 1)

    def swap_y(self, array):
        return self.flip_dp(array, 2)

    def own_first(self, array, axis=-1):
        low, high = jnp.split(array, 2, axis=axis)
        flipped = jnp.concatenate([high, low], axis=axis)
        return jnp.where(self.core == 0, array, flipped)


def after(array, *others):
    if not others:
        return array
    return lax.optimization_barrier((array, *others))[0]


def place_kernel(meta_ref, *refs, plan, sources):
    outs, sems = refs[sources:-1], refs[-1]
    copies = []
    for source, row, spot, column, wide, target, flag in plan:
        top = pl.multiple_of(meta_ref[spot], 48)
        left = pl.multiple_of(meta_ref[flag[0]] * 128 + flag[1], 128)
        copies.append(
            pltpu.make_async_copy(
                refs[source].at[pl.ds(row, 48), pl.ds(column, wide)],
                outs[target].at[pl.ds(top, 48), pl.ds(left, wide)],
                sems.at[len(copies)],
            )
        )
        copies[-1].start()
    for copy in copies:
        copy.wait()


def place(net, pieces, widths, halves, own_columns, own_rows):
    spots = {}
    values = []

    def scalar(key, value):
        if key not in spots:
            spots[key] = len(values)
            values.append(jnp.asarray(value, jnp.int32))
        return spots[key]

    plan = []
    rows = 192
    for source, (array, corners, first, mine) in enumerate(pieces):
        for part, (dy, dx) in enumerate(corners):
            for block in range(4):
                for target, (half, start) in enumerate(zip(widths, halves)):
                    low = max(start, first)
                    high = min(start + half, first + array.shape[1])
                    if low >= high:
                        continue
                    flip = own_rows[target]
                    top = (net.y ^ dy ^ net.core) if flip else (net.y ^ dy)
                    spot = scalar(
                        (dy, dx, block, flip),
                        (top * 2 + (net.x ^ dx)) * rows + (net.z + 1 + block) % 4 * 48,
                    )
                    if own_columns[target]:
                        base = scalar("zero", 0)
                        shift = 0 if mine else half
                    else:
                        side = net.core if mine else 1 - net.core
                        base = scalar((mine, half), side * (half // 128))
                        shift = 0
                    plan.append(
                        (
                            source,
                            part * rows + block * 48,
                            spot,
                            low - first,
                            high - low,
                            target,
                            (base, shift + low - start),
                        )
                    )
    count = len(pieces)
    size = sum(widths) * 2 * 4 * rows
    return pl.pallas_call(
        lambda *refs: place_kernel(*refs, plan=plan, sources=count),
        in_specs=[pl.BlockSpec(memory_space=pltpu.SMEM)]
        + [pl.BlockSpec(memory_space=pl.ANY)] * count,
        out_specs=[pl.BlockSpec(memory_space=pltpu.VMEM)] * len(widths),
        out_shape=[jax.ShapeDtypeStruct((4 * rows, 2 * half), BF) for half in widths],
        scratch_shapes=[pltpu.SemaphoreType.DMA((len(plan),))],
        compiler_params=pltpu.CompilerParams(vmem_limit_bytes=VMEM),
        cost_estimate=pl.CostEstimate(flops=0, bytes_accessed=4 * size, transcendentals=0),
    )(jnp.stack(values), *[piece[0] for piece in pieces])


class Gather:
    def __init__(self, net, shards, own_columns, own_rows, cut, *ready):
        self.net, self.own_columns, self.own_rows, self.cut = net, own_columns, own_rows, cut
        self.shards = [after(shard, *ready).astype(BF) for shard in shards]
        self.widths = [shard.shape[1] // 2 for shard in shards]
        if not net.tree:
            return
        low = [shard[:, :half] for shard, half in zip(self.shards, self.widths)]
        high = [shard[:, half:] for shard, half in zip(self.shards, self.widths)]
        low, high = jnp.concatenate(low, axis=1), jnp.concatenate(high, axis=1)
        keep = jnp.where(net.core == 0, low, high)
        got = net.swap_core(jnp.where(net.core == 0, high, low))
        first = jnp.where(net.core == 0, keep, got)
        second = jnp.where(net.core == 0, got, keep)
        self.chip = jnp.concatenate([first, second], axis=0)

    def over_z(self, *ready):
        if not self.net.tree:
            return ()
        chip = after(self.chip, *ready)
        self.line = [self.net.shift_z(chip, by) for by in (3, 2, 1)] + [chip]
        return (chip,)

    def join(self, *ready):
        if not self.net.tree:
            return ()
        line = [after(part, *ready) for part in self.line]
        self.one = jnp.concatenate([part[:, : self.cut] for part in line], axis=0)
        self.two = jnp.concatenate([part[:, self.cut :] for part in line], axis=0)
        return (self.one, self.two)

    def first(self, ready=(), join=()):
        if not self.net.tree:
            return ()
        one, two = after(self.one, *ready), after(self.two, *ready)
        self.one = jnp.concatenate([one, after(self.net.swap_x(one), *join)], axis=0)
        self.two = jnp.concatenate([two, after(self.net.swap_y(two), *join)], axis=0)
        return (self.one, self.two)

    def second(self, ready=(), join=()):
        if not self.net.tree:
            return ()
        one, two = after(self.one, *ready), after(self.two, *ready)
        self.one_far = after(self.net.swap_y(one), *join)
        self.two_far = after(self.net.swap_x(two), *join)
        return (self.one_far, self.two_far)

    def finish(self):
        net = self.net
        if not net.tree:
            outs = []
            for shard, columns, rows in zip(self.shards, self.own_columns, self.own_rows):
                whole = lax.all_gather(shard, ("dp", "tok"), axis=0, tiled=True)
                whole = net.own_first(whole, 1) if columns else whole
                outs.append(net.own_first(whole, 0) if rows else whole)
            return outs
        pieces = []
        for array, corners, first in (
            (self.one, ((0, 0), (0, 1)), 0),
            (self.two, ((0, 0), (1, 0)), self.cut),
            (self.one_far, ((1, 0), (1, 1)), 0),
            (self.two_far, ((0, 1), (1, 1)), self.cut),
        ):
            pieces.append((array, corners, first, True))
            pieces.append((net.swap_core(array), corners, first, False))
        starts = [sum(self.widths[:i]) for i in range(len(self.widths))]
        return place(net, pieces, self.widths, starts, self.own_columns, self.own_rows)


def pick(array, index, axis):
    return lax.dynamic_index_in_dim(array, index, axis, keepdims=False)


def add(*parts):
    total = parts[0].astype(F32)
    for part in parts[1:]:
        total = total + part.astype(F32)
    return total


class Sum:
    def __init__(self, net, mine, theirs, cut):
        self.net, self.cut = net, cut
        self.mine, self.theirs = mine, theirs
        self.halves = [grad.shape[1] for grad in mine]
        if not net.tree:
            return
        rows, wide = mine[0].shape[0], sum(self.halves)
        self.rows, self.wide = rows, wide
        got = net.swap_core(jnp.concatenate(theirs, axis=1)).reshape(2, 2, rows // 4, wide)
        own = jnp.concatenate(mine, axis=1).reshape(2, 2, rows // 4, wide)
        self.parts = (own, got)

    def start(self, *join):
        if not self.net.tree:
            return
        own, got, cut = self.parts[0], after(self.parts[1], *join), self.cut
        one = (own[..., :cut], got[..., :cut])
        two = (own[..., cut:], got[..., cut:])
        self.one = [self.halve(one, 0, self.net.y, keep) for keep in (True, False)]
        self.two = [self.halve(two, 1, self.net.x, keep) for keep in (True, False)]

    def halve(self, parts, axis, index, keep):
        index = index if keep else 1 - index
        return add(*[pick(part, index, axis) for part in parts]).astype(BF)

    def state(self):
        return (*self.one, *self.two) if self.net.tree else ()

    def first(self, ready=(), join=()):
        if not self.net.tree:
            return
        net = self.net
        one = (self.one[0], after(net.swap_y(after(self.one[1], *ready)), *join))
        two = (self.two[0], after(net.swap_x(after(self.two[1], *ready)), *join))
        self.one = [self.halve(one, 0, net.x, keep) for keep in (True, False)]
        self.two = [self.halve(two, 0, net.y, keep) for keep in (True, False)]

    def second(self, ready=(), join=()):
        if not self.net.tree:
            return
        net = self.net
        one = (self.one[0], after(net.swap_x(after(self.one[1], *ready)), *join))
        two = (self.two[0], after(net.swap_y(after(self.two[1], *ready)), *join))
        shape = (4, self.rows // 16, -1)
        one, two = [part.reshape(shape) for part in one], [part.reshape(shape) for part in two]

        def chunk(at):
            sums = [add(*[pick(part, at, 0) for part in parts]) for parts in (one, two)]
            return jnp.concatenate(sums, axis=1)

        self.own = chunk(net.z)
        self.sent = [chunk((net.z + by) % 4).astype(BF) for by in (1, 2, 3)]

    def pending(self):
        return tuple(self.sent) if self.net.tree else ()

    def finish(self, ready=(), join=()):
        net = self.net
        if not net.tree:
            outs = []
            for mine, theirs in zip(self.mine, self.theirs):
                whole = net.own_first(jnp.concatenate([mine, theirs], axis=1), 1)
                total = lax.psum_scatter(whole, ("dp", "tok"), scatter_dimension=0, tiled=True)
                outs.append(total.astype(F32))
            return outs
        got = [
            after(net.shift_z(after(sent, *ready), by), *join)
            for by, sent in zip((1, 2, 3), self.sent)
        ]
        total = add(self.own, *got).reshape(2, self.rows // 32, self.wide)
        keep = pick(total, net.core, 0)
        other = net.swap_core(pick(total, 1 - net.core, 0))
        low = jnp.where(net.core == 0, keep, other)
        high = jnp.where(net.core == 0, other, keep)
        outs = []
        start = 0
        for half in self.halves:
            part = slice(start, start + half)
            outs.append(jnp.concatenate([low[:, part], high[:, part]], axis=1))
            start += half
        return outs


def gather_tok(net, array):
    if not net.tree:
        return lax.all_gather(array, "tok", axis=0), jnp.arange(net.n_tok, dtype=jnp.int32)
    steps = (0, 1, 2, 3)
    array = jnp.stack([array] + [net.shift_z(array, by) for by in steps[1:]])
    array = jnp.concatenate([array, net.swap_core(array)], axis=0)
    source = [(net.z - by) % 4 * 2 + net.core for by in steps]
    source += [(net.z - by) % 4 * 2 + 1 - net.core for by in steps]
    return array, jnp.stack(source).astype(jnp.int32)


def gather_dp(net, array):
    if not net.tree:
        whole = lax.all_gather(array, "dp", axis=0)
        order = net.dp ^ jnp.arange(net.n_dp, dtype=jnp.int32)
        same = order[:, None] == jnp.arange(net.n_dp, dtype=jnp.int32)[None, :]
        zero = jnp.zeros((), array.dtype)
        turned = jnp.sum(jnp.where(same[:, :, None, None], whole[None], zero), axis=1)
        return turned.reshape(-1, array.shape[1]).astype(array.dtype)
    array = jnp.concatenate([array, net.swap_x(array)], axis=0)
    return jnp.concatenate([array, net.swap_y(array)], axis=0)


def sum_small(net, array):
    bit = 1
    while bit < net.n_tok:
        array = array + net.tok_to(array, lambda t, bit=bit: t ^ bit)
        bit *= 2
    bit = 1
    while bit < net.n_dp:
        array = array + net.flip_dp(array, bit)
        bit *= 2
    return array


def per_device(
    encoder_input,
    decoder_input,
    output_cotangent,
    pair_lengths,
    pair_offset,
    pair_query,
    attention_master,
    attention_moment,
    attention_average,
    feedforward_master,
    feedforward_moment,
    feedforward_average,
    decoder_master,
    decoder_moment,
    decoder_average,
    expansion_master,
    expansion_moment,
    expansion_average,
    gain_master,
    gain_moment,
    gain_average,
    bias_master,
    bias_moment,
    bias_average,
):
    net = Net()
    length = encoder_input.shape[1]
    width = encoder_input.shape[2]
    buckets, heads = bias_master.shape
    head_size = width // heads
    pairs = pair_lengths.shape[1]
    nquery = decoder_input.shape[0]

    half = width // 2
    wide = feedforward_master.shape[2] // 2
    att = [attention_master[i] for i in range(6)]
    feed = [feedforward_master[i] for i in range(2)]
    dec = [decoder_master[i] for i in range(4)]
    expand = [expansion_master[i] for i in range(2)]
    get_att = Gather(net, att[:4], [True] * 3 + [False], [False] * 3 + [True], 2 * half)
    chip = get_att.over_z()
    both = jnp.concatenate([decoder_input, output_cotangent], axis=1)
    got, source = gather_tok(net, both)
    spot = source[None, :] == jnp.arange(net.n_tok, dtype=jnp.int32)[:, None]
    ordered = jnp.sum(jnp.where(spot[:, :, None, None], got[None], jnp.zeros((), BF)), axis=1)
    ordered = gather_dp(net, ordered.astype(BF).reshape(net.n_tok * nquery, 2 * width))
    get_feed = Gather(net, feed, [True] * 2, [False] * 2, wide, *chip)
    step = get_att.join()
    get_feed.over_z(*step)
    get_att.first((ordered,))
    step_att = get_att.second()
    get_dec = Gather(net, att[4:] + dec, [True] * 2 + [False] * 4, [False] * 6, 3 * half, *step)
    get_exp = Gather(net, expand, [True] * 2, [False] * 2, wide, *step)
    step_feed = get_feed.join(*step_att)
    get_dec.over_z(*step_feed)
    w_q, w_k, w_v, w_out = get_att.finish()

    counter = jnp.arange(pairs, dtype=jnp.int32)
    hidden = encoder_input[0].astype(F32)
    lengths = pair_lengths[0]
    ends = jnp.sum(jnp.where(counter[:, None] <= counter[None, :], lengths[:, None], 0), axis=0)
    position = jnp.arange(length, dtype=jnp.int32)
    segment = jnp.sum((position[:, None] >= ends[None, :]).astype(jnp.int32), axis=1)
    onehot = diagonal_onehot(buckets)
    bias_rows = jnp.sum(bias_master.T[:, None, :] * onehot[None], axis=2)
    bias_rows = net.own_first(bias_rows, 0)

    normed = rms_norm(hidden, gain_master[0]).astype(BF)
    queries, keys, values = (dot_nn(normed, weight).astype(BF) for weight in (w_q, w_k, w_v))
    feed_half = get_feed.first(join=(queries, keys, values))
    attended = attention_forward(after(queries, *feed_half), keys, values, bias_rows, segment)
    residual = hidden + dot_nn(attended, w_out)
    normed_two = rms_norm(residual, gain_master[1]).astype(BF)
    step_two = get_feed.second(join=(normed_two,))
    step_dec = get_dec.join(*step_two)
    get_exp.over_z(*step_dec)
    w_up, w_down = get_feed.finish()
    inner = dot_nn(normed_two, w_up)
    activated = jax.nn.gelu(inner).astype(BF)
    dec_half = get_dec.first(join=(activated,))
    encoded = (residual + dot_nt(after(activated, *dec_half), w_down)).astype(BF)
    step_three = get_dec.second(join=(encoded,))
    w_ck, w_cv, e_zero, e_one, e_two, e_three = get_dec.finish()
    cross_keys = dot_nn(encoded, w_ck).astype(BF)
    cross_values = dot_nn(encoded, w_cv).astype(BF)
    get_exp.join(*step_three)

    state = ordered[:, :width].astype(F32)
    up_low = ordered[:, width:]
    upstream = up_low.astype(F32)
    group = net.n_tok * nquery
    total_rows = state.shape[0]
    row_id = jnp.arange(total_rows, dtype=jnp.int32)
    own_row = (row_id // nquery == net.tok)[:, None]

    def own_rows(rows):
        return lax.dynamic_slice_in_dim(rows, net.tok * nquery, nquery, axis=0)

    self_in = rms_norm(state, gain_master[2]).astype(BF)
    self_values = dot_nn(self_in, e_zero).astype(BF)
    after_self = state + dot_nn(self_values, e_one)
    cross_in = rms_norm(after_self, gain_master[3]).astype(BF)
    cross_query = dot_nn(cross_in, e_two).astype(BF)

    offsets = pair_offset[0]
    owners = pair_query[0]
    query_id = jnp.arange(group, dtype=jnp.int32)
    own_id = (net.tok + offsets) % net.n_tok * nquery + owners
    own_match = own_id[:, None] == query_id[None, :]

    def at_pairs(rows):
        return jnp.sum(jnp.where(own_match[:, :, None], rows[None, :group].astype(F32), 0.0), axis=1)

    pair_match = (source[:, None] + offsets[None, :]) % net.n_tok * nquery + owners[None, :]
    pair_match = pair_match.reshape(1, -1) == query_id[:, None]

    def sum_pairs(rows):
        return lax.dot_general(
            pair_match.astype(F32),
            rows,
            (((1,), (0,)), ((), ())),
            precision=lax.Precision.HIGHEST,
            preferred_element_type=F32,
        )

    exp_half = get_exp.first(join=(cross_query, cross_keys, cross_values))
    pair_queries = at_pairs(after(cross_query, *exp_half))
    partial = cross_forward(net.core, pair_queries, cross_keys, cross_values, segment, heads)
    get_exp.second(join=(partial,))
    got, _ = gather_tok(net, partial)
    got = got.reshape(-1, width + 256)
    pair_peak = got[:, width : width + heads]
    pair_total = got[:, width + 128 : width + 128 + heads]
    row_peak = jnp.max(jnp.where(pair_match[:, :, None], pair_peak[None], NEGATIVE), axis=1)
    factor = jnp.where(pair_match[:, :, None], jnp.exp(pair_peak[None] - row_peak[:, None]), 0.0)
    row_total = jnp.sum(factor * pair_total[None], axis=1)
    factor = jnp.sum(factor / row_total[:, None], axis=0)
    cross_wide = sum_pairs(got[:, :width] * jnp.repeat(factor, head_size, axis=1))
    row_log = row_peak + jnp.log(row_total)
    cross_out = gather_dp(net, cross_wide.astype(BF))

    after_cross = after_self + dot_nn(cross_out, e_three)
    final_in = rms_norm(after_cross, gain_master[4]).astype(BF)
    x_up, x_down = get_exp.finish()
    grad_act = dot_nn(up_low, x_down)
    final_inner = dot_nn(final_in, x_up)
    grad_inner = gelu_back(final_inner, grad_act).astype(BF)
    grad_final_in = dot_nt(grad_inner, x_up)

    def decoder_norm_back(values, gain, up):
        grad, _ = norm_back(values, gain, up)
        _, grad_gain = norm_back(values, gain, jnp.where(own_row, up, 0.0))
        return grad, grad_gain

    grad_state_four, grad_gain_four = decoder_norm_back(after_cross, gain_master[4], grad_final_in)
    grad_cross_total = upstream + grad_state_four
    cross_grad_low = grad_cross_total.astype(BF)
    grad_cross_out = dot_nt(cross_grad_low, e_three)[:group].astype(BF).astype(F32)
    row_inner = jnp.sum((grad_cross_out * cross_wide).reshape(group, heads, head_size), axis=2)
    empty = jnp.zeros((group, 128 - heads), F32)
    back = at_pairs(jnp.concatenate([grad_cross_out, row_log, empty, row_inner, empty], axis=1))
    final_act = jax.nn.gelu(final_inner).astype(BF)
    decoder_output = own_rows(after_cross + dot_nt(final_act, x_down))

    grad_keys_cross, grad_values_cross, grad_query_part = cross_backward(
        net.core,
        pair_queries,
        back[:, :width],
        back[:, width:],
        cross_keys,
        cross_values,
        segment,
        heads,
    )
    grad_encoded = (dot_nt(grad_keys_cross, w_ck) + dot_nt(grad_values_cross, w_cv)).astype(BF)

    grad_down = [
        dot_tn(grad_encoded, part).astype(BF) for part in (activated[:, :wide], activated[:, wide:])
    ]
    crosses = [
        dot_tn(encoded, grad_keys_cross).astype(BF),
        dot_tn(encoded, grad_values_cross).astype(BF),
    ]
    down = Sum(
        net,
        [grad_down[0], *[grad[:, :half] for grad in crosses]],
        [grad_down[1], *[grad[:, half:] for grad in crosses]],
        3 * half,
    )
    grad_activated = dot_nn(after(grad_encoded, *grad_down, *crosses), w_down)
    grad_inner_enc = gelu_back(inner, grad_activated).astype(BF)
    down.start(grad_inner_enc)
    grad_inner_enc = after(grad_inner_enc, *down.state())
    grad_up = [
        dot_tn(normed_two, part).astype(BF)
        for part in (grad_inner_enc[:, :wide], grad_inner_enc[:, wide:])
    ]
    grad_normed_two = dot_nt(after(grad_inner_enc, *grad_up), w_up)
    grad_resid, grad_gain_one = norm_back(residual, gain_master[1], grad_normed_two)
    grad_residual = grad_encoded.astype(F32) + grad_resid
    attn_low = grad_residual.astype(BF)
    grad_out = dot_tn(net.own_first(attended), net.own_first(attn_low)).astype(BF)
    middle = Sum(
        net,
        [grad_up[0], grad_out[:, :half]],
        [grad_up[1], grad_out[:, half:]],
        7 * half // 3,
    )
    grad_attended = dot_nt(after(attn_low, grad_out), w_out).astype(BF)
    down.first(join=(grad_attended,))
    middle.start(grad_attended)
    grad_attended = after(grad_attended, *middle.state(), *down.state())
    blocks = width // 256

    def attention_part(up, first):
        grads = attention_backward(queries, keys, values, up, bias_rows, segment, first, blocks)
        return grads[:3], [dot_tn(normed, grad).astype(BF) for grad in grads[:3]], grads[3]

    their_grads, their_qkv, their_diagonals = attention_part(grad_attended, blocks)
    down.second(join=their_qkv)
    middle.first(join=their_qkv)
    own_up = after(grad_attended, *their_qkv, *down.pending(), *middle.state())
    own_grads, own_qkv, own_diagonals = attention_part(own_up, 0)
    last = Sum(net, own_qkv, their_qkv, 5 * half // 3)
    sum_down, sum_ck, sum_cv = down.finish(join=own_qkv)
    middle.second(join=own_qkv)
    diagonals = jnp.concatenate([own_diagonals, their_diagonals], axis=0)
    grad_normed = sum(
        dot_nt(jnp.concatenate([after(own, *own_qkv), their], axis=1), weight)
        for own, their, weight in zip(own_grads, their_grads, (w_q, w_k, w_v))
    )
    last.start(grad_normed)
    grad_input_part, grad_gain_zero = norm_back(hidden, gain_master[0], grad_normed)
    encoder_gradient = (grad_residual + grad_input_part)[None]

    got, _ = gather_tok(net, after(grad_query_part, *their_qkv))
    got = after(got, grad_normed)
    grad_query_cross = (sum_pairs(got.reshape(-1, width)) * SCALING).astype(BF)
    grad_query_cross = after(gather_dp(net, grad_query_cross), *last.state())
    grad_cross_in = dot_nt(grad_query_cross, e_two)
    grad_state_three, grad_gain_three = decoder_norm_back(
        after_self, gain_master[3], grad_cross_in
    )
    grad_self_total = grad_cross_total + grad_state_three
    self_grad_low = grad_self_total.astype(BF)
    grad_self_values = dot_nt(self_grad_low, e_one).astype(BF)
    grad_self_in = dot_nt(grad_self_values, e_zero)
    grad_state_two, grad_gain_two = decoder_norm_back(state, gain_master[2], grad_self_in)
    decoder_gradient = own_rows(grad_self_total + grad_state_two)
    own = decoder_master.shape[1]
    rank = net.dp * net.n_tok + net.tok

    def own_weight_rows(left, right):
        return dot_tn(lax.dynamic_slice_in_dim(left, rank * own, own, axis=1), right)

    grad_dec = jnp.stack(
        [
            own_weight_rows(self_in, grad_self_values),
            own_weight_rows(self_values, self_grad_low),
            own_weight_rows(cross_in, grad_query_cross),
            own_weight_rows(cross_out, cross_grad_low),
        ]
    )
    grad_exp = jnp.stack(
        [
            net.own_first(own_weight_rows(final_in, grad_inner)),
            net.own_first(own_weight_rows(up_low, final_act)),
        ]
    )

    last.first(join=(decoder_gradient,))
    sum_up, sum_out = middle.finish(join=(decoder_gradient,))
    last.second(join=(grad_dec, grad_exp))
    sum_q, sum_k, sum_v = last.finish()
    grad_table = jnp.dot(
        net.own_first(diagonals, 0),
        onehot,
        precision=lax.Precision.HIGHEST,
        preferred_element_type=F32,
    ).T
    gain_grad = jnp.concatenate(
        [grad_gain_zero, grad_gain_one, grad_gain_two, grad_gain_three, grad_gain_four]
    )
    small = sum_small(net, jnp.concatenate([gain_grad, grad_table.reshape(-1)]))
    gain_sum = small[: 5 * width].reshape(5, width)
    bias_sum = small[5 * width :].reshape(buckets, heads)

    results = [decoder_output, encoder_gradient, decoder_gradient]
    groups = (
        (
            attention_master,
            attention_moment,
            attention_average,
            jnp.stack([sum_q, sum_k, sum_v, sum_out, sum_ck, sum_cv]),
        ),
        (
            feedforward_master,
            feedforward_moment,
            feedforward_average,
            jnp.stack([sum_up, sum_down]),
        ),
        (decoder_master, decoder_moment, decoder_average, grad_dec),
        (expansion_master, expansion_moment, expansion_average, grad_exp),
        (gain_master, gain_moment, gain_average, gain_sum),
        (bias_master, bias_moment, bias_average, bias_sum),
    )
    for weight, moment, average, gradient in groups:
        results.extend(update(weight, moment, average, gradient))
    return tuple(results)


def solution(mesh):
    spread = P(("dp", "tok"), None)
    weights = P(None, ("dp", "tok"), None)
    in_specs = (
        P(("dp", "tok"), None, None),
        spread,
        spread,
        spread,
        P("dp", None),
        P("dp", None),
        *[weights] * 12,
        *[P()] * 6,
    )
    out_specs = (spread, P(("dp", "tok"), None, None), spread, *[weights] * 16, *[P()] * 8)
    return jax.shard_map(
        per_device, mesh=mesh, in_specs=in_specs, out_specs=out_specs, check_vma=False
    )
```

```python
import jax
import jax.numpy as jnp
from jax import lax
from jax.experimental import pallas as pl
from jax.experimental.pallas import tpu as pltpu
from jax.sharding import PartitionSpec as P

EPSILON = 1e-06
SCALING = 0.125
NEGATIVE = -1e30
MOMENTUM = 0.5
AVERAGING = 0.5
RATE = 0.02
THRESHOLDS = (12, 16, 23, 32, 46, 64, 91)
BF = jnp.bfloat16
F32 = jnp.float32
QB = 128
DIAG = 512
SPAN = 3 * QB
VMEM = 48 * 2**20


def cost(flops, count):
    return pl.CostEstimate(flops=flops, bytes_accessed=count, transcendentals=flops // 1024)


def bucket_ids(relative):
    magnitude = jnp.abs(relative)
    bucket = jnp.minimum(magnitude, 8)
    for limit in THRESHOLDS:
        bucket = bucket + (magnitude >= limit).astype(jnp.int32)
    return bucket + 16 * (relative > 0).astype(jnp.int32)


def rms_norm(values, gain):
    return values * lax.rsqrt(jnp.mean(values * values, axis=-1, keepdims=True) + EPSILON) * gain


def dot_nn(left, right):
    return lax.dot_general(left, right, (((1,), (0,)), ((), ())), preferred_element_type=F32)


def dot_nt(left, right):
    return lax.dot_general(left, right, (((1,), (1,)), ((), ())), preferred_element_type=F32)


def dot_tn(left, right):
    return lax.dot_general(left, right, (((0,), (0,)), ((), ())), preferred_element_type=F32)


def norm_back(values, gain, upstream):
    result, pullback = jax.vjp(rms_norm, values, gain)
    return pullback(upstream)


def gelu_back(values, upstream):
    result, pullback = jax.vjp(jax.nn.gelu, values)
    return pullback(upstream)[0]


def update(weight, moment, average, gradient):
    new_moment = MOMENTUM * moment + gradient
    new_weight = weight - RATE * (gradient + MOMENTUM * new_moment)
    new_average = AVERAGING * average + (1.0 - AVERAGING) * new_weight
    return (new_moment, new_average, new_weight, new_weight.astype(BF))


def window(block, blocks):
    return max(0, block - 1) * QB, min(blocks, block + 2) * QB


def diagonal_onehot(buckets):
    place = jnp.arange(DIAG, dtype=jnp.int32)
    relative = jnp.where(place < SPAN, place, place - DIAG) - QB
    return (bucket_ids(relative)[:, None] == jnp.arange(buckets, dtype=jnp.int32)[None, :]).astype(
        F32
    )


def bias_tile(rows_ref, head):
    row = jnp.broadcast_to(rows_ref[0, head : head + 1, :], (QB, DIAG))
    return pltpu.roll(row, 0, 1, stride=1, stride_axis=0)[:, :SPAN]


def attention_kernel(qkv_ref, rows_ref, column_ref, line_ref, out_ref):
    q_ref, k_ref, v_ref = (qkv_ref.at[:, i * 128 : (i + 1) * 128] for i in range(3))
    blocks = qkv_ref.shape[0] // QB
    half = lax.broadcasted_iota(jnp.int32, (QB, QB), 1) < 64
    bias = [bias_tile(rows_ref, head) for head in range(2)]
    for block in range(blocks):
        low, high = window(block, blocks)
        off = low - (block - 1) * QB
        mine = pl.ds(block * QB, QB)
        query = q_ref[mine, :]
        same = column_ref[mine, :] == line_ref[:, low:high]
        outs = []
        for head in range(2):
            part = jnp.where(half if head == 0 else ~half, query, jnp.zeros((), BF))
            scores = dot_nt(part, k_ref[low:high, :]) * SCALING
            scores = jnp.where(same, scores + bias[head][:, off : off + high - low], NEGATIVE)
            expo = jnp.exp(scores - jnp.max(scores, axis=1, keepdims=True))
            probs = (expo * (1.0 / jnp.sum(expo, axis=1, keepdims=True))).astype(BF)
            outs.append(dot_nn(probs, v_ref[low:high, :]))
        out_ref[mine, :] = jnp.where(half, outs[0], outs[1]).astype(BF)


def attention_back_kernel(
    qkv_ref,
    up_ref,
    rows_ref,
    column_ref,
    line_ref,
    grad_ref,
    diag_ref,
    gk_sum,
    gv_sum,
    grid_sum,
):
    q_ref, k_ref, v_ref = (qkv_ref.at[:, i * 128 : (i + 1) * 128] for i in range(3))
    blocks = qkv_ref.shape[0] // QB
    lanes = lax.broadcasted_iota(jnp.int32, (QB, QB), 1)
    half = lanes < 64
    flip = (lax.broadcasted_iota(jnp.int32, (QB, QB), 0) + lanes == QB - 1).astype(BF)
    bias = [bias_tile(rows_ref, head) for head in range(2)]
    gk_sum[...] = jnp.zeros_like(gk_sum)
    gv_sum[...] = jnp.zeros_like(gv_sum)
    grid_sum[...] = jnp.zeros_like(grid_sum)
    for block in range(blocks):
        low, high = window(block, blocks)
        off = low - (block - 1) * QB
        span = high - low
        mine = pl.ds(block * QB, QB)
        query = q_ref[mine, :]
        up = up_ref[mine, :]
        same = column_ref[mine, :] == line_ref[:, low:high]
        outs = []
        gks = 0.0
        gvs = 0.0
        for head in range(2):
            keep = half if head == 0 else ~half
            query_part = jnp.where(keep, query, jnp.zeros((), BF))
            up_part = jnp.where(keep, up, jnp.zeros((), BF))
            scores = dot_nt(query_part, k_ref[low:high, :]) * SCALING
            scores = jnp.where(same, scores + bias[head][:, off : off + span], NEGATIVE)
            expo = jnp.exp(scores - jnp.max(scores, axis=1, keepdims=True))
            probs = expo * (1.0 / jnp.sum(expo, axis=1, keepdims=True))
            grad = dot_nt(up_part, v_ref[low:high, :])
            inner = jnp.sum(probs * grad, axis=1, keepdims=True)
            grad = (probs * (grad - inner)).astype(BF)
            outs.append(dot_nn(grad, k_ref[low:high, :]))
            gvs = gvs + dot_tn(probs.astype(BF), up_part)
            gks = gks + dot_tn(grad, query_part)
            grid_sum[head, :, off : off + span] += dot_nn(flip, grad)
        gk_sum[low:high, :] += gks
        gv_sum[low:high, :] += gvs
        grad_ref[mine, :128] = (jnp.where(half, outs[0], outs[1]) * SCALING).astype(BF)
    grad_ref[:, 128:256] = (gk_sum[...] * SCALING).astype(BF)
    grad_ref[:, 256:] = gv_sum[...].astype(BF)
    for head in range(2):
        rolled = pltpu.roll(grid_sum[head], DIAG - QB + 1, 1, stride=1, stride_axis=0)
        diag_ref[0, head : head + 1, :] = jnp.sum(rolled, axis=0, keepdims=True)


def attention_specs(length, first=0):
    slab = pl.BlockSpec((length, 384), lambda h: (0, h + first))
    up = pl.BlockSpec((length, 128), lambda h: (0, h + first))
    rows = pl.BlockSpec((1, 2, DIAG), lambda h: (h + first, 0, 0))
    column = pl.BlockSpec((length, 1), lambda h: (0, 0))
    line = pl.BlockSpec((1, length), lambda h: (0, 0))
    return slab, up, [rows, column, line]


def attention_forward(qkv, rows, segment):
    length = qkv.shape[0]
    pairs = qkv.shape[1] // 384
    slab, up, others = attention_specs(length)
    return pl.pallas_call(
        attention_kernel,
        grid=(pairs,),
        in_specs=[slab, *others],
        out_specs=up,
        out_shape=jax.ShapeDtypeStruct((length, pairs * 128), BF),
        compiler_params=pltpu.CompilerParams(vmem_limit_bytes=VMEM),
        cost_estimate=cost(10 * 10**9, 4 * qkv.size),
    )(qkv, rows.reshape(pairs, 2, DIAG), segment[:, None], segment[None, :])


def attention_backward(qkv, up, rows, segment, first, count):
    length = qkv.shape[0]
    pairs = qkv.shape[1] // 384
    slab, up_spec, others = attention_specs(length, first)
    grads, diag = pl.pallas_call(
        attention_back_kernel,
        grid=(count,),
        in_specs=[slab, up_spec, *others],
        out_specs=[
            pl.BlockSpec((length, 384), lambda h: (0, h)),
            pl.BlockSpec((1, 2, DIAG), lambda h: (h, 0, 0)),
        ],
        out_shape=[
            jax.ShapeDtypeStruct((length, count * 384), BF),
            jax.ShapeDtypeStruct((count, 2, DIAG), F32),
        ],
        scratch_shapes=[
            pltpu.VMEM((length, 128), F32),
            pltpu.VMEM((length, 128), F32),
            pltpu.VMEM((2, QB, DIAG), F32),
        ],
        compiler_params=pltpu.CompilerParams(vmem_limit_bytes=VMEM),
        cost_estimate=cost(count * 3 * 10**9, 6 * qkv.size),
    )(qkv, up, rows.reshape(pairs, 2, DIAG), segment[:, None], segment[None, :])
    return grads, diag.reshape(2 * count, DIAG)


def spread_heads(rows, lane_head, heads):
    parts = [jnp.where(lane_head == head, rows, 0.0) for head in range(heads)]
    return jnp.concatenate(parts, axis=0).astype(BF)


def own_turn(rows, core):
    return jnp.where(core == 0, rows, pltpu.roll(rows, rows.shape[1] // 2, 1))


def cross_setup(core_ref, query_ref, key_ref, line_ref, heads):
    core = core_ref[0]
    pairs, width = query_ref.shape
    lane_head = lax.broadcasted_iota(jnp.int32, (pairs, width), 1) // (width // heads)
    query_heads = spread_heads(own_turn(query_ref[...], core), lane_head, heads)
    scores = dot_nt(query_heads, key_ref[...]) * SCALING
    row = lax.broadcasted_iota(jnp.int32, scores.shape, 0)
    inside = lax.rem(row, pairs) == line_ref[...]
    return core, lane_head, query_heads, scores, inside


def gather_heads(rows, lane_head, heads, core):
    pairs = lane_head.shape[0]
    total = jnp.zeros(lane_head.shape, F32)
    for head in range(heads):
        total = jnp.where(lane_head == head, rows[head * pairs : (head + 1) * pairs], total)
    return own_turn(total, core)


def cross_kernel(core_ref, query_ref, key_ref, value_ref, line_ref, out_ref, *, heads):
    pairs, width = query_ref.shape
    core, lane_head, _, scores, inside = cross_setup(core_ref, query_ref, key_ref, line_ref, heads)
    scores = jnp.where(inside, scores, NEGATIVE)
    peak = jnp.max(scores, axis=1, keepdims=True)
    expo = jnp.exp(scores - peak)
    total = jnp.sum(expo, axis=1, keepdims=True)
    high = expo.astype(BF)
    low = (expo - high.astype(F32)).astype(BF)
    weighted = dot_nn(high, value_ref[...]) + dot_nn(low, value_ref[...])
    out_ref[:, :width] = gather_heads(weighted, lane_head, heads, core)
    lane = lax.broadcasted_iota(jnp.int32, (pairs, 128), 1)
    peaks = jnp.zeros((pairs, 128), F32)
    totals = jnp.ones((pairs, 128), F32)
    for head in range(heads):
        there = lane == lax.rem(head + core * (heads // 2), heads)
        part = slice(head * pairs, (head + 1) * pairs)
        peaks = jnp.where(there, peak[part], peaks)
        totals = jnp.where(there, total[part], totals)
    out_ref[:, width : width + 128] = peaks
    out_ref[:, width + 128 :] = totals


def cross_back_kernel(
    core_ref, query_ref, up_ref, stat_ref, key_ref, value_ref, line_ref, gk_ref, gv_ref, gq_ref, *, heads
):
    pairs, width = query_ref.shape
    core, lane_head, query_heads, scores, inside = cross_setup(
        core_ref, query_ref, key_ref, line_ref, heads
    )
    up_heads = spread_heads(own_turn(up_ref[...], core), lane_head, heads)
    lane = lax.broadcasted_iota(jnp.int32, (pairs, 128), 1)
    logs = []
    inners = []
    for head in range(heads):
        there = lane == lax.rem(head + core * (heads // 2), heads)
        logs.append(jnp.sum(jnp.where(there, stat_ref[:, :128], 0.0), axis=1, keepdims=True))
        inners.append(jnp.sum(jnp.where(there, stat_ref[:, 128:], 0.0), axis=1, keepdims=True))
    log = jnp.concatenate(logs, axis=0)
    inner = jnp.concatenate(inners, axis=0)
    probs = jnp.exp(jnp.where(inside, scores - log, NEGATIVE))
    grad = dot_nt(up_heads, value_ref[...])
    grad = (probs * (grad - inner)).astype(BF)
    gv_ref[...] = dot_tn(probs.astype(BF), up_heads).astype(BF)
    gk_ref[...] = (dot_tn(grad, query_heads) * SCALING).astype(BF)
    gq_ref[...] = gather_heads(dot_nn(grad, key_ref[...]), lane_head, heads, core)


def cross_forward(core, query, keys, values, segment, heads):
    pairs, width = query.shape
    vmem = pl.BlockSpec(memory_space=pltpu.VMEM)
    return pl.pallas_call(
        lambda *refs: cross_kernel(*refs, heads=heads),
        in_specs=[pl.BlockSpec(memory_space=pltpu.SMEM)] + [vmem] * 4,
        out_specs=vmem,
        out_shape=jax.ShapeDtypeStruct((pairs, width + 256), F32),
        compiler_params=pltpu.CompilerParams(vmem_limit_bytes=VMEM),
        cost_estimate=cost(600 * keys.size, 4 * keys.size),
    )(core.reshape(1), query, keys, values, segment[None, :])


def cross_backward(core, query, up, stat, keys, values, segment, heads):
    pairs, width = query.shape
    vmem = pl.BlockSpec(memory_space=pltpu.VMEM)
    grad = jax.ShapeDtypeStruct(keys.shape, BF)
    return pl.pallas_call(
        lambda *refs: cross_back_kernel(*refs, heads=heads),
        in_specs=[pl.BlockSpec(memory_space=pltpu.SMEM)] + [vmem] * 6,
        out_specs=[vmem] * 3,
        out_shape=[grad, grad, jax.ShapeDtypeStruct((pairs, width), F32)],
        compiler_params=pltpu.CompilerParams(vmem_limit_bytes=VMEM),
        cost_estimate=cost(1000 * keys.size, 8 * keys.size),
    )(core.reshape(1), query, up, stat, keys, values, segment[None, :])


def combine_kernel(id_ref, part_ref, wide_ref, log_ref, *, heads):
    count, width = wide_ref.shape
    ids = id_ref[...]
    peak = part_ref[:, width : width + 128]
    total = part_ref[:, width + 128 :]
    factor = jnp.zeros(peak.shape, F32)
    for query in range(count):
        there = ids == query
        top = jnp.max(jnp.where(there, peak, NEGATIVE), axis=0, keepdims=True)
        expo = jnp.where(there, jnp.exp(jnp.minimum(peak - top, 0.0)), 0.0)
        mass = jnp.sum(expo * total, axis=0, keepdims=True)
        factor = factor + expo / mass
        log_ref[query : query + 1, :] = top + jnp.log(mass)
    lane_head = lax.broadcasted_iota(jnp.int32, (peak.shape[0], width), 1) // (width // heads)
    scale = jnp.zeros((peak.shape[0], width), F32)
    for head in range(heads):
        scale = jnp.where(lane_head == head, factor[:, head : head + 1], scale)
    scaled = part_ref[:, :width] * scale
    for query in range(count):
        rows = jnp.where(ids == query, scaled, 0.0)
        wide_ref[query : query + 1, :] = jnp.sum(rows, axis=0, keepdims=True)


def combine(ids, parts, count, width, heads):
    vmem = pl.BlockSpec(memory_space=pltpu.VMEM)
    return pl.pallas_call(
        lambda *refs: combine_kernel(*refs, heads=heads),
        in_specs=[vmem] * 2,
        out_specs=[vmem] * 2,
        out_shape=[
            jax.ShapeDtypeStruct((count, width), F32),
            jax.ShapeDtypeStruct((count, 128), F32),
        ],
        compiler_params=pltpu.CompilerParams(vmem_limit_bytes=VMEM),
        cost_estimate=cost(10 * parts.size, 4 * parts.size),
    )(ids, parts)


class Net:
    def __init__(self):
        self.n_dp = lax.axis_size("dp")
        self.n_tok = lax.axis_size("tok")
        self.n_z = self.n_tok // 2
        self.tree = self.n_dp == 4 and self.n_z == 4
        self.dp, self.tok = lax.axis_index("dp"), lax.axis_index("tok")
        self.core, self.z = self.tok % 2, self.tok // 2
        self.x, self.y = self.dp % 2, self.dp // 2

    def tok_to(self, array, where):
        return lax.ppermute(array, "tok", [(t, where(t)) for t in range(self.n_tok)])

    def swap_core(self, array):
        return self.tok_to(array, lambda t: t ^ 1)

    def shift_z(self, array, by):
        return self.tok_to(array, lambda t: (t + 2 * by) % self.n_tok)

    def flip_dp(self, array, bit):
        return lax.ppermute(array, "dp", [(d, d ^ bit) for d in range(self.n_dp)])

    def swap_x(self, array):
        return self.flip_dp(array, 1)

    def swap_y(self, array):
        return self.flip_dp(array, 2)

    def own_first(self, array, axis=-1):
        low, high = jnp.split(array, 2, axis=axis)
        flipped = jnp.concatenate([high, low], axis=axis)
        return jnp.where(self.core == 0, array, flipped)


def after(array, *others):
    if not others:
        return array
    return lax.optimization_barrier((array, *others))[0]


def copies_of(plan, meta_ref, sources, outs, sems):
    copies = []
    for source, row, spot, column, wide, target, flag in plan:
        top = pl.multiple_of(meta_ref[spot], 48)
        left = pl.multiple_of(meta_ref[flag[0]] * 128 + flag[1], 128)
        copies.append(
            pltpu.make_async_copy(
                sources[source].at[pl.ds(row, 48), pl.ds(column, wide)],
                outs[target].at[pl.ds(top, 48), pl.ds(left, wide)],
                sems.at[len(copies)],
            )
        )
    return copies


def layout(net, pieces, widths, halves, own_columns, own_rows):
    spots = {}
    values = []

    def scalar(key, value):
        if key not in spots:
            spots[key] = len(values)
            values.append(jnp.asarray(value, jnp.int32))
        return spots[key]

    plan = []
    rows = 192
    for source, (array, corners, first, mine) in enumerate(pieces):
        for part, (dy, dx) in enumerate(corners):
            for block in range(4):
                for target, (half, start) in enumerate(zip(widths, halves)):
                    low = max(start, first)
                    high = min(start + half, first + array.shape[1])
                    if low >= high:
                        continue
                    flip = own_rows[target]
                    top = (net.y ^ dy ^ net.core) if flip else (net.y ^ dy)
                    spot = scalar(
                        (dy, dx, block, flip),
                        (top * 2 + (net.x ^ dx)) * rows + (net.z + 1 + block) % 4 * 48,
                    )
                    if own_columns[target]:
                        base = scalar("zero", 0)
                        shift = 0 if mine else half
                    else:
                        side = net.core if mine else 1 - net.core
                        base = scalar((mine, half), side * (half // 128))
                        shift = 0
                    plan.append(
                        (
                            source,
                            part * rows + block * 48,
                            spot,
                            low - first,
                            high - low,
                            target,
                            (base, shift + low - start),
                        )
                    )
    return plan, jnp.stack(values)


def place_kernel(meta_ref, *refs, plan, sources):
    copies = copies_of(plan, meta_ref, refs[:sources], refs[sources:-1], refs[-1])
    for copy in copies:
        copy.start()
    for copy in copies:
        copy.wait()


def place(plan, values, arrays, widths):
    count = len(arrays)
    return pl.pallas_call(
        lambda *refs: place_kernel(*refs, plan=plan, sources=count),
        in_specs=[pl.BlockSpec(memory_space=pltpu.SMEM)]
        + [pl.BlockSpec(memory_space=pl.ANY)] * count,
        out_specs=[pl.BlockSpec(memory_space=pltpu.VMEM)] * len(widths),
        out_shape=[jax.ShapeDtypeStruct((768, 2 * half), BF) for half in widths],
        scratch_shapes=[pltpu.SemaphoreType.DMA((len(plan),))],
        compiler_params=pltpu.CompilerParams(vmem_limit_bytes=VMEM),
        cost_estimate=cost(1, 768 * sum(widths) * 8),
    )(values, *arrays)


def expand_kernel(meta_ref, in_ref, up_ref, *refs, plan, sources):
    act_ref, grad_ref, out_ref, back_ref, first_ref, second_ref, sems = refs[sources:]
    weights = (first_ref, second_ref)
    copies = copies_of(plan, meta_ref, refs[:sources], weights, sems)
    for copy in copies:
        copy.start()
    for copy, step in zip(copies, plan):
        if step[5] == 0:
            copy.wait()
    width = first_ref.shape[1]
    tile = width // 4
    inner = [dot_nn(in_ref[...], first_ref[:, t * tile : (t + 1) * tile]) for t in range(4)]
    for copy, step in zip(copies, plan):
        if step[5] == 1:
            copy.wait()
    out = jnp.zeros(out_ref.shape, F32)
    back = jnp.zeros(back_ref.shape, F32)
    for t in range(4):
        part = slice(t * tile, (t + 1) * tile)
        up = dot_nn(up_ref[...], second_ref[:, part])
        act = jax.nn.gelu(inner[t]).astype(BF)
        grad = gelu_back(inner[t], up).astype(BF)
        act_ref[:, part] = act
        grad_ref[:, part] = grad
        back = back + dot_nt(grad, first_ref[:, part])
        out = out + dot_nt(act, second_ref[:, part])
    out_ref[...] = out
    back_ref[...] = back


def expand(plan, values, arrays, inputs, up, width):
    count = len(arrays)
    rows, model = inputs.shape
    vmem = pl.BlockSpec(memory_space=pltpu.VMEM)
    wide = jax.ShapeDtypeStruct((rows, width), BF)
    small = jax.ShapeDtypeStruct((rows, model), F32)
    return pl.pallas_call(
        lambda *refs: expand_kernel(*refs, plan=plan, sources=count),
        in_specs=[pl.BlockSpec(memory_space=pltpu.SMEM), vmem, vmem]
        + [pl.BlockSpec(memory_space=pl.ANY)] * count,
        out_specs=[vmem] * 4,
        out_shape=[wide, wide, small, small],
        scratch_shapes=[
            pltpu.VMEM((model, width), BF),
            pltpu.VMEM((model, width), BF),
            pltpu.SemaphoreType.DMA((len(plan),)),
        ],
        compiler_params=pltpu.CompilerParams(vmem_limit_bytes=VMEM),
        cost_estimate=cost(8 * rows * model * width, 4 * model * width),
    )(values, inputs, up, *arrays)


class Gather:
    def __init__(self, net, shards, own_columns, own_rows, cut):
        self.net, self.own_columns, self.own_rows, self.cut = net, own_columns, own_rows, cut
        self.shards = [shard.astype(BF) for shard in shards]
        self.widths = [shard.shape[1] // 2 for shard in shards]

    def halves(self, extra=None):
        core = self.net.core
        low = [shard[:, :half] for shard, half in zip(self.shards, self.widths)]
        high = [shard[:, half:] for shard, half in zip(self.shards, self.widths)]
        low, high = jnp.concatenate(low, axis=1), jnp.concatenate(high, axis=1)
        keep, sent = jnp.where(core == 0, low, high), jnp.where(core == 0, high, low)
        if extra is not None:
            keep = jnp.concatenate([keep, extra], axis=1)
            sent = jnp.concatenate([sent, extra], axis=1)
        return keep, sent

    def take(self, keep, got):
        first = jnp.where(self.net.core == 0, keep, got)
        second = jnp.where(self.net.core == 0, got, keep)
        self.chip = jnp.concatenate([first, second], axis=0)

    def over_z(self, *ready):
        if not self.net.tree:
            return ()
        chip = after(self.chip, *ready)
        self.line = [self.net.shift_z(chip, by) for by in (3, 2, 1)] + [chip]
        return (chip,)

    def join(self, *ready):
        if not self.net.tree:
            return ()
        line = [after(part, *ready) for part in self.line]
        self.one = jnp.concatenate([part[:, : self.cut] for part in line], axis=0)
        self.two = jnp.concatenate([part[:, self.cut :] for part in line], axis=0)
        return (self.one, self.two)

    def first(self, ready=(), join=()):
        if not self.net.tree:
            return ()
        one, two = after(self.one, *ready), after(self.two, *ready)
        self.one = jnp.concatenate([one, after(self.net.swap_x(one), *join)], axis=0)
        self.two = jnp.concatenate([two, after(self.net.swap_y(two), *join)], axis=0)
        return (self.one, self.two)

    def second(self, ready=(), join=()):
        if not self.net.tree:
            return ()
        one, two = after(self.one, *ready), after(self.two, *ready)
        self.near = (self.net.swap_core(self.one), self.net.swap_core(self.two))
        self.one_far = after(self.net.swap_y(one), *join)
        self.two_far = after(self.net.swap_x(two), *join)
        return (self.one_far, self.two_far)

    def extras(self, count, *ready):
        net = self.net
        parts = []
        for array in (self.two, self.two_far):
            block = after(array, *ready)[:, -128:].reshape(2, 4, 2 * count, -1)
            order = (net.z + 1 + jnp.arange(4, dtype=jnp.int32)) % 4
            same = order[None, :] == jnp.arange(4, dtype=jnp.int32)[:, None]
            zero = jnp.zeros((), BF)
            turned = jnp.where(same[None, :, :, None, None], block[:, None], zero)
            turned = jnp.sum(turned, axis=2).astype(BF)
            parts.append(turned.reshape(2, 8 * count, -1))
        near, far = parts
        return jnp.concatenate([near[0], far[0], near[1], far[1]], axis=0)

    def finish(self):
        net = self.net
        if not net.tree:
            outs = []
            for shard, columns, rows in zip(self.shards, self.own_columns, self.own_rows):
                whole = lax.all_gather(shard, ("dp", "tok"), axis=0, tiled=True)
                whole = net.own_first(whole, 1) if columns else whole
                outs.append(net.own_first(whole, 0) if rows else whole)
            return outs
        plan, values, arrays = self.parts()
        return place(plan, values, arrays, self.widths)

    def parts(self):
        net = self.net
        pieces = []
        far = (net.swap_core(self.one_far), net.swap_core(self.two_far))
        for array, other, corners, first in (
            (self.one, self.near[0], ((0, 0), (0, 1)), 0),
            (self.two, self.near[1], ((0, 0), (1, 0)), self.cut),
            (self.one_far, far[0], ((1, 0), (1, 1)), 0),
            (self.two_far, far[1], ((0, 1), (1, 1)), self.cut),
        ):
            pieces.append((array, corners, first, True))
            pieces.append((other, corners, first, False))
        starts = [sum(self.widths[:i]) for i in range(len(self.widths))]
        plan, values = layout(net, pieces, self.widths, starts, self.own_columns, self.own_rows)
        return plan, values, [piece[0] for piece in pieces]


def between_cores(net, gathers, extra=None):
    if not net.tree:
        return
    keeps, sents = zip(*[one.halves(extra) for one in gathers])
    got = net.swap_core(jnp.concatenate(sents, axis=1))
    start = 0
    for one, keep in zip(gathers, keeps):
        one.take(keep, got[:, start : start + keep.shape[1]])
        start += keep.shape[1]


def pick(array, index, axis):
    return lax.dynamic_index_in_dim(array, index, axis, keepdims=False)


def add(*parts):
    total = parts[0].astype(F32)
    for part in parts[1:]:
        total = total + part.astype(F32)
    return total


class Sum:
    def __init__(self, net, theirs, cut):
        self.net, self.cut, self.theirs = net, cut, theirs
        self.halves = [grad.shape[1] for grad in theirs]
        self.rows, self.wide = theirs[0].shape[0], sum(self.halves)
        self.got = net.swap_core(jnp.concatenate(theirs, axis=1)) if net.tree else theirs[0]

    def start(self, mine, join=()):
        self.mine = mine
        if not self.net.tree:
            return
        cut, shape = self.cut, (2, 2, self.rows // 4, self.wide)
        own = jnp.concatenate(mine, axis=1).reshape(shape)
        got = after(self.got, *join).reshape(shape)
        one = (own[..., :cut], got[..., :cut])
        two = (own[..., cut:], got[..., cut:])
        self.one = [self.halve(one, 0, self.net.y, keep) for keep in (True, False)]
        self.two = [self.halve(two, 1, self.net.x, keep) for keep in (True, False)]

    def halve(self, parts, axis, index, keep):
        index = index if keep else 1 - index
        return add(*[pick(part, index, axis) for part in parts]).astype(BF)

    def state(self):
        return (*self.one, *self.two) if self.net.tree else ()

    def first(self, ready=(), join=()):
        if not self.net.tree:
            return
        net = self.net
        one = (self.one[0], after(net.swap_y(after(self.one[1], *ready)), *join))
        two = (self.two[0], after(net.swap_x(after(self.two[1], *ready)), *join))
        self.one = [self.halve(one, 0, net.x, keep) for keep in (True, False)]
        self.two = [self.halve(two, 0, net.y, keep) for keep in (True, False)]

    def second(self, ready=(), join=()):
        if not self.net.tree:
            return
        net = self.net
        one = (self.one[0], after(net.swap_x(after(self.one[1], *ready)), *join))
        two = (self.two[0], after(net.swap_y(after(self.two[1], *ready)), *join))
        shape = (4, self.rows // 16, -1)
        one, two = [part.reshape(shape) for part in one], [part.reshape(shape) for part in two]

        def chunk(at):
            sums = [add(*[pick(part, at, 0) for part in parts]) for parts in (one, two)]
            return jnp.concatenate(sums, axis=1)

        self.own = chunk(net.z)
        self.sent = [chunk((net.z + by) % 4).astype(BF) for by in (1, 2, 3)]

    def pending(self):
        return tuple(self.sent) if self.net.tree else ()


def finish(net, sums, join=()):
    if not net.tree:
        outs = []
        for one in sums:
            for mine, theirs in zip(one.mine, one.theirs):
                whole = net.own_first(jnp.concatenate([mine, theirs], axis=1), 1)
                total = lax.psum_scatter(whole, ("dp", "tok"), scatter_dimension=0, tiled=True)
                outs.append(total.astype(F32))
        return outs
    rows = sums[0].rows
    got = []
    for i, by in enumerate((1, 2, 3)):
        sent = jnp.concatenate([one.sent[i] for one in sums], axis=1)
        got.append(after(net.shift_z(sent, by), *join))
    total = add(jnp.concatenate([one.own for one in sums], axis=1), *got)
    total = total.reshape(2, rows // 32, -1)
    keep = pick(total, net.core, 0)
    other = net.swap_core(pick(total, 1 - net.core, 0))
    low = jnp.where(net.core == 0, keep, other)
    high = jnp.where(net.core == 0, other, keep)
    outs = []
    start = 0
    for half in [half for one in sums for half in one.halves]:
        part = slice(start, start + half)
        outs.append(jnp.concatenate([low[:, part], high[:, part]], axis=1))
        start += half
    return outs


def gather_tok(net, array, join=(), over_core=()):
    if not net.tree:
        return lax.all_gather(array, "tok", axis=0), jnp.arange(net.n_tok, dtype=jnp.int32)
    steps = (0, 1, 2, 3)
    array = jnp.stack([array] + [after(net.shift_z(array, by), *join) for by in steps[1:]])
    array = jnp.concatenate([array, after(net.swap_core(array), *over_core)], axis=0)
    source = [(net.z - by) % 4 * 2 + net.core for by in steps]
    source += [(net.z - by) % 4 * 2 + 1 - net.core for by in steps]
    return array, jnp.stack(source).astype(jnp.int32)


def gather_dp(net, array, over_x=(), over_y=()):
    if not net.tree:
        whole = lax.all_gather(array, "dp", axis=0)
        order = net.dp ^ jnp.arange(net.n_dp, dtype=jnp.int32)
        same = order[:, None] == jnp.arange(net.n_dp, dtype=jnp.int32)[None, :]
        zero = jnp.zeros((), array.dtype)
        turned = jnp.sum(jnp.where(same[:, :, None, None], whole[None], zero), axis=1)
        return turned.reshape(-1, array.shape[1]).astype(array.dtype)
    array = jnp.concatenate([array, after(net.swap_x(array), *over_x)], axis=0)
    return jnp.concatenate([array, after(net.swap_y(array), *over_y)], axis=0)


def sum_small(net, array, joins):
    joins = list(joins)
    bit = 1
    while bit < net.n_tok:
        other = net.tok_to(array, lambda t, bit=bit: t ^ bit)
        array = array + after(other, *(joins.pop(0) if joins else ()))
        bit *= 2
    bit = 1
    while bit < net.n_dp:
        array = array + after(net.flip_dp(array, bit), *(joins.pop(0) if joins else ()))
        bit *= 2
    return array


def per_device(
    encoder_input,
    decoder_input,
    output_cotangent,
    pair_lengths,
    pair_offset,
    pair_query,
    attention_master,
    attention_moment,
    attention_average,
    feedforward_master,
    feedforward_moment,
    feedforward_average,
    decoder_master,
    decoder_moment,
    decoder_average,
    expansion_master,
    expansion_moment,
    expansion_average,
    gain_master,
    gain_moment,
    gain_average,
    bias_master,
    bias_moment,
    bias_average,
):
    net = Net()
    length = encoder_input.shape[1]
    width = encoder_input.shape[2]
    buckets, heads = bias_master.shape
    head_size = width // heads
    pairs = pair_lengths.shape[1]
    nquery = decoder_input.shape[0]

    half = width // 2
    wide = feedforward_master.shape[2] // 2
    att = [attention_master[i] for i in range(6)]
    feed = [feedforward_master[i] for i in range(2)]
    dec = [decoder_master[i] for i in range(4)]
    widen = [expansion_master[i] for i in range(2)]
    three = jnp.transpose(
        attention_master[:3].astype(BF).reshape(3, -1, width // 128, 128), (1, 2, 0, 3)
    ).reshape(-1, 3 * width)
    both = jnp.concatenate([decoder_input, output_cotangent], axis=1)
    get_att = Gather(
        net,
        [three, att[3]],
        [True, False],
        [False, True],
        7 * half // 3 - 128,
    )
    between_cores(net, [get_att], both.reshape(-1, 128))
    early = get_att.over_z()
    feed, dec, widen, others = (
        [after(shard, *early) for shard in shards] for shards in (feed, dec, widen, att[4:])
    )
    get_feed = Gather(net, feed, [True] * 2, [False] * 2, wide)
    get_dec = Gather(net, others + dec, [True] * 2 + [False] * 4, [False] * 6, 3 * half)
    get_exp = Gather(net, widen, [True] * 2, [False] * 2, wide)
    between_cores(net, [get_feed, get_dec, get_exp])
    step = get_att.join()
    get_feed.over_z(*step)
    get_att.first()
    step_att = get_att.second()
    step_feed = get_feed.join(*step_att)
    get_dec.over_z(*step_feed)
    w_qkv, w_out = get_att.finish()

    counter = jnp.arange(pairs, dtype=jnp.int32)
    hidden = after(encoder_input, *early)[0].astype(F32)
    lengths = after(pair_lengths, *early)[0]
    ends = jnp.sum(jnp.where(counter[:, None] <= counter[None, :], lengths[:, None], 0), axis=0)
    position = jnp.arange(length, dtype=jnp.int32)
    segment = jnp.sum((position[:, None] >= ends[None, :]).astype(jnp.int32), axis=1)
    onehot = diagonal_onehot(buckets)
    bias_rows = jnp.sum(after(bias_master, *early).T[:, None, :] * onehot[None], axis=2)
    bias_rows = net.own_first(bias_rows, 0)

    normed = rms_norm(hidden, gain_master[0]).astype(BF)
    qkv = dot_nn(normed, w_qkv).astype(BF)
    feed_half = get_feed.first(join=(qkv,))
    attended = attention_forward(after(qkv, *feed_half), bias_rows, segment)
    residual = hidden + dot_nn(attended, w_out)
    normed_two = rms_norm(residual, gain_master[1]).astype(BF)
    step_two = get_feed.second(join=(normed_two,))
    step_dec = get_dec.join(*step_two)
    get_exp.over_z(*step_dec)
    w_up, w_down = get_feed.finish()
    dec_half = get_dec.first(join=(w_up, w_down))
    inner = dot_nn(after(normed_two, *dec_half), w_up)
    activated = jax.nn.gelu(inner).astype(BF)
    if net.tree:
        ordered = get_att.extras(nquery, activated)
    else:
        ordered = gather_dp(net, lax.all_gather(both, "tok", axis=0, tiled=True))
    encoded = (residual + dot_nt(activated, w_down)).astype(BF)
    step_three = get_dec.second(join=(encoded,))
    w_ck, w_cv, e_zero, e_one, e_two, e_three = get_dec.finish()
    cross_keys = dot_nn(encoded, w_ck).astype(BF)
    cross_values = dot_nn(encoded, w_cv).astype(BF)
    get_exp.join(*step_three)

    state = ordered[:, :width].astype(F32)
    up_low = ordered[:, width:]
    upstream = up_low.astype(F32)
    group = net.n_tok * nquery
    total_rows = state.shape[0]
    row_id = jnp.arange(total_rows, dtype=jnp.int32)
    own_row = (row_id // nquery == net.tok)[:, None]

    def own_rows(rows):
        return lax.dynamic_slice_in_dim(rows, net.tok * nquery, nquery, axis=0)

    self_in = rms_norm(state, gain_master[2]).astype(BF)
    self_values = dot_nn(self_in, e_zero).astype(BF)
    after_self = state + dot_nn(self_values, e_one)
    cross_in = rms_norm(after_self, gain_master[3]).astype(BF)
    cross_query = dot_nn(cross_in, e_two).astype(BF)

    offsets = pair_offset[0]
    owners = pair_query[0]
    query_id = jnp.arange(group, dtype=jnp.int32)
    own_id = (net.tok + offsets) % net.n_tok * nquery + owners
    own_match = own_id[:, None] == query_id[None, :]

    def at_pairs(rows):
        return jnp.sum(jnp.where(own_match[:, :, None], rows[None, :group].astype(F32), 0.0), axis=1)

    exp_half = get_exp.first(join=(cross_query,))
    pair_queries = at_pairs(after(cross_query, *exp_half))
    get_exp.second()
    partial = cross_forward(net.core, pair_queries, cross_keys, cross_values, segment, heads)
    got, source = gather_tok(net, after(partial, *get_exp.near) if net.tree else partial)
    pair_id = (source[:, None] + offsets[None, :]) % net.n_tok * nquery + owners[None, :]
    pair_match = pair_id.reshape(1, -1) == query_id[:, None]

    def sum_pairs(rows):
        return lax.dot_general(
            pair_match.astype(F32),
            rows,
            (((1,), (0,)), ((), ())),
            precision=lax.Precision.HIGHEST,
            preferred_element_type=F32,
        )

    got = got.reshape(-1, width + 256)
    cross_wide, row_log = combine(pair_id.reshape(-1, 1), got, group, width, heads)
    cross_out = gather_dp(net, cross_wide.astype(BF))

    after_cross = after_self + dot_nn(cross_out, e_three)
    final_in = rms_norm(after_cross, gain_master[4]).astype(BF)
    if net.tree:
        final_act, grad_inner, final_out, grad_final_in = expand(
            *get_exp.parts(), final_in, up_low, 2 * wide
        )
    else:
        x_up, x_down = get_exp.finish()
        grad_act = dot_nn(up_low, x_down)
        final_inner = dot_nn(final_in, x_up)
        grad_inner = gelu_back(final_inner, grad_act).astype(BF)
        grad_final_in = dot_nt(grad_inner, x_up)
        final_act = jax.nn.gelu(final_inner).astype(BF)
        final_out = dot_nt(final_act, x_down)

    def decoder_norm_back(values, gain, up):
        grad, _ = norm_back(values, gain, up)
        _, grad_gain = norm_back(values, gain, jnp.where(own_row, up, 0.0))
        return grad, grad_gain

    grad_state_four, grad_gain_four = decoder_norm_back(after_cross, gain_master[4], grad_final_in)
    grad_cross_total = upstream + grad_state_four
    cross_grad_low = grad_cross_total.astype(BF)
    grad_cross_out = dot_nt(cross_grad_low, e_three)[:group].astype(BF).astype(F32)
    row_inner = jnp.sum((grad_cross_out * cross_wide).reshape(group, heads, head_size), axis=2)
    empty = jnp.zeros((group, 128 - heads), F32)
    back = at_pairs(jnp.concatenate([grad_cross_out, row_log, row_inner, empty], axis=1))
    decoder_output = own_rows(after_cross + final_out)

    grad_keys_cross, grad_values_cross, grad_query_part = cross_backward(
        net.core,
        pair_queries,
        back[:, :width],
        back[:, width:],
        cross_keys,
        cross_values,
        segment,
        heads,
    )
    grad_encoded = (dot_nt(grad_keys_cross, w_ck) + dot_nt(grad_values_cross, w_cv)).astype(BF)

    grad_down = [
        dot_tn(grad_encoded, part).astype(BF) for part in (activated[:, :wide], activated[:, wide:])
    ]
    crosses = [
        dot_tn(encoded, grad_keys_cross).astype(BF),
        dot_tn(encoded, grad_values_cross).astype(BF),
    ]
    down = Sum(net, [grad_down[1], *[grad[:, half:] for grad in crosses]], 3 * half)
    grad_activated = dot_nn(after(grad_encoded, *grad_down, *crosses), w_down)
    grad_inner_enc = gelu_back(inner, grad_activated).astype(BF)
    own_down = [grad_down[0], *[grad[:, :half] for grad in crosses]]
    down.start(own_down, (grad_inner_enc,))
    grad_inner_enc = after(grad_inner_enc, *down.state())
    grad_up = [
        dot_tn(normed_two, part).astype(BF)
        for part in (grad_inner_enc[:, :wide], grad_inner_enc[:, wide:])
    ]
    grad_normed_two = dot_nt(after(grad_inner_enc, *grad_up), w_up)
    grad_resid, grad_gain_one = norm_back(residual, gain_master[1], grad_normed_two)
    grad_residual = grad_encoded.astype(F32) + grad_resid
    attn_low = grad_residual.astype(BF)
    down.first()
    got_query, _ = gather_tok(net, after(grad_query_part, grad_inner_enc))
    ready_low = after(attn_low, *down.state(), got_query)
    grad_out = dot_tn(net.own_first(attended), net.own_first(ready_low)).astype(BF)
    middle = Sum(net, [grad_up[1], grad_out[:, half:]], 7 * half // 3)
    grad_attended = dot_nt(after(attn_low, grad_out), w_out).astype(BF)
    middle.start([grad_up[0], grad_out[:, :half]])
    grad_attended = after(grad_attended, *middle.state(), *down.state())
    blocks = width // 256

    def attention_part(up, first):
        return attention_backward(qkv, up, bias_rows, segment, first, blocks)

    their_grads, their_diagonals = attention_part(grad_attended, blocks)
    down.second(join=(their_grads,))
    middle.first(join=(their_grads,))
    their_left = after(normed, *down.pending(), *middle.state())
    their_qkv = dot_tn(their_left, their_grads).astype(BF)
    last = Sum(net, [their_qkv], 5 * half // 3)
    middle.second(join=(their_qkv,))
    grad_query_cross = (sum_pairs(got_query.reshape(-1, width)) * SCALING).astype(BF)
    grad_query_cross = gather_dp(net, grad_query_cross, (their_grads,), (their_qkv,))
    own_up = after(grad_attended, last.got, grad_query_cross, *middle.pending())
    own_grads, own_diagonals = attention_part(own_up, 0)
    own_qkv = dot_tn(normed, own_grads).astype(BF)
    last.start([own_qkv])
    diagonals = jnp.concatenate([own_diagonals, their_diagonals], axis=0)
    own_grads = after(own_grads, *last.state())
    grad_normed = dot_nt(jnp.concatenate([own_grads, their_grads], axis=1), w_qkv)
    grad_input_part, grad_gain_zero = norm_back(hidden, gain_master[0], grad_normed)
    encoder_gradient = (grad_residual + grad_input_part)[None]

    grad_query_cross = after(grad_query_cross, own_grads)
    grad_cross_in = dot_nt(grad_query_cross, e_two)
    grad_state_three, grad_gain_three = decoder_norm_back(
        after_self, gain_master[3], grad_cross_in
    )
    grad_self_total = grad_cross_total + grad_state_three
    self_grad_low = grad_self_total.astype(BF)
    grad_self_values = dot_nt(self_grad_low, e_one).astype(BF)
    grad_self_in = dot_nt(grad_self_values, e_zero)
    grad_state_two, grad_gain_two = decoder_norm_back(state, gain_master[2], grad_self_in)
    decoder_gradient = own_rows(grad_self_total + grad_state_two)
    own = decoder_master.shape[1]
    rank = net.dp * net.n_tok + net.tok

    def own_weight_rows(left, right):
        return dot_tn(lax.dynamic_slice_in_dim(left, rank * own, own, axis=1), right)

    grad_dec = jnp.stack(
        [
            own_weight_rows(self_in, grad_self_values),
            own_weight_rows(self_values, self_grad_low),
            own_weight_rows(cross_in, grad_query_cross),
            own_weight_rows(cross_out, cross_grad_low),
        ]
    )
    grad_exp = jnp.stack(
        [
            net.own_first(own_weight_rows(final_in, grad_inner)),
            net.own_first(own_weight_rows(up_low, final_act)),
        ]
    )

    sum_down, sum_ck, sum_cv, sum_up, sum_out = finish(net, [down, middle], (own_qkv,))
    last.first(join=(encoder_gradient,))
    after_first = last.state()
    last.second()
    after_second = last.pending()
    (sum_three,) = finish(net, [last])
    grad_table = jnp.dot(
        net.own_first(diagonals, 0),
        onehot,
        precision=lax.Precision.HIGHEST,
        preferred_element_type=F32,
    ).T
    gain_grad = jnp.concatenate(
        [grad_gain_zero, grad_gain_one, grad_gain_two, grad_gain_three, grad_gain_four]
    )
    small = jnp.concatenate([gain_grad, grad_table.reshape(-1)])
    joins = [(encoder_gradient,), after_first, after_first, after_second]
    small = sum_small(net, small, joins)
    gain_sum = small[: 5 * width].reshape(5, width)
    bias_sum = small[5 * width :].reshape(buckets, heads)

    sum_three = jnp.transpose(sum_three.reshape(own, width // 128, 3, 128), (2, 0, 1, 3))
    sum_three = sum_three.reshape(3, own, width)
    results = [decoder_output, encoder_gradient, decoder_gradient]
    groups = (
        (
            attention_master,
            attention_moment,
            attention_average,
            jnp.concatenate([sum_three, jnp.stack([sum_out, sum_ck, sum_cv])], axis=0),
        ),
        (
            feedforward_master,
            feedforward_moment,
            feedforward_average,
            jnp.stack([sum_up, sum_down]),
        ),
        (decoder_master, decoder_moment, decoder_average, grad_dec),
        (expansion_master, expansion_moment, expansion_average, grad_exp),
        (gain_master, gain_moment, gain_average, gain_sum),
        (bias_master, bias_moment, bias_average, bias_sum),
    )
    for weight, moment, average, gradient in groups:
        results.extend(update(weight, moment, average, gradient))
    return tuple(results)


def solution(mesh):
    spread = P(("dp", "tok"), None)
    weights = P(None, ("dp", "tok"), None)
    in_specs = (
        P(("dp", "tok"), None, None),
        spread,
        spread,
        spread,
        P("dp", None),
        P("dp", None),
        *[weights] * 12,
        *[P()] * 6,
    )
    out_specs = (spread, P(("dp", "tok"), None, None), spread, *[weights] * 16, *[P()] * 8)
    return jax.shard_map(
        per_device, mesh=mesh, in_specs=in_specs, out_specs=out_specs, check_vma=False
    )
```

```python
import jax
import jax.numpy as jnp
from jax import lax
from jax.experimental import pallas as pl
from jax.experimental.pallas import tpu as pltpu
from jax.sharding import PartitionSpec as P

EPSILON = 1e-06
SCALING = 0.125
NEGATIVE = -1e30
MOMENTUM = 0.5
AVERAGING = 0.5
RATE = 0.02
THRESHOLDS = (12, 16, 23, 32, 46, 64, 91)
BF = jnp.bfloat16
F32 = jnp.float32
QB = 128
DIAG = 6 * QB
VMEM = 48 * 2**20


def cost(flops, count):
    return pl.CostEstimate(flops=flops, bytes_accessed=count, transcendentals=flops // 1024)


def bucket_ids(relative):
    magnitude = jnp.abs(relative)
    bucket = jnp.minimum(magnitude, 8)
    for limit in THRESHOLDS:
        bucket = bucket + (magnitude >= limit).astype(jnp.int32)
    return bucket + 16 * (relative > 0).astype(jnp.int32)


def rms_norm(values, gain):
    return values * lax.rsqrt(jnp.mean(values * values, axis=-1, keepdims=True) + EPSILON) * gain


def dot_nn(left, right):
    return lax.dot_general(left, right, (((1,), (0,)), ((), ())), preferred_element_type=F32)


def dot_nt(left, right):
    return lax.dot_general(left, right, (((1,), (1,)), ((), ())), preferred_element_type=F32)


def dot_tn(left, right):
    return lax.dot_general(left, right, (((0,), (0,)), ((), ())), preferred_element_type=F32)


def norm_back(values, gain, upstream):
    result, pullback = jax.vjp(rms_norm, values, gain)
    return pullback(upstream)


def gelu_back(values, upstream):
    result, pullback = jax.vjp(jax.nn.gelu, values)
    return pullback(upstream)[0]


def update(weight, moment, average, gradient):
    new_moment = MOMENTUM * moment + gradient
    new_weight = weight - RATE * (gradient + MOMENTUM * new_moment)
    new_average = AVERAGING * average + (1.0 - AVERAGING) * new_weight
    return (new_moment, new_average, new_weight, new_weight.astype(BF))


def window(block, blocks):
    return max(0, block - 1) * QB, min(blocks, block + 2) * QB


def diagonal_onehot(buckets):
    place = jnp.arange(DIAG, dtype=jnp.int32)
    turn = place % (2 * QB)
    relative = (place // (2 * QB) - 1) * QB - jnp.where(turn < QB, turn, turn - 2 * QB)
    return (bucket_ids(relative)[:, None] == jnp.arange(buckets, dtype=jnp.int32)[None, :]).astype(
        F32
    )


def bias_tiles(rows_ref, bias_ref):
    for head in range(2):
        for part in range(3):
            row = rows_ref[0, head : head + 1, part * 2 * QB : (part + 1) * 2 * QB]
            tile = pltpu.roll(jnp.broadcast_to(row, (QB, 2 * QB)), 0, 1, stride=1, stride_axis=0)
            bias_ref[head, part * QB : (part + 1) * QB, :] = tile[:, :QB]


def softmax_down(scores):
    expo = jnp.exp(scores - jnp.max(scores, axis=0, keepdims=True))
    return expo * (1.0 / jnp.sum(expo, axis=0, keepdims=True))


def attention_kernel(qkv_ref, rows_ref, column_ref, line_ref, out_ref, bias_ref):
    q_ref, k_ref, v_ref = (qkv_ref.at[:, i * 128 : (i + 1) * 128] for i in range(3))
    blocks = qkv_ref.shape[0] // QB
    half = lax.broadcasted_iota(jnp.int32, (QB, QB), 1) < 64
    bias_tiles(rows_ref, bias_ref)
    value_t = v_ref[...].T
    for block in range(blocks):
        low, high = window(block, blocks)
        off = low - (block - 1) * QB
        mine = slice(block * QB, (block + 1) * QB)
        query = q_ref[mine, :] * SCALING
        same = column_ref[low:high, :] == line_ref[:, mine]
        outs = []
        for head in range(2):
            part = jnp.where(half if head == 0 else ~half, query, jnp.zeros((), BF))
            scores = dot_nt(k_ref[low:high, :], part)
            scores = scores + bias_ref[head, off : off + high - low, :]
            probs = softmax_down(jnp.where(same, scores, NEGATIVE)).astype(BF)
            outs.append(dot_nn(value_t[head * 64 : (head + 1) * 64, low:high], probs))
        out_ref[mine, :] = jnp.concatenate(outs, axis=0).T.astype(BF)


def attention_back_kernel(
    qkv_ref,
    up_ref,
    rows_ref,
    column_ref,
    line_ref,
    grad_ref,
    diag_ref,
    gk_sum,
    gv_sum,
    grid_sum,
    bias_ref,
):
    q_ref, k_ref, v_ref = (qkv_ref.at[:, i * 128 : (i + 1) * 128] for i in range(3))
    blocks = qkv_ref.shape[0] // QB
    lanes = lax.broadcasted_iota(jnp.int32, (QB, QB), 1)
    half = lanes < 64
    bias_tiles(rows_ref, bias_ref)
    gk_sum[...] = jnp.zeros_like(gk_sum)
    gv_sum[...] = jnp.zeros_like(gv_sum)
    grid_sum[...] = jnp.zeros_like(grid_sum)
    key_t = k_ref[...].T
    for block in range(blocks):
        low, high = window(block, blocks)
        off = low - (block - 1) * QB
        span = high - low
        mine = slice(block * QB, (block + 1) * QB)
        query = q_ref[mine, :] * SCALING
        up = up_ref[mine, :]
        same = column_ref[low:high, :] == line_ref[:, mine]
        outs = []
        gks = 0.0
        gvs = 0.0
        for head in range(2):
            keep = half if head == 0 else ~half
            query_part = jnp.where(keep, query, jnp.zeros((), BF))
            up_part = jnp.where(keep, up, jnp.zeros((), BF))
            scores = dot_nt(k_ref[low:high, :], query_part)
            scores = scores + bias_ref[head, off : off + span, :]
            probs = softmax_down(jnp.where(same, scores, NEGATIVE))
            grad = dot_nt(v_ref[low:high, :], up_part)
            grad = probs * (grad - jnp.sum(probs * grad, axis=0, keepdims=True))
            low_grad = grad.astype(BF)
            outs.append(dot_nn(key_t[head * 64 : (head + 1) * 64, low:high], low_grad))
            gvs = gvs + dot_nn(probs.astype(BF), up_part)
            gks = gks + dot_nn(low_grad, query_part)
            grid_sum[head, off : off + span, :] += low_grad.astype(F32)
        gk_sum[low:high, :] += gks
        gv_sum[low:high, :] += gvs
        grad_ref[mine, :128] = (jnp.concatenate(outs, axis=0).T * SCALING).astype(BF)
    grad_ref[:, 128:256] = gk_sum[...].astype(BF)
    grad_ref[:, 256:] = gv_sum[...].astype(BF)
    flip = (lax.broadcasted_iota(jnp.int32, (QB, QB), 0) + lanes == QB - 1).astype(F32)
    for head in range(2):
        for part in range(3):
            turned = lax.dot_general(
                flip,
                grid_sum[head, part * QB : (part + 1) * QB, :],
                (((1,), (0,)), ((), ())),
                precision=lax.Precision.HIGHEST,
                preferred_element_type=F32,
            )
            wide = jnp.concatenate([turned, jnp.zeros((QB, QB), F32)], axis=1)
            rolled = pltpu.roll(wide, QB + 1, 1, stride=1, stride_axis=0)
            line = slice(part * 2 * QB, (part + 1) * 2 * QB)
            diag_ref[0, head : head + 1, line] = jnp.sum(rolled, axis=0, keepdims=True)


def attention_specs(length, first=0):
    slab = pl.BlockSpec((length, 384), lambda h: (0, h + first))
    up = pl.BlockSpec((length, 128), lambda h: (0, h + first))
    rows = pl.BlockSpec((1, 2, DIAG), lambda h: (h + first, 0, 0))
    column = pl.BlockSpec((length, 1), lambda h: (0, 0))
    line = pl.BlockSpec((1, length), lambda h: (0, 0))
    return slab, up, [rows, column, line]


def attention_forward(qkv, rows, segment):
    length = qkv.shape[0]
    pairs = qkv.shape[1] // 384
    slab, up, others = attention_specs(length)
    return pl.pallas_call(
        attention_kernel,
        grid=(pairs,),
        in_specs=[slab, *others],
        out_specs=up,
        out_shape=jax.ShapeDtypeStruct((length, pairs * 128), BF),
        scratch_shapes=[pltpu.VMEM((2, 3 * QB, QB), F32)],
        compiler_params=pltpu.CompilerParams(vmem_limit_bytes=VMEM),
        cost_estimate=cost(10 * 10**9, 4 * qkv.size),
    )(qkv, rows.reshape(pairs, 2, DIAG), segment[:, None], segment[None, :])


def attention_backward(qkv, up, rows, segment, first, count):
    length = qkv.shape[0]
    pairs = qkv.shape[1] // 384
    slab, up_spec, others = attention_specs(length, first)
    grads, diag = pl.pallas_call(
        attention_back_kernel,
        grid=(count,),
        in_specs=[slab, up_spec, *others],
        out_specs=[
            pl.BlockSpec((length, 384), lambda h: (0, h)),
            pl.BlockSpec((1, 2, DIAG), lambda h: (h, 0, 0)),
        ],
        out_shape=[
            jax.ShapeDtypeStruct((length, count * 384), BF),
            jax.ShapeDtypeStruct((count, 2, DIAG), F32),
        ],
        scratch_shapes=[
            pltpu.VMEM((length, 128), F32),
            pltpu.VMEM((length, 128), F32),
            pltpu.VMEM((2, 3 * QB, QB), F32),
            pltpu.VMEM((2, 3 * QB, QB), F32),
        ],
        compiler_params=pltpu.CompilerParams(vmem_limit_bytes=VMEM),
        cost_estimate=cost(count * 3 * 10**9, 6 * qkv.size),
    )(qkv, up, rows.reshape(pairs, 2, DIAG), segment[:, None], segment[None, :])
    return grads, diag.reshape(2 * count, DIAG)


def spread_heads(rows, lane_head, heads):
    parts = [jnp.where(lane_head == head, rows, 0.0) for head in range(heads)]
    return jnp.concatenate(parts, axis=0).astype(BF)


def own_turn(rows, core):
    return jnp.where(core == 0, rows, pltpu.roll(rows, rows.shape[1] // 2, 1))


def cross_setup(core_ref, query_ref, key_ref, line_ref, heads):
    core = core_ref[0]
    pairs, width = query_ref.shape
    lane_head = lax.broadcasted_iota(jnp.int32, (pairs, width), 1) // (width // heads)
    query_heads = spread_heads(own_turn(query_ref[...], core), lane_head, heads)
    scores = dot_nt(query_heads, key_ref[...]) * SCALING
    row = lax.broadcasted_iota(jnp.int32, scores.shape, 0)
    inside = lax.rem(row, pairs) == line_ref[...]
    return core, lane_head, query_heads, scores, inside


def gather_heads(rows, lane_head, heads, core):
    pairs = lane_head.shape[0]
    total = jnp.zeros(lane_head.shape, F32)
    for head in range(heads):
        total = jnp.where(lane_head == head, rows[head * pairs : (head + 1) * pairs], total)
    return own_turn(total, core)


def cross_kernel(core_ref, query_ref, key_ref, value_ref, line_ref, out_ref, *, heads):
    pairs, width = query_ref.shape
    core, lane_head, _, scores, inside = cross_setup(core_ref, query_ref, key_ref, line_ref, heads)
    scores = jnp.where(inside, scores, NEGATIVE)
    peak = jnp.max(scores, axis=1, keepdims=True)
    expo = jnp.exp(scores - peak)
    total = jnp.sum(expo, axis=1, keepdims=True)
    high = expo.astype(BF)
    low = (expo - high.astype(F32)).astype(BF)
    weighted = dot_nn(high, value_ref[...]) + dot_nn(low, value_ref[...])
    out_ref[:, :width] = gather_heads(weighted, lane_head, heads, core)
    lane = lax.broadcasted_iota(jnp.int32, (pairs, 128), 1)
    peaks = jnp.zeros((pairs, 128), F32)
    totals = jnp.ones((pairs, 128), F32)
    for head in range(heads):
        there = lane == lax.rem(head + core * (heads // 2), heads)
        part = slice(head * pairs, (head + 1) * pairs)
        peaks = jnp.where(there, peak[part], peaks)
        totals = jnp.where(there, total[part], totals)
    out_ref[:, width : width + 128] = peaks
    out_ref[:, width + 128 :] = totals


def cross_back_kernel(
    core_ref, query_ref, up_ref, stat_ref, key_ref, value_ref, line_ref, gk_ref, gv_ref, gq_ref, *, heads
):
    pairs, width = query_ref.shape
    core, lane_head, query_heads, scores, inside = cross_setup(
        core_ref, query_ref, key_ref, line_ref, heads
    )
    up_heads = spread_heads(own_turn(up_ref[...], core), lane_head, heads)
    lane = lax.broadcasted_iota(jnp.int32, (pairs, 128), 1)
    logs = []
    inners = []
    for head in range(heads):
        there = lane == lax.rem(head + core * (heads // 2), heads)
        logs.append(jnp.sum(jnp.where(there, stat_ref[:, :128], 0.0), axis=1, keepdims=True))
        inners.append(jnp.sum(jnp.where(there, stat_ref[:, 128:], 0.0), axis=1, keepdims=True))
    log = jnp.concatenate(logs, axis=0)
    inner = jnp.concatenate(inners, axis=0)
    probs = jnp.exp(jnp.where(inside, scores - log, NEGATIVE))
    grad = dot_nt(up_heads, value_ref[...])
    grad = (probs * (grad - inner)).astype(BF)
    gv_ref[...] = dot_tn(probs.astype(BF), up_heads).astype(BF)
    gk_ref[...] = (dot_tn(grad, query_heads) * SCALING).astype(BF)
    gq_ref[...] = gather_heads(dot_nn(grad, key_ref[...]), lane_head, heads, core)


def cross_forward(core, query, keys, values, segment, heads):
    pairs, width = query.shape
    vmem = pl.BlockSpec(memory_space=pltpu.VMEM)
    return pl.pallas_call(
        lambda *refs: cross_kernel(*refs, heads=heads),
        in_specs=[pl.BlockSpec(memory_space=pltpu.SMEM)] + [vmem] * 4,
        out_specs=vmem,
        out_shape=jax.ShapeDtypeStruct((pairs, width + 256), F32),
        compiler_params=pltpu.CompilerParams(vmem_limit_bytes=VMEM),
        cost_estimate=cost(600 * keys.size, 4 * keys.size),
    )(core.reshape(1), query, keys, values, segment[None, :])


def cross_backward(core, query, up, stat, keys, values, segment, heads):
    pairs, width = query.shape
    vmem = pl.BlockSpec(memory_space=pltpu.VMEM)
    grad = jax.ShapeDtypeStruct(keys.shape, BF)
    return pl.pallas_call(
        lambda *refs: cross_back_kernel(*refs, heads=heads),
        in_specs=[pl.BlockSpec(memory_space=pltpu.SMEM)] + [vmem] * 6,
        out_specs=[vmem] * 3,
        out_shape=[grad, grad, jax.ShapeDtypeStruct((pairs, width), F32)],
        compiler_params=pltpu.CompilerParams(vmem_limit_bytes=VMEM),
        cost_estimate=cost(1000 * keys.size, 8 * keys.size),
    )(core.reshape(1), query, up, stat, keys, values, segment[None, :])


def combine_kernel(id_ref, part_ref, wide_ref, log_ref, *, heads):
    count, width = wide_ref.shape
    ids = id_ref[...]
    peak = part_ref[:, width : width + 128]
    total = part_ref[:, width + 128 :]
    factor = jnp.zeros(peak.shape, F32)
    for query in range(count):
        there = ids == query
        top = jnp.max(jnp.where(there, peak, NEGATIVE), axis=0, keepdims=True)
        expo = jnp.where(there, jnp.exp(jnp.minimum(peak - top, 0.0)), 0.0)
        mass = jnp.sum(expo * total, axis=0, keepdims=True)
        factor = factor + expo / mass
        log_ref[query : query + 1, :] = top + jnp.log(mass)
    lane_head = lax.broadcasted_iota(jnp.int32, (peak.shape[0], width), 1) // (width // heads)
    scale = jnp.zeros((peak.shape[0], width), F32)
    for head in range(heads):
        scale = jnp.where(lane_head == head, factor[:, head : head + 1], scale)
    scaled = part_ref[:, :width] * scale
    for query in range(count):
        rows = jnp.where(ids == query, scaled, 0.0)
        wide_ref[query : query + 1, :] = jnp.sum(rows, axis=0, keepdims=True)


def combine(ids, parts, count, width, heads):
    vmem = pl.BlockSpec(memory_space=pltpu.VMEM)
    return pl.pallas_call(
        lambda *refs: combine_kernel(*refs, heads=heads),
        in_specs=[vmem] * 2,
        out_specs=[vmem] * 2,
        out_shape=[
            jax.ShapeDtypeStruct((count, width), F32),
            jax.ShapeDtypeStruct((count, 128), F32),
        ],
        compiler_params=pltpu.CompilerParams(vmem_limit_bytes=VMEM),
        cost_estimate=cost(10 * parts.size, 4 * parts.size),
    )(ids, parts)


class Net:
    def __init__(self):
        self.n_dp = lax.axis_size("dp")
        self.n_tok = lax.axis_size("tok")
        self.n_z = self.n_tok // 2
        self.tree = self.n_dp == 4 and self.n_z == 4
        self.dp, self.tok = lax.axis_index("dp"), lax.axis_index("tok")
        self.core, self.z = self.tok % 2, self.tok // 2
        self.x, self.y = self.dp % 2, self.dp // 2

    def tok_to(self, array, where):
        return lax.ppermute(array, "tok", [(t, where(t)) for t in range(self.n_tok)])

    def swap_core(self, array):
        return self.tok_to(array, lambda t: t ^ 1)

    def shift_z(self, array, by):
        return self.tok_to(array, lambda t: (t + 2 * by) % self.n_tok)

    def flip_dp(self, array, bit):
        return lax.ppermute(array, "dp", [(d, d ^ bit) for d in range(self.n_dp)])

    def swap_x(self, array):
        return self.flip_dp(array, 1)

    def swap_y(self, array):
        return self.flip_dp(array, 2)

    def own_first(self, array, axis=-1):
        low, high = jnp.split(array, 2, axis=axis)
        flipped = jnp.concatenate([high, low], axis=axis)
        return jnp.where(self.core == 0, array, flipped)


def after(array, *others):
    if not others:
        return array
    return lax.optimization_barrier((array, *others))[0]


def copies_of(plan, meta_ref, sources, outs, sems):
    copies = []
    for source, row, spot, column, wide, target, flag in plan:
        top = pl.multiple_of(meta_ref[spot], 48)
        left = pl.multiple_of(meta_ref[flag[0]] * 128 + flag[1], 128)
        copies.append(
            pltpu.make_async_copy(
                sources[source].at[pl.ds(row, 48), pl.ds(column, wide)],
                outs[target].at[pl.ds(top, 48), pl.ds(left, wide)],
                sems.at[len(copies)],
            )
        )
    return copies


def layout(net, pieces, widths, halves, own_columns, own_rows):
    spots = {}
    values = []

    def scalar(key, value):
        if key not in spots:
            spots[key] = len(values)
            values.append(jnp.asarray(value, jnp.int32))
        return spots[key]

    plan = []
    rows = 192
    for source, (array, corners, first, mine) in enumerate(pieces):
        for part, (dy, dx) in enumerate(corners):
            for block in range(4):
                for target, (half, start) in enumerate(zip(widths, halves)):
                    low = max(start, first)
                    high = min(start + half, first + array.shape[1])
                    if low >= high:
                        continue
                    flip = own_rows[target]
                    top = (net.y ^ dy ^ net.core) if flip else (net.y ^ dy)
                    spot = scalar(
                        (dy, dx, block, flip),
                        (top * 2 + (net.x ^ dx)) * rows + (net.z + 1 + block) % 4 * 48,
                    )
                    if own_columns[target]:
                        base = scalar("zero", 0)
                        shift = 0 if mine else half
                    else:
                        side = net.core if mine else 1 - net.core
                        base = scalar((mine, half), side * (half // 128))
                        shift = 0
                    plan.append(
                        (
                            source,
                            part * rows + block * 48,
                            spot,
                            low - first,
                            high - low,
                            target,
                            (base, shift + low - start),
                        )
                    )
    return plan, jnp.stack(values)


def place_kernel(meta_ref, *refs, plan, sources):
    copies = copies_of(plan, meta_ref, refs[:sources], refs[sources:-1], refs[-1])
    for copy in copies:
        copy.start()
    for copy in copies:
        copy.wait()


def place(plan, values, arrays, widths):
    count = len(arrays)
    return pl.pallas_call(
        lambda *refs: place_kernel(*refs, plan=plan, sources=count),
        in_specs=[pl.BlockSpec(memory_space=pltpu.SMEM)]
        + [pl.BlockSpec(memory_space=pl.ANY)] * count,
        out_specs=[pl.BlockSpec(memory_space=pltpu.VMEM)] * len(widths),
        out_shape=[jax.ShapeDtypeStruct((768, 2 * half), BF) for half in widths],
        scratch_shapes=[pltpu.SemaphoreType.DMA((len(plan),))],
        compiler_params=pltpu.CompilerParams(vmem_limit_bytes=VMEM),
        cost_estimate=cost(1, 768 * sum(widths) * 8),
    )(values, *arrays)


def expand_kernel(meta_ref, in_ref, up_ref, *refs, plan, sources):
    act_ref, grad_ref, out_ref, back_ref, first_ref, second_ref, sems = refs[sources:]
    weights = (first_ref, second_ref)
    copies = copies_of(plan, meta_ref, refs[:sources], weights, sems)
    for copy in copies:
        copy.start()
    for copy, step in zip(copies, plan):
        if step[5] == 0:
            copy.wait()
    width = first_ref.shape[1]
    tile = width // 4
    inner = [dot_nn(in_ref[...], first_ref[:, t * tile : (t + 1) * tile]) for t in range(4)]
    for copy, step in zip(copies, plan):
        if step[5] == 1:
            copy.wait()
    out = jnp.zeros(out_ref.shape, F32)
    back = jnp.zeros(back_ref.shape, F32)
    for t in range(4):
        part = slice(t * tile, (t + 1) * tile)
        up = dot_nn(up_ref[...], second_ref[:, part])
        act = jax.nn.gelu(inner[t]).astype(BF)
        grad = gelu_back(inner[t], up).astype(BF)
        act_ref[:, part] = act
        grad_ref[:, part] = grad
        back = back + dot_nt(grad, first_ref[:, part])
        out = out + dot_nt(act, second_ref[:, part])
    out_ref[...] = out
    back_ref[...] = back


def expand(plan, values, arrays, inputs, up, width):
    count = len(arrays)
    rows, model = inputs.shape
    vmem = pl.BlockSpec(memory_space=pltpu.VMEM)
    wide = jax.ShapeDtypeStruct((rows, width), BF)
    small = jax.ShapeDtypeStruct((rows, model), F32)
    return pl.pallas_call(
        lambda *refs: expand_kernel(*refs, plan=plan, sources=count),
        in_specs=[pl.BlockSpec(memory_space=pltpu.SMEM), vmem, vmem]
        + [pl.BlockSpec(memory_space=pl.ANY)] * count,
        out_specs=[vmem] * 4,
        out_shape=[wide, wide, small, small],
        scratch_shapes=[
            pltpu.VMEM((model, width), BF),
            pltpu.VMEM((model, width), BF),
            pltpu.SemaphoreType.DMA((len(plan),)),
        ],
        compiler_params=pltpu.CompilerParams(vmem_limit_bytes=VMEM),
        cost_estimate=cost(8 * rows * model * width, 4 * model * width),
    )(values, inputs, up, *arrays)


class Gather:
    def __init__(self, net, shards, own_columns, own_rows, cut):
        self.net, self.own_columns, self.own_rows, self.cut = net, own_columns, own_rows, cut
        self.shards = [shard.astype(BF) for shard in shards]
        self.widths = [shard.shape[1] // 2 for shard in shards]

    def halves(self, extra=None):
        core = self.net.core
        low = [shard[:, :half] for shard, half in zip(self.shards, self.widths)]
        high = [shard[:, half:] for shard, half in zip(self.shards, self.widths)]
        low, high = jnp.concatenate(low, axis=1), jnp.concatenate(high, axis=1)
        keep, sent = jnp.where(core == 0, low, high), jnp.where(core == 0, high, low)
        if extra is not None:
            keep = jnp.concatenate([keep, extra], axis=1)
            sent = jnp.concatenate([sent, extra], axis=1)
        return keep, sent

    def take(self, keep, got):
        first = jnp.where(self.net.core == 0, keep, got)
        second = jnp.where(self.net.core == 0, got, keep)
        self.chip = jnp.concatenate([first, second], axis=0)

    def over_z(self, *ready):
        if not self.net.tree:
            return ()
        chip = after(self.chip, *ready)
        self.line = [self.net.shift_z(chip, by) for by in (3, 2, 1)] + [chip]
        return (chip,)

    def join(self, *ready):
        if not self.net.tree:
            return ()
        line = [after(part, *ready) for part in self.line]
        self.one = jnp.concatenate([part[:, : self.cut] for part in line], axis=0)
        self.two = jnp.concatenate([part[:, self.cut :] for part in line], axis=0)
        return (self.one, self.two)

    def first(self, ready=(), join=()):
        if not self.net.tree:
            return ()
        one, two = after(self.one, *ready), after(self.two, *ready)
        self.one = jnp.concatenate([one, after(self.net.swap_x(one), *join)], axis=0)
        self.two = jnp.concatenate([two, after(self.net.swap_y(two), *join)], axis=0)
        return (self.one, self.two)

    def second(self, ready=(), join=()):
        if not self.net.tree:
            return ()
        one, two = after(self.one, *ready), after(self.two, *ready)
        self.near = (self.net.swap_core(self.one), self.net.swap_core(self.two))
        self.one_far = after(self.net.swap_y(one), *join)
        self.two_far = after(self.net.swap_x(two), *join)
        return (self.one_far, self.two_far)

    def extras(self, count, *ready):
        net = self.net
        parts = []
        for array in (self.two, self.two_far):
            block = after(array, *ready)[:, -128:].reshape(2, 4, 2 * count, -1)
            order = (net.z + 1 + jnp.arange(4, dtype=jnp.int32)) % 4
            same = order[None, :] == jnp.arange(4, dtype=jnp.int32)[:, None]
            zero = jnp.zeros((), BF)
            turned = jnp.where(same[None, :, :, None, None], block[:, None], zero)
            turned = jnp.sum(turned, axis=2).astype(BF)
            parts.append(turned.reshape(2, 8 * count, -1))
        near, far = parts
        return jnp.concatenate([near[0], far[0], near[1], far[1]], axis=0)

    def finish(self):
        net = self.net
        if not net.tree:
            outs = []
            for shard, columns, rows in zip(self.shards, self.own_columns, self.own_rows):
                whole = lax.all_gather(shard, ("dp", "tok"), axis=0, tiled=True)
                whole = net.own_first(whole, 1) if columns else whole
                outs.append(net.own_first(whole, 0) if rows else whole)
            return outs
        plan, values, arrays = self.parts()
        return place(plan, values, arrays, self.widths)

    def parts(self):
        net = self.net
        pieces = []
        far = (net.swap_core(self.one_far), net.swap_core(self.two_far))
        for array, other, corners, first in (
            (self.one, self.near[0], ((0, 0), (0, 1)), 0),
            (self.two, self.near[1], ((0, 0), (1, 0)), self.cut),
            (self.one_far, far[0], ((1, 0), (1, 1)), 0),
            (self.two_far, far[1], ((0, 1), (1, 1)), self.cut),
        ):
            pieces.append((array, corners, first, True))
            pieces.append((other, corners, first, False))
        starts = [sum(self.widths[:i]) for i in range(len(self.widths))]
        plan, values = layout(net, pieces, self.widths, starts, self.own_columns, self.own_rows)
        return plan, values, [piece[0] for piece in pieces]


def between_cores(net, gathers, extra=None):
    if not net.tree:
        return
    keeps, sents = zip(*[one.halves(extra) for one in gathers])
    got = net.swap_core(jnp.concatenate(sents, axis=1))
    start = 0
    for one, keep in zip(gathers, keeps):
        one.take(keep, got[:, start : start + keep.shape[1]])
        start += keep.shape[1]


def pick(array, index, axis):
    return lax.dynamic_index_in_dim(array, index, axis, keepdims=False)


def add(*parts):
    total = parts[0].astype(F32)
    for part in parts[1:]:
        total = total + part.astype(F32)
    return total


class Sum:
    def __init__(self, net, theirs, cut):
        self.net, self.cut, self.theirs = net, cut, theirs
        self.halves = [grad.shape[1] for grad in theirs]
        self.rows, self.wide = theirs[0].shape[0], sum(self.halves)
        self.got = net.swap_core(jnp.concatenate(theirs, axis=1)) if net.tree else theirs[0]

    def start(self, mine, join=()):
        self.mine = mine
        if not self.net.tree:
            return
        cut, shape = self.cut, (2, 2, self.rows // 4, self.wide)
        own = jnp.concatenate(mine, axis=1).reshape(shape)
        got = after(self.got, *join).reshape(shape)
        one = (own[..., :cut], got[..., :cut])
        two = (own[..., cut:], got[..., cut:])
        self.one = [self.halve(one, 0, self.net.y, keep) for keep in (True, False)]
        self.two = [self.halve(two, 1, self.net.x, keep) for keep in (True, False)]

    def halve(self, parts, axis, index, keep):
        index = index if keep else 1 - index
        return add(*[pick(part, index, axis) for part in parts]).astype(BF)

    def state(self):
        return (*self.one, *self.two) if self.net.tree else ()

    def first(self, ready=(), join=()):
        if not self.net.tree:
            return
        net = self.net
        one = (self.one[0], after(net.swap_y(after(self.one[1], *ready)), *join))
        two = (self.two[0], after(net.swap_x(after(self.two[1], *ready)), *join))
        self.one = [self.halve(one, 0, net.x, keep) for keep in (True, False)]
        self.two = [self.halve(two, 0, net.y, keep) for keep in (True, False)]

    def second(self, ready=(), join=()):
        if not self.net.tree:
            return
        net = self.net
        one = (self.one[0], after(net.swap_x(after(self.one[1], *ready)), *join))
        two = (self.two[0], after(net.swap_y(after(self.two[1], *ready)), *join))
        shape = (4, self.rows // 16, -1)
        one, two = [part.reshape(shape) for part in one], [part.reshape(shape) for part in two]

        def chunk(at):
            sums = [add(*[pick(part, at, 0) for part in parts]) for parts in (one, two)]
            return jnp.concatenate(sums, axis=1)

        self.own = chunk(net.z)
        self.sent = [chunk((net.z + by) % 4).astype(BF) for by in (1, 2, 3)]

    def pending(self):
        return tuple(self.sent) if self.net.tree else ()


def finish(net, sums, join=()):
    if not net.tree:
        outs = []
        for one in sums:
            for mine, theirs in zip(one.mine, one.theirs):
                whole = net.own_first(jnp.concatenate([mine, theirs], axis=1), 1)
                total = lax.psum_scatter(whole, ("dp", "tok"), scatter_dimension=0, tiled=True)
                outs.append(total.astype(F32))
        return outs
    rows = sums[0].rows
    got = []
    for i, by in enumerate((1, 2, 3)):
        sent = jnp.concatenate([one.sent[i] for one in sums], axis=1)
        got.append(after(net.shift_z(sent, by), *join))
    total = add(jnp.concatenate([one.own for one in sums], axis=1), *got)
    total = total.reshape(2, rows // 32, -1)
    keep = pick(total, net.core, 0)
    other = net.swap_core(pick(total, 1 - net.core, 0))
    low = jnp.where(net.core == 0, keep, other)
    high = jnp.where(net.core == 0, other, keep)
    outs = []
    start = 0
    for half in [half for one in sums for half in one.halves]:
        part = slice(start, start + half)
        outs.append(jnp.concatenate([low[:, part], high[:, part]], axis=1))
        start += half
    return outs


def gather_tok(net, array, join=(), over_core=()):
    if not net.tree:
        return lax.all_gather(array, "tok", axis=0), jnp.arange(net.n_tok, dtype=jnp.int32)
    steps = (0, 1, 2, 3)
    array = jnp.stack([array] + [after(net.shift_z(array, by), *join) for by in steps[1:]])
    array = jnp.concatenate([array, after(net.swap_core(array), *over_core)], axis=0)
    source = [(net.z - by) % 4 * 2 + net.core for by in steps]
    source += [(net.z - by) % 4 * 2 + 1 - net.core for by in steps]
    return array, jnp.stack(source).astype(jnp.int32)


def gather_dp(net, array, over_x=(), over_y=()):
    if not net.tree:
        whole = lax.all_gather(array, "dp", axis=0)
        order = net.dp ^ jnp.arange(net.n_dp, dtype=jnp.int32)
        same = order[:, None] == jnp.arange(net.n_dp, dtype=jnp.int32)[None, :]
        zero = jnp.zeros((), array.dtype)
        turned = jnp.sum(jnp.where(same[:, :, None, None], whole[None], zero), axis=1)
        return turned.reshape(-1, array.shape[1]).astype(array.dtype)
    array = jnp.concatenate([array, after(net.swap_x(array), *over_x)], axis=0)
    return jnp.concatenate([array, after(net.swap_y(array), *over_y)], axis=0)


def sum_small(net, array, joins):
    joins = list(joins)
    bit = 1
    while bit < net.n_tok:
        other = net.tok_to(array, lambda t, bit=bit: t ^ bit)
        array = array + after(other, *(joins.pop(0) if joins else ()))
        bit *= 2
    bit = 1
    while bit < net.n_dp:
        array = array + after(net.flip_dp(array, bit), *(joins.pop(0) if joins else ()))
        bit *= 2
    return array


def per_device(
    encoder_input,
    decoder_input,
    output_cotangent,
    pair_lengths,
    pair_offset,
    pair_query,
    attention_master,
    attention_moment,
    attention_average,
    feedforward_master,
    feedforward_moment,
    feedforward_average,
    decoder_master,
    decoder_moment,
    decoder_average,
    expansion_master,
    expansion_moment,
    expansion_average,
    gain_master,
    gain_moment,
    gain_average,
    bias_master,
    bias_moment,
    bias_average,
):
    net = Net()
    length = encoder_input.shape[1]
    width = encoder_input.shape[2]
    buckets, heads = bias_master.shape
    head_size = width // heads
    pairs = pair_lengths.shape[1]
    nquery = decoder_input.shape[0]

    half = width // 2
    wide = feedforward_master.shape[2] // 2
    att = [attention_master[i] for i in range(6)]
    feed = [feedforward_master[i] for i in range(2)]
    dec = [decoder_master[i] for i in range(4)]
    widen = [expansion_master[i] for i in range(2)]
    three = jnp.transpose(
        attention_master[:3].astype(BF).reshape(3, -1, width // 128, 128), (1, 2, 0, 3)
    ).reshape(-1, 3 * width)
    both = jnp.concatenate([decoder_input, output_cotangent], axis=1)
    get_att = Gather(
        net,
        [three, att[3]],
        [True, False],
        [False, True],
        7 * half // 3 - 128,
    )
    between_cores(net, [get_att], both.reshape(-1, 128))
    early = get_att.over_z()
    feed, dec, widen, others = (
        [after(shard, *early) for shard in shards] for shards in (feed, dec, widen, att[4:])
    )
    get_feed = Gather(net, feed, [True] * 2, [False] * 2, wide)
    get_dec = Gather(net, others + dec, [True] * 2 + [False] * 4, [False] * 6, 3 * half)
    get_exp = Gather(net, widen, [True] * 2, [False] * 2, wide)
    between_cores(net, [get_feed, get_dec, get_exp])
    step = get_att.join()
    get_feed.over_z(*step)
    get_att.first()
    step_att = get_att.second()
    step_feed = get_feed.join(*step_att)
    get_dec.over_z(*step_feed)
    w_qkv, w_out = get_att.finish()

    counter = jnp.arange(pairs, dtype=jnp.int32)
    hidden = after(encoder_input, *early)[0].astype(F32)
    lengths = after(pair_lengths, *early)[0]
    ends = jnp.sum(jnp.where(counter[:, None] <= counter[None, :], lengths[:, None], 0), axis=0)
    position = jnp.arange(length, dtype=jnp.int32)
    segment = jnp.sum((position[:, None] >= ends[None, :]).astype(jnp.int32), axis=1)
    onehot = diagonal_onehot(buckets)
    bias_rows = jnp.sum(after(bias_master, *early).T[:, None, :] * onehot[None], axis=2)
    bias_rows = net.own_first(bias_rows, 0)

    normed = rms_norm(hidden, gain_master[0]).astype(BF)
    qkv = dot_nn(normed, w_qkv).astype(BF)
    feed_half = get_feed.first(join=(qkv,))
    attended = attention_forward(after(qkv, *feed_half), bias_rows, segment)
    residual = hidden + dot_nn(attended, w_out)
    normed_two = rms_norm(residual, gain_master[1]).astype(BF)
    step_two = get_feed.second(join=(normed_two,))
    step_dec = get_dec.join(normed_two)
    get_exp.over_z(*step_dec, *step_two)
    w_up, w_down = get_feed.finish()
    dec_half = get_dec.first(step_two, (w_up, w_down))
    inner = dot_nn(after(normed_two, *dec_half), w_up)
    activated = jax.nn.gelu(inner).astype(BF)
    if net.tree:
        ordered = get_att.extras(nquery, activated)
    else:
        ordered = gather_dp(net, lax.all_gather(both, "tok", axis=0, tiled=True))
    encoded = (residual + dot_nt(activated, w_down)).astype(BF)
    step_three = get_dec.second(join=(encoded,))
    w_ck, w_cv, e_zero, e_one, e_two, e_three = get_dec.finish()
    cross_keys = dot_nn(encoded, w_ck).astype(BF)
    cross_values = dot_nn(encoded, w_cv).astype(BF)
    get_exp.join(*step_three)

    state = ordered[:, :width].astype(F32)
    up_low = ordered[:, width:]
    upstream = up_low.astype(F32)
    group = net.n_tok * nquery
    total_rows = state.shape[0]
    row_id = jnp.arange(total_rows, dtype=jnp.int32)
    own_row = (row_id // nquery == net.tok)[:, None]

    def own_rows(rows):
        return lax.dynamic_slice_in_dim(rows, net.tok * nquery, nquery, axis=0)

    self_in = rms_norm(state, gain_master[2]).astype(BF)
    self_values = dot_nn(self_in, e_zero).astype(BF)
    after_self = state + dot_nn(self_values, e_one)
    cross_in = rms_norm(after_self, gain_master[3]).astype(BF)
    cross_query = dot_nn(cross_in, e_two).astype(BF)

    offsets = pair_offset[0]
    owners = pair_query[0]
    query_id = jnp.arange(group, dtype=jnp.int32)
    own_id = (net.tok + offsets) % net.n_tok * nquery + owners
    own_match = own_id[:, None] == query_id[None, :]

    def at_pairs(rows):
        return jnp.sum(jnp.where(own_match[:, :, None], rows[None, :group].astype(F32), 0.0), axis=1)

    exp_half = get_exp.first(join=(cross_query,))
    pair_queries = at_pairs(after(cross_query, *exp_half))
    get_exp.second()
    partial = cross_forward(net.core, pair_queries, cross_keys, cross_values, segment, heads)
    got, source = gather_tok(net, after(partial, *get_exp.near) if net.tree else partial)
    pair_id = (source[:, None] + offsets[None, :]) % net.n_tok * nquery + owners[None, :]
    pair_match = pair_id.reshape(1, -1) == query_id[:, None]

    def sum_pairs(rows):
        return lax.dot_general(
            pair_match.astype(F32),
            rows,
            (((1,), (0,)), ((), ())),
            precision=lax.Precision.HIGHEST,
            preferred_element_type=F32,
        )

    got = got.reshape(-1, width + 256)
    cross_wide, row_log = combine(pair_id.reshape(-1, 1), got, group, width, heads)
    cross_out = gather_dp(net, cross_wide.astype(BF))

    after_cross = after_self + dot_nn(cross_out, e_three)
    final_in = rms_norm(after_cross, gain_master[4]).astype(BF)
    if net.tree:
        final_act, grad_inner, final_out, grad_final_in = expand(
            *get_exp.parts(), final_in, up_low, 2 * wide
        )
    else:
        x_up, x_down = get_exp.finish()
        grad_act = dot_nn(up_low, x_down)
        final_inner = dot_nn(final_in, x_up)
        grad_inner = gelu_back(final_inner, grad_act).astype(BF)
        grad_final_in = dot_nt(grad_inner, x_up)
        final_act = jax.nn.gelu(final_inner).astype(BF)
        final_out = dot_nt(final_act, x_down)

    def decoder_norm_back(values, gain, up):
        grad, _ = norm_back(values, gain, up)
        _, grad_gain = norm_back(values, gain, jnp.where(own_row, up, 0.0))
        return grad, grad_gain

    grad_state_four, grad_gain_four = decoder_norm_back(after_cross, gain_master[4], grad_final_in)
    grad_cross_total = upstream + grad_state_four
    cross_grad_low = grad_cross_total.astype(BF)
    grad_cross_out = dot_nt(cross_grad_low, e_three)[:group].astype(BF).astype(F32)
    row_inner = jnp.sum((grad_cross_out * cross_wide).reshape(group, heads, head_size), axis=2)
    empty = jnp.zeros((group, 128 - heads), F32)
    back = at_pairs(jnp.concatenate([grad_cross_out, row_log, row_inner, empty], axis=1))
    decoder_output = own_rows(after_cross + final_out)

    grad_keys_cross, grad_values_cross, grad_query_part = cross_backward(
        net.core,
        pair_queries,
        back[:, :width],
        back[:, width:],
        cross_keys,
        cross_values,
        segment,
        heads,
    )
    grad_encoded = (dot_nt(grad_keys_cross, w_ck) + dot_nt(grad_values_cross, w_cv)).astype(BF)

    grad_down = [
        dot_tn(grad_encoded, part).astype(BF) for part in (activated[:, :wide], activated[:, wide:])
    ]
    crosses = [
        dot_tn(encoded, grad_keys_cross).astype(BF),
        dot_tn(encoded, grad_values_cross).astype(BF),
    ]
    down = Sum(net, [grad_down[1]], 2 * half)
    grad_activated = dot_nn(after(grad_encoded, *grad_down), w_down)
    grad_inner_enc = gelu_back(inner, grad_activated).astype(BF)
    down.start(grad_down[:1], (grad_inner_enc,))
    grad_inner_enc = after(grad_inner_enc, *down.state())
    grad_up = [
        dot_tn(normed_two, part).astype(BF)
        for part in (grad_inner_enc[:, :wide], grad_inner_enc[:, wide:])
    ]
    grad_normed_two = dot_nt(after(grad_inner_enc, *grad_up), w_up)
    grad_resid, grad_gain_one = norm_back(residual, gain_master[1], grad_normed_two)
    grad_residual = grad_encoded.astype(F32) + grad_resid
    attn_low = grad_residual.astype(BF)
    down.first()
    got_query, _ = gather_tok(net, after(grad_query_part, grad_inner_enc))
    ready_low = after(attn_low, *down.state(), got_query)
    grad_out = dot_tn(net.own_first(attended), net.own_first(ready_low)).astype(BF)
    others = [grad_out, *crosses]
    middle = Sum(net, [grad_up[1], *[grad[:, half:] for grad in others]], 11 * half // 3)
    grad_attended = dot_nt(after(attn_low, grad_out), w_out).astype(BF)
    middle.start([grad_up[0], *[grad[:, :half] for grad in others]])
    grad_attended = after(grad_attended, *middle.state(), *down.state())
    blocks = width // 256

    def attention_part(up, first):
        return attention_backward(qkv, up, bias_rows, segment, first, blocks)

    their_grads, their_diagonals = attention_part(grad_attended, blocks)
    down.second(join=(their_grads,))
    middle.first(join=(their_grads,))
    their_left = after(normed, *down.pending(), *middle.state())
    their_qkv = dot_tn(their_left, their_grads).astype(BF)
    last = Sum(net, [their_qkv], 5 * half // 3)
    middle.second(join=(their_qkv,))
    grad_query_cross = (sum_pairs(got_query.reshape(-1, width)) * SCALING).astype(BF)
    grad_query_cross = gather_dp(net, grad_query_cross, (their_grads,), (their_qkv,))
    own_up = after(grad_attended, last.got, grad_query_cross, *middle.pending())
    own_grads, own_diagonals = attention_part(own_up, 0)
    own_qkv = dot_tn(normed, own_grads).astype(BF)
    last.start([own_qkv])
    diagonals = jnp.concatenate([own_diagonals, their_diagonals], axis=0)
    own_grads = after(own_grads, *last.state())
    grad_normed = dot_nt(jnp.concatenate([own_grads, their_grads], axis=1), w_qkv)
    grad_input_part, grad_gain_zero = norm_back(hidden, gain_master[0], grad_normed)
    encoder_gradient = (grad_residual + grad_input_part)[None]

    grad_query_cross = after(grad_query_cross, own_grads)
    grad_cross_in = dot_nt(grad_query_cross, e_two)
    grad_state_three, grad_gain_three = decoder_norm_back(
        after_self, gain_master[3], grad_cross_in
    )
    grad_self_total = grad_cross_total + grad_state_three
    self_grad_low = grad_self_total.astype(BF)
    grad_self_values = dot_nt(self_grad_low, e_one).astype(BF)
    grad_self_in = dot_nt(grad_self_values, e_zero)
    grad_state_two, grad_gain_two = decoder_norm_back(state, gain_master[2], grad_self_in)
    decoder_gradient = own_rows(grad_self_total + grad_state_two)
    own = decoder_master.shape[1]
    rank = net.dp * net.n_tok + net.tok

    def own_weight_rows(left, right):
        return dot_tn(lax.dynamic_slice_in_dim(left, rank * own, own, axis=1), right)

    grad_dec = jnp.stack(
        [
            own_weight_rows(self_in, grad_self_values),
            own_weight_rows(self_values, self_grad_low),
            own_weight_rows(cross_in, grad_query_cross),
            own_weight_rows(cross_out, cross_grad_low),
        ]
    )
    grad_exp = jnp.stack(
        [
            net.own_first(own_weight_rows(final_in, grad_inner)),
            net.own_first(own_weight_rows(up_low, final_act)),
        ]
    )

    sum_down, sum_up, sum_out, sum_ck, sum_cv = finish(net, [down, middle], (own_qkv,))
    last.first(join=(grad_gain_zero,))
    after_first = last.state()
    last.second()
    after_second = last.pending()
    (sum_three,) = finish(net, [last])
    grad_table = jnp.dot(
        net.own_first(diagonals, 0),
        onehot,
        precision=lax.Precision.HIGHEST,
        preferred_element_type=F32,
    ).T
    gain_grad = jnp.concatenate(
        [grad_gain_zero, grad_gain_one, grad_gain_two, grad_gain_three, grad_gain_four]
    )
    small = jnp.concatenate([gain_grad, grad_table.reshape(-1)])
    joins = [(encoder_gradient,), after_first, after_first, after_second]
    small = sum_small(net, small, joins)
    gain_sum = small[: 5 * width].reshape(5, width)
    bias_sum = small[5 * width :].reshape(buckets, heads)

    sum_three = jnp.transpose(sum_three.reshape(own, width // 128, 3, 128), (2, 0, 1, 3))
    sum_three = sum_three.reshape(3, own, width)
    results = [decoder_output, encoder_gradient, decoder_gradient]
    groups = (
        (
            attention_master,
            attention_moment,
            attention_average,
            jnp.concatenate([sum_three, jnp.stack([sum_out, sum_ck, sum_cv])], axis=0),
        ),
        (
            feedforward_master,
            feedforward_moment,
            feedforward_average,
            jnp.stack([sum_up, sum_down]),
        ),
        (decoder_master, decoder_moment, decoder_average, grad_dec),
        (expansion_master, expansion_moment, expansion_average, grad_exp),
        (gain_master, gain_moment, gain_average, gain_sum),
        (bias_master, bias_moment, bias_average, bias_sum),
    )
    for weight, moment, average, gradient in groups:
        results.extend(update(weight, moment, average, gradient))
    return tuple(results)


def solution(mesh):
    spread = P(("dp", "tok"), None)
    weights = P(None, ("dp", "tok"), None)
    in_specs = (
        P(("dp", "tok"), None, None),
        spread,
        spread,
        spread,
        P("dp", None),
        P("dp", None),
        *[weights] * 12,
        *[P()] * 6,
    )
    out_specs = (spread, P(("dp", "tok"), None, None), spread, *[weights] * 16, *[P()] * 8)
    return jax.shard_map(
        per_device, mesh=mesh, in_specs=in_specs, out_specs=out_specs, check_vma=False
    )
```

```python
import jax
import jax.numpy as jnp
from jax import lax
from jax.experimental import pallas as pl
from jax.experimental.pallas import tpu as pltpu
from jax.sharding import PartitionSpec as P

EPSILON = 1e-06
SCALING = 0.125
NEGATIVE = -1e30
MOMENTUM = 0.5
AVERAGING = 0.5
RATE = 0.02
THRESHOLDS = (12, 16, 23, 32, 46, 64, 91)
BF = jnp.bfloat16
F32 = jnp.float32
QB = 128
DIAG = 6 * QB
VMEM = 48 * 2**20


def cost(flops, count):
    return pl.CostEstimate(flops=flops, bytes_accessed=count, transcendentals=flops // 1024)


def bucket_ids(relative):
    magnitude = jnp.abs(relative)
    bucket = jnp.minimum(magnitude, 8)
    for limit in THRESHOLDS:
        bucket = bucket + (magnitude >= limit).astype(jnp.int32)
    return bucket + 16 * (relative > 0).astype(jnp.int32)


def rms_norm(values, gain):
    return values * lax.rsqrt(jnp.mean(values * values, axis=-1, keepdims=True) + EPSILON) * gain


def dot_nn(left, right):
    return lax.dot_general(left, right, (((1,), (0,)), ((), ())), preferred_element_type=F32)


def dot_nt(left, right):
    return lax.dot_general(left, right, (((1,), (1,)), ((), ())), preferred_element_type=F32)


def dot_tn(left, right):
    return lax.dot_general(left, right, (((0,), (0,)), ((), ())), preferred_element_type=F32)


def norm_back(values, gain, upstream):
    result, pullback = jax.vjp(rms_norm, values, gain)
    return pullback(upstream)


def gelu_back(values, upstream):
    result, pullback = jax.vjp(jax.nn.gelu, values)
    return pullback(upstream)[0]


def update(weight, moment, average, gradient):
    new_moment = MOMENTUM * moment + gradient
    new_weight = weight - RATE * (gradient + MOMENTUM * new_moment)
    new_average = AVERAGING * average + (1.0 - AVERAGING) * new_weight
    return (new_moment, new_average, new_weight, new_weight.astype(BF))


def window(block, blocks):
    return max(0, block - 1) * QB, min(blocks, block + 2) * QB


def diagonal_onehot(buckets):
    place = jnp.arange(DIAG, dtype=jnp.int32)
    turn = place % (2 * QB)
    relative = (place // (2 * QB) - 1) * QB - jnp.where(turn < QB, turn, turn - 2 * QB)
    return (bucket_ids(relative)[:, None] == jnp.arange(buckets, dtype=jnp.int32)[None, :]).astype(
        F32
    )


def bias_tiles(rows_ref, bias_ref):
    for head in range(2):
        for part in range(3):
            row = rows_ref[0, head : head + 1, part * 2 * QB : (part + 1) * 2 * QB]
            tile = pltpu.roll(jnp.broadcast_to(row, (QB, 2 * QB)), 0, 1, stride=1, stride_axis=0)
            bias_ref[head, part * QB : (part + 1) * QB, :] = tile[:, :QB]


def softmax_down(scores):
    expo = jnp.exp(scores - jnp.max(scores, axis=0, keepdims=True))
    return expo * (1.0 / jnp.sum(expo, axis=0, keepdims=True))


def attention_kernel(qkv_ref, rows_ref, column_ref, line_ref, out_ref, bias_ref):
    q_ref, k_ref, v_ref = (qkv_ref.at[:, i * 128 : (i + 1) * 128] for i in range(3))
    blocks = qkv_ref.shape[0] // QB
    half = lax.broadcasted_iota(jnp.int32, (QB, QB), 1) < 64
    bias_tiles(rows_ref, bias_ref)
    value_t = v_ref[...].T
    for block in range(blocks):
        low, high = window(block, blocks)
        off = low - (block - 1) * QB
        mine = slice(block * QB, (block + 1) * QB)
        query = q_ref[mine, :] * SCALING
        same = column_ref[low:high, :] == line_ref[:, mine]
        outs = []
        for head in range(2):
            part = jnp.where(half if head == 0 else ~half, query, jnp.zeros((), BF))
            scores = dot_nt(k_ref[low:high, :], part)
            scores = scores + bias_ref[head, off : off + high - low, :]
            probs = softmax_down(jnp.where(same, scores, NEGATIVE)).astype(BF)
            outs.append(dot_nn(value_t[head * 64 : (head + 1) * 64, low:high], probs))
        out_ref[mine, :] = jnp.concatenate(outs, axis=0).T.astype(BF)


def attention_back_kernel(
    qkv_ref,
    up_ref,
    rows_ref,
    column_ref,
    line_ref,
    grad_ref,
    diag_ref,
    gk_sum,
    gv_sum,
    grid_sum,
    bias_ref,
):
    q_ref, k_ref, v_ref = (qkv_ref.at[:, i * 128 : (i + 1) * 128] for i in range(3))
    blocks = qkv_ref.shape[0] // QB
    lanes = lax.broadcasted_iota(jnp.int32, (QB, QB), 1)
    half = lanes < 64
    bias_tiles(rows_ref, bias_ref)
    gk_sum[...] = jnp.zeros_like(gk_sum)
    gv_sum[...] = jnp.zeros_like(gv_sum)
    grid_sum[...] = jnp.zeros_like(grid_sum)
    key_t = k_ref[...].T
    for block in range(blocks):
        low, high = window(block, blocks)
        off = low - (block - 1) * QB
        span = high - low
        mine = slice(block * QB, (block + 1) * QB)
        query = q_ref[mine, :] * SCALING
        up = up_ref[mine, :]
        same = column_ref[low:high, :] == line_ref[:, mine]
        outs = []
        gks = 0.0
        gvs = 0.0
        for head in range(2):
            keep = half if head == 0 else ~half
            query_part = jnp.where(keep, query, jnp.zeros((), BF))
            up_part = jnp.where(keep, up, jnp.zeros((), BF))
            scores = dot_nt(k_ref[low:high, :], query_part)
            scores = scores + bias_ref[head, off : off + span, :]
            probs = softmax_down(jnp.where(same, scores, NEGATIVE))
            grad = dot_nt(v_ref[low:high, :], up_part)
            grad = probs * (grad - jnp.sum(probs * grad, axis=0, keepdims=True))
            low_grad = grad.astype(BF)
            outs.append(dot_nn(key_t[head * 64 : (head + 1) * 64, low:high], low_grad))
            gvs = gvs + dot_nn(probs.astype(BF), up_part)
            gks = gks + dot_nn(low_grad, query_part)
            grid_sum[head, off : off + span, :] += low_grad.astype(F32)
        gk_sum[low:high, :] += gks
        gv_sum[low:high, :] += gvs
        grad_ref[mine, :128] = (jnp.concatenate(outs, axis=0).T * SCALING).astype(BF)
    grad_ref[:, 128:256] = gk_sum[...].astype(BF)
    grad_ref[:, 256:] = gv_sum[...].astype(BF)
    flip = (lax.broadcasted_iota(jnp.int32, (QB, QB), 0) + lanes == QB - 1).astype(F32)
    for head in range(2):
        for part in range(3):
            turned = lax.dot_general(
                flip,
                grid_sum[head, part * QB : (part + 1) * QB, :],
                (((1,), (0,)), ((), ())),
                precision=lax.Precision.HIGHEST,
                preferred_element_type=F32,
            )
            wide = jnp.concatenate([turned, jnp.zeros((QB, QB), F32)], axis=1)
            rolled = pltpu.roll(wide, QB + 1, 1, stride=1, stride_axis=0)
            line = slice(part * 2 * QB, (part + 1) * 2 * QB)
            diag_ref[0, head : head + 1, line] = jnp.sum(rolled, axis=0, keepdims=True)


def attention_specs(length, first=0):
    slab = pl.BlockSpec((length, 384), lambda h: (0, h + first))
    up = pl.BlockSpec((length, 128), lambda h: (0, h + first))
    rows = pl.BlockSpec((1, 2, DIAG), lambda h: (h + first, 0, 0))
    column = pl.BlockSpec((length, 1), lambda h: (0, 0))
    line = pl.BlockSpec((1, length), lambda h: (0, 0))
    return slab, up, [rows, column, line]


def attention_forward(qkv, rows, segment):
    length = qkv.shape[0]
    pairs = qkv.shape[1] // 384
    slab, up, others = attention_specs(length)
    return pl.pallas_call(
        attention_kernel,
        grid=(pairs,),
        in_specs=[slab, *others],
        out_specs=up,
        out_shape=jax.ShapeDtypeStruct((length, pairs * 128), BF),
        scratch_shapes=[pltpu.VMEM((2, 3 * QB, QB), F32)],
        compiler_params=pltpu.CompilerParams(vmem_limit_bytes=VMEM),
        cost_estimate=cost(10 * 10**9, 4 * qkv.size),
    )(qkv, rows.reshape(pairs, 2, DIAG), segment[:, None], segment[None, :])


def attention_backward(qkv, up, rows, segment, first, count):
    length = qkv.shape[0]
    pairs = qkv.shape[1] // 384
    slab, up_spec, others = attention_specs(length, first)
    grads, diag = pl.pallas_call(
        attention_back_kernel,
        grid=(count,),
        in_specs=[slab, up_spec, *others],
        out_specs=[
            pl.BlockSpec((length, 384), lambda h: (0, h)),
            pl.BlockSpec((1, 2, DIAG), lambda h: (h, 0, 0)),
        ],
        out_shape=[
            jax.ShapeDtypeStruct((length, count * 384), BF),
            jax.ShapeDtypeStruct((count, 2, DIAG), F32),
        ],
        scratch_shapes=[
            pltpu.VMEM((length, 128), F32),
            pltpu.VMEM((length, 128), F32),
            pltpu.VMEM((2, 3 * QB, QB), F32),
            pltpu.VMEM((2, 3 * QB, QB), F32),
        ],
        compiler_params=pltpu.CompilerParams(vmem_limit_bytes=VMEM),
        cost_estimate=cost(count * 3 * 10**9, 6 * qkv.size),
    )(qkv, up, rows.reshape(pairs, 2, DIAG), segment[:, None], segment[None, :])
    return grads, diag.reshape(2 * count, DIAG)


def spread_heads(rows, lane_head, heads):
    parts = [jnp.where(lane_head == head, rows, 0.0) for head in range(heads)]
    return jnp.concatenate(parts, axis=0).astype(BF)


def own_turn(rows, core):
    return jnp.where(core == 0, rows, pltpu.roll(rows, rows.shape[1] // 2, 1))


def cross_setup(core_ref, query_ref, key_ref, line_ref, heads):
    core = core_ref[0]
    pairs, width = query_ref.shape
    lane_head = lax.broadcasted_iota(jnp.int32, (pairs, width), 1) // (width // heads)
    query_heads = spread_heads(own_turn(query_ref[...], core), lane_head, heads)
    scores = dot_nt(query_heads, key_ref[...]) * SCALING
    row = lax.broadcasted_iota(jnp.int32, scores.shape, 0)
    inside = lax.rem(row, pairs) == line_ref[...]
    return core, lane_head, query_heads, scores, inside


def gather_heads(rows, lane_head, heads, core):
    pairs = lane_head.shape[0]
    total = jnp.zeros(lane_head.shape, F32)
    for head in range(heads):
        total = jnp.where(lane_head == head, rows[head * pairs : (head + 1) * pairs], total)
    return own_turn(total, core)


def cross_kernel(core_ref, query_ref, key_ref, value_ref, line_ref, out_ref, *, heads):
    pairs, width = query_ref.shape
    core, lane_head, _, scores, inside = cross_setup(core_ref, query_ref, key_ref, line_ref, heads)
    scores = jnp.where(inside, scores, NEGATIVE)
    peak = jnp.max(scores, axis=1, keepdims=True)
    expo = jnp.exp(scores - peak)
    total = jnp.sum(expo, axis=1, keepdims=True)
    high = expo.astype(BF)
    low = (expo - high.astype(F32)).astype(BF)
    weighted = dot_nn(high, value_ref[...]) + dot_nn(low, value_ref[...])
    out_ref[:, :width] = gather_heads(weighted, lane_head, heads, core)
    lane = lax.broadcasted_iota(jnp.int32, (pairs, 128), 1)
    peaks = jnp.zeros((pairs, 128), F32)
    totals = jnp.ones((pairs, 128), F32)
    for head in range(heads):
        there = lane == lax.rem(head + core * (heads // 2), heads)
        part = slice(head * pairs, (head + 1) * pairs)
        peaks = jnp.where(there, peak[part], peaks)
        totals = jnp.where(there, total[part], totals)
    out_ref[:, width : width + 128] = peaks
    out_ref[:, width + 128 :] = totals


def cross_back_kernel(
    core_ref, query_ref, up_ref, stat_ref, key_ref, value_ref, line_ref, gk_ref, gv_ref, gq_ref, *, heads
):
    pairs, width = query_ref.shape
    core, lane_head, query_heads, scores, inside = cross_setup(
        core_ref, query_ref, key_ref, line_ref, heads
    )
    up_heads = spread_heads(own_turn(up_ref[...], core), lane_head, heads)
    lane = lax.broadcasted_iota(jnp.int32, (pairs, 128), 1)
    logs = []
    inners = []
    for head in range(heads):
        there = lane == lax.rem(head + core * (heads // 2), heads)
        logs.append(jnp.sum(jnp.where(there, stat_ref[:, :128], 0.0), axis=1, keepdims=True))
        inners.append(jnp.sum(jnp.where(there, stat_ref[:, 128:], 0.0), axis=1, keepdims=True))
    log = jnp.concatenate(logs, axis=0)
    inner = jnp.concatenate(inners, axis=0)
    probs = jnp.exp(jnp.where(inside, scores - log, NEGATIVE))
    grad = dot_nt(up_heads, value_ref[...])
    grad = (probs * (grad - inner)).astype(BF)
    gv_ref[...] = dot_tn(probs.astype(BF), up_heads).astype(BF)
    gk_ref[...] = (dot_tn(grad, query_heads) * SCALING).astype(BF)
    gq_ref[...] = gather_heads(dot_nn(grad, key_ref[...]), lane_head, heads, core)


def cross_forward(core, query, keys, values, segment, heads):
    pairs, width = query.shape
    vmem = pl.BlockSpec(memory_space=pltpu.VMEM)
    return pl.pallas_call(
        lambda *refs: cross_kernel(*refs, heads=heads),
        in_specs=[pl.BlockSpec(memory_space=pltpu.SMEM)] + [vmem] * 4,
        out_specs=vmem,
        out_shape=jax.ShapeDtypeStruct((pairs, width + 256), F32),
        compiler_params=pltpu.CompilerParams(vmem_limit_bytes=VMEM),
        cost_estimate=cost(600 * keys.size, 4 * keys.size),
    )(core.reshape(1), query, keys, values, segment[None, :])


def cross_backward(core, query, up, stat, keys, values, segment, heads):
    pairs, width = query.shape
    vmem = pl.BlockSpec(memory_space=pltpu.VMEM)
    grad = jax.ShapeDtypeStruct(keys.shape, BF)
    return pl.pallas_call(
        lambda *refs: cross_back_kernel(*refs, heads=heads),
        in_specs=[pl.BlockSpec(memory_space=pltpu.SMEM)] + [vmem] * 6,
        out_specs=[vmem] * 3,
        out_shape=[grad, grad, jax.ShapeDtypeStruct((pairs, width), F32)],
        compiler_params=pltpu.CompilerParams(vmem_limit_bytes=VMEM),
        cost_estimate=cost(1000 * keys.size, 8 * keys.size),
    )(core.reshape(1), query, up, stat, keys, values, segment[None, :])


def combine_kernel(id_ref, part_ref, wide_ref, log_ref, *, heads):
    count, width = wide_ref.shape
    ids = id_ref[...]
    peak = part_ref[:, width : width + 128]
    total = part_ref[:, width + 128 :]
    factor = jnp.zeros(peak.shape, F32)
    for query in range(count):
        there = ids == query
        top = jnp.max(jnp.where(there, peak, NEGATIVE), axis=0, keepdims=True)
        expo = jnp.where(there, jnp.exp(jnp.minimum(peak - top, 0.0)), 0.0)
        mass = jnp.sum(expo * total, axis=0, keepdims=True)
        factor = factor + expo / mass
        log_ref[query : query + 1, :] = top + jnp.log(mass)
    lane_head = lax.broadcasted_iota(jnp.int32, (peak.shape[0], width), 1) // (width // heads)
    scale = jnp.zeros((peak.shape[0], width), F32)
    for head in range(heads):
        scale = jnp.where(lane_head == head, factor[:, head : head + 1], scale)
    scaled = part_ref[:, :width] * scale
    for query in range(count):
        rows = jnp.where(ids == query, scaled, 0.0)
        wide_ref[query : query + 1, :] = jnp.sum(rows, axis=0, keepdims=True)


def combine(ids, parts, count, width, heads):
    vmem = pl.BlockSpec(memory_space=pltpu.VMEM)
    return pl.pallas_call(
        lambda *refs: combine_kernel(*refs, heads=heads),
        in_specs=[vmem] * 2,
        out_specs=[vmem] * 2,
        out_shape=[
            jax.ShapeDtypeStruct((count, width), F32),
            jax.ShapeDtypeStruct((count, 128), F32),
        ],
        compiler_params=pltpu.CompilerParams(vmem_limit_bytes=VMEM),
        cost_estimate=cost(10 * parts.size, 4 * parts.size),
    )(ids, parts)


class Net:
    def __init__(self):
        self.n_dp = lax.axis_size("dp")
        self.n_tok = lax.axis_size("tok")
        self.n_z = self.n_tok // 2
        self.tree = self.n_dp == 4 and self.n_z == 4
        self.dp, self.tok = lax.axis_index("dp"), lax.axis_index("tok")
        self.core, self.z = self.tok % 2, self.tok // 2
        self.x, self.y = self.dp % 2, self.dp // 2

    def tok_to(self, array, where):
        return lax.ppermute(array, "tok", [(t, where(t)) for t in range(self.n_tok)])

    def swap_core(self, array):
        return self.tok_to(array, lambda t: t ^ 1)

    def shift_z(self, array, by):
        return self.tok_to(array, lambda t: (t + 2 * by) % self.n_tok)

    def flip_dp(self, array, bit):
        return lax.ppermute(array, "dp", [(d, d ^ bit) for d in range(self.n_dp)])

    def swap_x(self, array):
        return self.flip_dp(array, 1)

    def swap_y(self, array):
        return self.flip_dp(array, 2)

    def own_first(self, array, axis=-1):
        low, high = jnp.split(array, 2, axis=axis)
        flipped = jnp.concatenate([high, low], axis=axis)
        return jnp.where(self.core == 0, array, flipped)


def after(array, *others):
    if not others:
        return array
    return lax.optimization_barrier((array, *others))[0]


def copies_of(plan, meta_ref, sources, outs, sems):
    copies = []
    for source, row, spot, column, wide, target, flag in plan:
        top = pl.multiple_of(meta_ref[spot], 48)
        left = pl.multiple_of(meta_ref[flag[0]] * 128 + flag[1], 128)
        copies.append(
            pltpu.make_async_copy(
                sources[source].at[pl.ds(row, 48), pl.ds(column, wide)],
                outs[target].at[pl.ds(top, 48), pl.ds(left, wide)],
                sems.at[len(copies)],
            )
        )
    return copies


def layout(net, pieces, widths, halves, own_columns, own_rows):
    spots = {}
    values = []

    def scalar(key, value):
        if key not in spots:
            spots[key] = len(values)
            values.append(jnp.asarray(value, jnp.int32))
        return spots[key]

    plan = []
    rows = 192
    for source, (array, corners, first, mine) in enumerate(pieces):
        for part, (dy, dx) in enumerate(corners):
            for block in range(4):
                for target, (half, start) in enumerate(zip(widths, halves)):
                    low = max(start, first)
                    high = min(start + half, first + array.shape[1])
                    if low >= high:
                        continue
                    flip = own_rows[target]
                    top = (net.y ^ dy ^ net.core) if flip else (net.y ^ dy)
                    spot = scalar(
                        (dy, dx, block, flip),
                        (top * 2 + (net.x ^ dx)) * rows + (net.z + 1 + block) % 4 * 48,
                    )
                    if own_columns[target]:
                        base = scalar("zero", 0)
                        shift = 0 if mine else half
                    else:
                        side = net.core if mine else 1 - net.core
                        base = scalar((mine, half), side * (half // 128))
                        shift = 0
                    plan.append(
                        (
                            source,
                            part * rows + block * 48,
                            spot,
                            low - first,
                            high - low,
                            target,
                            (base, shift + low - start),
                        )
                    )
    return plan, jnp.stack(values)


def place_kernel(meta_ref, *refs, plan, sources):
    copies = copies_of(plan, meta_ref, refs[:sources], refs[sources:-1], refs[-1])
    for copy in copies:
        copy.start()
    for copy in copies:
        copy.wait()


def place(plan, values, arrays, widths):
    count = len(arrays)
    return pl.pallas_call(
        lambda *refs: place_kernel(*refs, plan=plan, sources=count),
        in_specs=[pl.BlockSpec(memory_space=pltpu.SMEM)]
        + [pl.BlockSpec(memory_space=pl.ANY)] * count,
        out_specs=[pl.BlockSpec(memory_space=pltpu.VMEM)] * len(widths),
        out_shape=[jax.ShapeDtypeStruct((768, 2 * half), BF) for half in widths],
        scratch_shapes=[pltpu.SemaphoreType.DMA((len(plan),))],
        compiler_params=pltpu.CompilerParams(vmem_limit_bytes=VMEM),
        cost_estimate=cost(1, 768 * sum(widths) * 8),
    )(values, *arrays)


def expand_kernel(meta_ref, in_ref, up_ref, *refs, plan, sources):
    act_ref, grad_ref, out_ref, back_ref, first_ref, second_ref, sems = refs[sources:]
    weights = (first_ref, second_ref)
    copies = copies_of(plan, meta_ref, refs[:sources], weights, sems)
    for copy in copies:
        copy.start()
    for copy, step in zip(copies, plan):
        if step[5] == 0:
            copy.wait()
    width = first_ref.shape[1]
    tile = width // 4
    inner = [dot_nn(in_ref[...], first_ref[:, t * tile : (t + 1) * tile]) for t in range(4)]
    for copy, step in zip(copies, plan):
        if step[5] == 1:
            copy.wait()
    out = jnp.zeros(out_ref.shape, F32)
    back = jnp.zeros(back_ref.shape, F32)
    for t in range(4):
        part = slice(t * tile, (t + 1) * tile)
        up = dot_nn(up_ref[...], second_ref[:, part])
        act = jax.nn.gelu(inner[t]).astype(BF)
        grad = gelu_back(inner[t], up).astype(BF)
        act_ref[:, part] = act
        grad_ref[:, part] = grad
        back = back + dot_nt(grad, first_ref[:, part])
        out = out + dot_nt(act, second_ref[:, part])
    out_ref[...] = out
    back_ref[...] = back


def expand(plan, values, arrays, inputs, up, width):
    count = len(arrays)
    rows, model = inputs.shape
    vmem = pl.BlockSpec(memory_space=pltpu.VMEM)
    wide = jax.ShapeDtypeStruct((rows, width), BF)
    small = jax.ShapeDtypeStruct((rows, model), F32)
    return pl.pallas_call(
        lambda *refs: expand_kernel(*refs, plan=plan, sources=count),
        in_specs=[pl.BlockSpec(memory_space=pltpu.SMEM), vmem, vmem]
        + [pl.BlockSpec(memory_space=pl.ANY)] * count,
        out_specs=[vmem] * 4,
        out_shape=[wide, wide, small, small],
        scratch_shapes=[
            pltpu.VMEM((model, width), BF),
            pltpu.VMEM((model, width), BF),
            pltpu.SemaphoreType.DMA((len(plan),)),
        ],
        compiler_params=pltpu.CompilerParams(vmem_limit_bytes=VMEM),
        cost_estimate=cost(8 * rows * model * width, 4 * model * width),
    )(values, inputs, up, *arrays)


class Gather:
    def __init__(self, net, shards, own_columns, own_rows, cut):
        self.net, self.own_columns, self.own_rows, self.cut = net, own_columns, own_rows, cut
        self.shards = [shard.astype(BF) for shard in shards]
        self.widths = [shard.shape[1] // 2 for shard in shards]

    def halves(self, extra=None):
        core = self.net.core
        low = [shard[:, :half] for shard, half in zip(self.shards, self.widths)]
        high = [shard[:, half:] for shard, half in zip(self.shards, self.widths)]
        low, high = jnp.concatenate(low, axis=1), jnp.concatenate(high, axis=1)
        keep, sent = jnp.where(core == 0, low, high), jnp.where(core == 0, high, low)
        if extra is not None:
            keep = jnp.concatenate([keep, extra], axis=1)
            sent = jnp.concatenate([sent, extra], axis=1)
        return keep, sent

    def take(self, keep, got):
        first = jnp.where(self.net.core == 0, keep, got)
        second = jnp.where(self.net.core == 0, got, keep)
        self.chip = jnp.concatenate([first, second], axis=0)

    def over_z(self, *ready):
        if not self.net.tree:
            return ()
        chip = after(self.chip, *ready)
        self.line = [self.net.shift_z(chip, by) for by in (3, 2, 1)] + [chip]
        return (chip,)

    def join(self, *ready):
        if not self.net.tree:
            return ()
        line = [after(part, *ready) for part in self.line]
        self.one = jnp.concatenate([part[:, : self.cut] for part in line], axis=0)
        self.two = jnp.concatenate([part[:, self.cut :] for part in line], axis=0)
        return (self.one, self.two)

    def first(self, ready=(), join=()):
        if not self.net.tree:
            return ()
        one, two = after(self.one, *ready), after(self.two, *ready)
        self.one = jnp.concatenate([one, after(self.net.swap_x(one), *join)], axis=0)
        self.two = jnp.concatenate([two, after(self.net.swap_y(two), *join)], axis=0)
        return (self.one, self.two)

    def second(self, ready=(), join=()):
        if not self.net.tree:
            return ()
        one, two = after(self.one, *ready), after(self.two, *ready)
        self.near = (self.net.swap_core(self.one), self.net.swap_core(self.two))
        self.one_far = after(self.net.swap_y(one), *join)
        self.two_far = after(self.net.swap_x(two), *join)
        return (self.one_far, self.two_far)

    def extras(self, count, *ready):
        net = self.net
        parts = []
        for array in (self.two, self.two_far):
            block = after(array, *ready)[:, -128:].reshape(2, 4, 2 * count, -1)
            order = (net.z + 1 + jnp.arange(4, dtype=jnp.int32)) % 4
            same = order[None, :] == jnp.arange(4, dtype=jnp.int32)[:, None]
            zero = jnp.zeros((), BF)
            turned = jnp.where(same[None, :, :, None, None], block[:, None], zero)
            turned = jnp.sum(turned, axis=2).astype(BF)
            parts.append(turned.reshape(2, 8 * count, -1))
        near, far = parts
        return jnp.concatenate([near[0], far[0], near[1], far[1]], axis=0)

    def finish(self):
        net = self.net
        if not net.tree:
            outs = []
            for shard, columns, rows in zip(self.shards, self.own_columns, self.own_rows):
                whole = lax.all_gather(shard, ("dp", "tok"), axis=0, tiled=True)
                whole = net.own_first(whole, 1) if columns else whole
                outs.append(net.own_first(whole, 0) if rows else whole)
            return outs
        plan, values, arrays = self.parts()
        return place(plan, values, arrays, self.widths)

    def parts(self):
        net = self.net
        pieces = []
        far = (net.swap_core(self.one_far), net.swap_core(self.two_far))
        for array, other, corners, first in (
            (self.one, self.near[0], ((0, 0), (0, 1)), 0),
            (self.two, self.near[1], ((0, 0), (1, 0)), self.cut),
            (self.one_far, far[0], ((1, 0), (1, 1)), 0),
            (self.two_far, far[1], ((0, 1), (1, 1)), self.cut),
        ):
            pieces.append((array, corners, first, True))
            pieces.append((other, corners, first, False))
        starts = [sum(self.widths[:i]) for i in range(len(self.widths))]
        plan, values = layout(net, pieces, self.widths, starts, self.own_columns, self.own_rows)
        return plan, values, [piece[0] for piece in pieces]


def between_cores(net, gathers, extra=None):
    if not net.tree:
        return
    keeps, sents = zip(*[one.halves(extra) for one in gathers])
    got = net.swap_core(jnp.concatenate(sents, axis=1))
    start = 0
    for one, keep in zip(gathers, keeps):
        one.take(keep, got[:, start : start + keep.shape[1]])
        start += keep.shape[1]


def pick(array, index, axis):
    return lax.dynamic_index_in_dim(array, index, axis, keepdims=False)


def add(*parts):
    total = parts[0].astype(F32)
    for part in parts[1:]:
        total = total + part.astype(F32)
    return total


class Sum:
    def __init__(self, net, theirs, cut):
        self.net, self.cut, self.theirs = net, cut, theirs
        self.halves = [grad.shape[1] for grad in theirs]
        self.rows, self.wide = theirs[0].shape[0], sum(self.halves)
        self.got = net.swap_core(jnp.concatenate(theirs, axis=1)) if net.tree else theirs[0]

    def start(self, mine, join=()):
        self.mine = mine
        if not self.net.tree:
            return
        cut, shape = self.cut, (2, 2, self.rows // 4, self.wide)
        own = jnp.concatenate(mine, axis=1).reshape(shape)
        got = after(self.got, *join).reshape(shape)
        one = (own[..., :cut], got[..., :cut])
        two = (own[..., cut:], got[..., cut:])
        self.one = [self.halve(one, 0, self.net.y, keep) for keep in (True, False)]
        self.two = [self.halve(two, 1, self.net.x, keep) for keep in (True, False)]

    def halve(self, parts, axis, index, keep):
        index = index if keep else 1 - index
        return add(*[pick(part, index, axis) for part in parts]).astype(BF)

    def state(self):
        return (*self.one, *self.two) if self.net.tree else ()

    def first(self, ready=(), join=()):
        if not self.net.tree:
            return
        net = self.net
        one = (self.one[0], after(net.swap_y(after(self.one[1], *ready)), *join))
        two = (self.two[0], after(net.swap_x(after(self.two[1], *ready)), *join))
        self.one = [self.halve(one, 0, net.x, keep) for keep in (True, False)]
        self.two = [self.halve(two, 0, net.y, keep) for keep in (True, False)]

    def second(self, ready=(), join=()):
        if not self.net.tree:
            return
        net = self.net
        one = (self.one[0], after(net.swap_x(after(self.one[1], *ready)), *join))
        two = (self.two[0], after(net.swap_y(after(self.two[1], *ready)), *join))
        shape = (4, self.rows // 16, -1)
        one, two = [part.reshape(shape) for part in one], [part.reshape(shape) for part in two]

        def chunk(at):
            sums = [add(*[pick(part, at, 0) for part in parts]) for parts in (one, two)]
            return jnp.concatenate(sums, axis=1)

        self.own = chunk(net.z)
        self.sent = [chunk((net.z + by) % 4).astype(BF) for by in (1, 2, 3)]

    def pending(self):
        return tuple(self.sent) if self.net.tree else ()


def finish(net, sums, join=()):
    if not net.tree:
        outs = []
        for one in sums:
            for mine, theirs in zip(one.mine, one.theirs):
                whole = net.own_first(jnp.concatenate([mine, theirs], axis=1), 1)
                total = lax.psum_scatter(whole, ("dp", "tok"), scatter_dimension=0, tiled=True)
                outs.append(total.astype(F32))
        return outs
    rows = sums[0].rows
    got = []
    for i, by in enumerate((1, 2, 3)):
        sent = jnp.concatenate([one.sent[i] for one in sums], axis=1)
        got.append(after(net.shift_z(sent, by), *join))
    total = add(jnp.concatenate([one.own for one in sums], axis=1), *got)
    total = total.reshape(2, rows // 32, -1)
    keep = pick(total, net.core, 0)
    other = net.swap_core(pick(total, 1 - net.core, 0))
    low = jnp.where(net.core == 0, keep, other)
    high = jnp.where(net.core == 0, other, keep)
    outs = []
    start = 0
    for half in [half for one in sums for half in one.halves]:
        part = slice(start, start + half)
        outs.append(jnp.concatenate([low[:, part], high[:, part]], axis=1))
        start += half
    return outs


def gather_tok(net, array, join=(), over_core=()):
    if not net.tree:
        return lax.all_gather(array, "tok", axis=0), jnp.arange(net.n_tok, dtype=jnp.int32)
    steps = (0, 1, 2, 3)
    array = jnp.stack([array] + [after(net.shift_z(array, by), *join) for by in steps[1:]])
    array = jnp.concatenate([array, after(net.swap_core(array), *over_core)], axis=0)
    source = [(net.z - by) % 4 * 2 + net.core for by in steps]
    source += [(net.z - by) % 4 * 2 + 1 - net.core for by in steps]
    return array, jnp.stack(source).astype(jnp.int32)


def gather_dp(net, array, over_x=(), over_y=()):
    if not net.tree:
        whole = lax.all_gather(array, "dp", axis=0)
        order = net.dp ^ jnp.arange(net.n_dp, dtype=jnp.int32)
        same = order[:, None] == jnp.arange(net.n_dp, dtype=jnp.int32)[None, :]
        zero = jnp.zeros((), array.dtype)
        turned = jnp.sum(jnp.where(same[:, :, None, None], whole[None], zero), axis=1)
        return turned.reshape(-1, array.shape[1]).astype(array.dtype)
    array = jnp.concatenate([array, after(net.swap_x(array), *over_x)], axis=0)
    return jnp.concatenate([array, after(net.swap_y(array), *over_y)], axis=0)


def sum_small(net, array, joins):
    joins = list(joins)
    bit = 1
    while bit < net.n_tok:
        other = net.tok_to(array, lambda t, bit=bit: t ^ bit)
        array = array + after(other, *(joins.pop(0) if joins else ()))
        bit *= 2
    bit = 1
    while bit < net.n_dp:
        array = array + after(net.flip_dp(array, bit), *(joins.pop(0) if joins else ()))
        bit *= 2
    return array


def per_device(
    encoder_input,
    decoder_input,
    output_cotangent,
    pair_lengths,
    pair_offset,
    pair_query,
    attention_master,
    attention_moment,
    attention_average,
    feedforward_master,
    feedforward_moment,
    feedforward_average,
    decoder_master,
    decoder_moment,
    decoder_average,
    expansion_master,
    expansion_moment,
    expansion_average,
    gain_master,
    gain_moment,
    gain_average,
    bias_master,
    bias_moment,
    bias_average,
):
    net = Net()
    length = encoder_input.shape[1]
    width = encoder_input.shape[2]
    buckets, heads = bias_master.shape
    head_size = width // heads
    pairs = pair_lengths.shape[1]
    nquery = decoder_input.shape[0]

    half = width // 2
    wide = feedforward_master.shape[2] // 2
    att = [attention_master[i] for i in range(6)]
    feed = [feedforward_master[i] for i in range(2)]
    dec = [decoder_master[i] for i in range(4)]
    widen = [expansion_master[i] for i in range(2)]
    three = jnp.transpose(
        attention_master[:3].astype(BF).reshape(3, -1, width // 128, 128), (1, 2, 0, 3)
    ).reshape(-1, 3 * width)
    both = jnp.concatenate([decoder_input, output_cotangent], axis=1)
    get_att = Gather(
        net,
        [three, att[3]],
        [True, False],
        [False, True],
        7 * half // 3 - 128,
    )
    between_cores(net, [get_att], both.reshape(-1, 128))
    early = get_att.over_z()
    feed, dec, widen, others = (
        [after(shard, *early) for shard in shards] for shards in (feed, dec, widen, att[4:])
    )
    get_feed = Gather(net, feed, [True] * 2, [False] * 2, wide)
    get_dec = Gather(net, others + dec, [True] * 2 + [False] * 4, [False] * 6, 3 * half)
    get_exp = Gather(net, widen, [True] * 2, [False] * 2, wide)
    between_cores(net, [get_feed, get_dec, get_exp])
    step = get_att.join()
    get_feed.over_z(*step)
    get_att.first()
    step_att = get_att.second()
    step_feed = get_feed.join(*step_att)
    get_dec.over_z(*step_feed)
    w_qkv, w_out = get_att.finish()

    counter = jnp.arange(pairs, dtype=jnp.int32)
    late = (
        pair_offset,
        pair_query,
        gain_master,
        gain_moment,
        gain_average,
        bias_master,
        bias_moment,
        bias_average,
        net.tok,
    )
    late = [after(array, *step) for array in late]
    pair_offset, pair_query, gain_master, gain_moment, gain_average = late[:5]
    bias_master, bias_moment, bias_average, tok = late[5:]
    hidden = after(encoder_input, *step)[0].astype(F32)
    lengths = after(pair_lengths, *step)[0]
    ends = jnp.sum(jnp.where(counter[:, None] <= counter[None, :], lengths[:, None], 0), axis=0)
    position = jnp.arange(length, dtype=jnp.int32)
    segment = jnp.sum((position[:, None] >= ends[None, :]).astype(jnp.int32), axis=1)
    onehot = diagonal_onehot(buckets)
    bias_rows = jnp.sum(bias_master.T[:, None, :] * onehot[None], axis=2)
    bias_rows = net.own_first(bias_rows, 0)

    normed = rms_norm(hidden, gain_master[0]).astype(BF)
    qkv = dot_nn(normed, w_qkv).astype(BF)
    feed_half = get_feed.first(join=(qkv,))
    attended = attention_forward(after(qkv, *feed_half), bias_rows, segment)
    residual = hidden + dot_nn(attended, w_out)
    normed_two = rms_norm(residual, gain_master[1]).astype(BF)
    step_two = get_feed.second(join=(normed_two,))
    step_dec = get_dec.join(normed_two)
    get_exp.over_z(*step_dec, *step_two)
    w_up, w_down = get_feed.finish()
    dec_half = get_dec.first(step_two, (w_up, w_down))
    inner = dot_nn(after(normed_two, *dec_half), w_up)
    activated = jax.nn.gelu(inner).astype(BF)
    if net.tree:
        ordered = get_att.extras(nquery, activated)
    else:
        ordered = gather_dp(net, lax.all_gather(both, "tok", axis=0, tiled=True))
    encoded = (residual + dot_nt(activated, w_down)).astype(BF)
    step_three = get_dec.second(join=(encoded,))
    w_ck, w_cv, e_zero, e_one, e_two, e_three = get_dec.finish()
    cross_keys = dot_nn(encoded, w_ck).astype(BF)
    cross_values = dot_nn(encoded, w_cv).astype(BF)
    get_exp.join(*step_three)

    state = ordered[:, :width].astype(F32)
    up_low = ordered[:, width:]
    upstream = up_low.astype(F32)
    group = net.n_tok * nquery
    total_rows = state.shape[0]
    row_id = jnp.arange(total_rows, dtype=jnp.int32)
    own_row = (row_id // nquery == tok)[:, None]

    def own_rows(rows):
        return lax.dynamic_slice_in_dim(rows, net.tok * nquery, nquery, axis=0)

    self_in = rms_norm(state, gain_master[2]).astype(BF)
    self_values = dot_nn(self_in, e_zero).astype(BF)
    after_self = state + dot_nn(self_values, e_one)
    cross_in = rms_norm(after_self, gain_master[3]).astype(BF)
    cross_query = dot_nn(cross_in, e_two).astype(BF)

    offsets = pair_offset[0]
    owners = pair_query[0]
    query_id = jnp.arange(group, dtype=jnp.int32)
    own_id = (tok + offsets) % net.n_tok * nquery + owners
    own_match = own_id[:, None] == query_id[None, :]

    def at_pairs(rows):
        return jnp.sum(jnp.where(own_match[:, :, None], rows[None, :group].astype(F32), 0.0), axis=1)

    exp_half = get_exp.first(join=(cross_query,))
    pair_queries = at_pairs(after(cross_query, *exp_half))
    get_exp.second()
    partial = cross_forward(net.core, pair_queries, cross_keys, cross_values, segment, heads)
    got, source = gather_tok(net, after(partial, *get_exp.near) if net.tree else partial)
    pair_id = (source[:, None] + offsets[None, :]) % net.n_tok * nquery + owners[None, :]
    pair_match = pair_id.reshape(1, -1) == query_id[:, None]

    def sum_pairs(rows):
        return lax.dot_general(
            pair_match.astype(F32),
            rows,
            (((1,), (0,)), ((), ())),
            precision=lax.Precision.HIGHEST,
            preferred_element_type=F32,
        )

    got = got.reshape(-1, width + 256)
    cross_wide, row_log = combine(pair_id.reshape(-1, 1), got, group, width, heads)
    cross_out = gather_dp(net, cross_wide.astype(BF))

    after_cross = after_self + dot_nn(cross_out, e_three)
    final_in = rms_norm(after_cross, gain_master[4]).astype(BF)
    if net.tree:
        final_act, grad_inner, final_out, grad_final_in = expand(
            *get_exp.parts(), final_in, up_low, 2 * wide
        )
    else:
        x_up, x_down = get_exp.finish()
        grad_act = dot_nn(up_low, x_down)
        final_inner = dot_nn(final_in, x_up)
        grad_inner = gelu_back(final_inner, grad_act).astype(BF)
        grad_final_in = dot_nt(grad_inner, x_up)
        final_act = jax.nn.gelu(final_inner).astype(BF)
        final_out = dot_nt(final_act, x_down)

    def decoder_norm_back(values, gain, up):
        grad, _ = norm_back(values, gain, up)
        _, grad_gain = norm_back(values, gain, jnp.where(own_row, up, 0.0))
        return grad, grad_gain

    grad_state_four, grad_gain_four = decoder_norm_back(after_cross, gain_master[4], grad_final_in)
    grad_cross_total = upstream + grad_state_four
    cross_grad_low = grad_cross_total.astype(BF)
    grad_cross_out = dot_nt(cross_grad_low, e_three)[:group].astype(BF).astype(F32)
    row_inner = jnp.sum((grad_cross_out * cross_wide).reshape(group, heads, head_size), axis=2)
    empty = jnp.zeros((group, 128 - heads), F32)
    back = at_pairs(jnp.concatenate([grad_cross_out, row_log, row_inner, empty], axis=1))
    decoder_output = own_rows(after_cross + final_out)

    grad_keys_cross, grad_values_cross, grad_query_part = cross_backward(
        net.core,
        pair_queries,
        back[:, :width],
        back[:, width:],
        cross_keys,
        cross_values,
        segment,
        heads,
    )
    grad_encoded = (dot_nt(grad_keys_cross, w_ck) + dot_nt(grad_values_cross, w_cv)).astype(BF)

    grad_down = [
        dot_tn(grad_encoded, part).astype(BF) for part in (activated[:, :wide], activated[:, wide:])
    ]
    crosses = [
        dot_tn(encoded, grad_keys_cross).astype(BF),
        dot_tn(encoded, grad_values_cross).astype(BF),
    ]
    down = Sum(net, [grad_down[1]], 2 * half)
    grad_activated = dot_nn(after(grad_encoded, *grad_down), w_down)
    grad_inner_enc = gelu_back(inner, grad_activated).astype(BF)
    down.start(grad_down[:1], (grad_inner_enc,))
    grad_inner_enc = after(grad_inner_enc, *down.state())
    grad_up = [
        dot_tn(normed_two, part).astype(BF)
        for part in (grad_inner_enc[:, :wide], grad_inner_enc[:, wide:])
    ]
    grad_normed_two = dot_nt(after(grad_inner_enc, *grad_up), w_up)
    grad_resid, grad_gain_one = norm_back(residual, gain_master[1], grad_normed_two)
    grad_residual = grad_encoded.astype(F32) + grad_resid
    attn_low = grad_residual.astype(BF)
    down.first()
    got_query, _ = gather_tok(net, after(grad_query_part, grad_inner_enc))
    ready_low = after(attn_low, *down.state(), got_query)
    grad_out = dot_tn(net.own_first(attended), net.own_first(ready_low)).astype(BF)
    others = [grad_out, *crosses]
    middle = Sum(net, [grad_up[1], *[grad[:, half:] for grad in others]], 11 * half // 3)
    grad_attended = dot_nt(after(attn_low, grad_out), w_out).astype(BF)
    middle.start([grad_up[0], *[grad[:, :half] for grad in others]])
    grad_attended = after(grad_attended, *middle.state(), *down.state())
    blocks = width // 256

    def attention_part(up, first):
        return attention_backward(qkv, up, bias_rows, segment, first, blocks)

    their_grads, their_diagonals = attention_part(grad_attended, blocks)
    down.second(join=(their_grads,))
    middle.first(join=(their_grads,))
    their_left = after(normed, *down.pending(), *middle.state())
    their_qkv = dot_tn(their_left, their_grads).astype(BF)
    last = Sum(net, [their_qkv], 5 * half // 3)
    middle.second(join=(their_qkv,))
    grad_query_cross = (sum_pairs(got_query.reshape(-1, width)) * SCALING).astype(BF)
    grad_query_cross = gather_dp(net, grad_query_cross, (their_grads,), (their_qkv,))
    own_up = after(grad_attended, last.got, grad_query_cross, *middle.pending())
    own_grads, own_diagonals = attention_part(own_up, 0)
    own_qkv = dot_tn(normed, own_grads).astype(BF)
    last.start([own_qkv])
    diagonals = jnp.concatenate([own_diagonals, their_diagonals], axis=0)
    own_grads = after(own_grads, *last.state())
    grad_normed = dot_nt(jnp.concatenate([own_grads, their_grads], axis=1), w_qkv)
    grad_input_part, grad_gain_zero = norm_back(hidden, gain_master[0], grad_normed)
    encoder_gradient = (grad_residual + grad_input_part)[None]

    grad_query_cross = after(grad_query_cross, own_grads)
    grad_cross_in = dot_nt(grad_query_cross, e_two)
    grad_state_three, grad_gain_three = decoder_norm_back(
        after_self, gain_master[3], grad_cross_in
    )
    grad_self_total = grad_cross_total + grad_state_three
    self_grad_low = grad_self_total.astype(BF)
    grad_self_values = dot_nt(self_grad_low, e_one).astype(BF)
    grad_self_in = dot_nt(grad_self_values, e_zero)
    grad_state_two, grad_gain_two = decoder_norm_back(state, gain_master[2], grad_self_in)
    decoder_gradient = own_rows(grad_self_total + grad_state_two)
    own = decoder_master.shape[1]
    rank = net.dp * net.n_tok + net.tok

    def own_weight_rows(left, right):
        return dot_tn(lax.dynamic_slice_in_dim(left, rank * own, own, axis=1), right)

    grad_dec = jnp.stack(
        [
            own_weight_rows(self_in, grad_self_values),
            own_weight_rows(self_values, self_grad_low),
            own_weight_rows(cross_in, grad_query_cross),
            own_weight_rows(cross_out, cross_grad_low),
        ]
    )
    grad_exp = jnp.stack(
        [
            net.own_first(own_weight_rows(final_in, grad_inner)),
            net.own_first(own_weight_rows(up_low, final_act)),
        ]
    )

    sum_down, sum_up, sum_out, sum_ck, sum_cv = finish(net, [down, middle], (own_qkv,))
    last.first(join=(grad_gain_zero,))
    after_first = last.state()
    last.second()
    after_second = last.pending()
    (sum_three,) = finish(net, [last])
    grad_table = jnp.dot(
        net.own_first(diagonals, 0),
        onehot,
        precision=lax.Precision.HIGHEST,
        preferred_element_type=F32,
    ).T
    gain_grad = jnp.concatenate(
        [grad_gain_zero, grad_gain_one, grad_gain_two, grad_gain_three, grad_gain_four]
    )
    small = jnp.concatenate([gain_grad, grad_table.reshape(-1)])
    joins = [(encoder_gradient,), after_first, after_first, after_second]
    small = sum_small(net, small, joins)
    gain_sum = small[: 5 * width].reshape(5, width)
    bias_sum = small[5 * width :].reshape(buckets, heads)

    sum_three = jnp.transpose(sum_three.reshape(own, width // 128, 3, 128), (2, 0, 1, 3))
    sum_three = sum_three.reshape(3, own, width)
    results = [decoder_output, encoder_gradient, decoder_gradient]
    groups = (
        (
            attention_master,
            attention_moment,
            attention_average,
            jnp.concatenate([sum_three, jnp.stack([sum_out, sum_ck, sum_cv])], axis=0),
        ),
        (
            feedforward_master,
            feedforward_moment,
            feedforward_average,
            jnp.stack([sum_up, sum_down]),
        ),
        (decoder_master, decoder_moment, decoder_average, grad_dec),
        (expansion_master, expansion_moment, expansion_average, grad_exp),
        (gain_master, gain_moment, gain_average, gain_sum),
        (bias_master, bias_moment, bias_average, bias_sum),
    )
    for weight, moment, average, gradient in groups:
        results.extend(update(weight, moment, average, gradient))
    return tuple(results)


def solution(mesh):
    spread = P(("dp", "tok"), None)
    weights = P(None, ("dp", "tok"), None)
    in_specs = (
        P(("dp", "tok"), None, None),
        spread,
        spread,
        spread,
        P("dp", None),
        P("dp", None),
        *[weights] * 12,
        *[P()] * 6,
    )
    out_specs = (spread, P(("dp", "tok"), None, None), spread, *[weights] * 16, *[P()] * 8)
    return jax.shard_map(
        per_device, mesh=mesh, in_specs=in_specs, out_specs=out_specs, check_vma=False
    )
```
